32 devices in a mesh: cluster: 4 (over z), member: 8 (over y, x, core).
Axes of the slice: x: 2, y: 2, z: 4, core: 2. Of those that a mesh axis runs over, the one named last changes fastest.
Arguments:
- dual_load: float32 [4, 8, 64, 2, 1024], P('cluster', 'member'), may hold values from -110 to 110
- dual_operator: bfloat16 [2048, 2048], replicated, may hold values from -1.5859375 to 3.5859375, as said below
- index_map: int32 [4, 8, 2048], P('cluster', 'member'), may hold values from 0 to 2047, as said below
- stiffness: float32 [4, 8], P('cluster', 'member'), may hold values from 1 to 10
- coarse_basis: float32 [4, 8, 6, 2048], P('cluster', 'member'), may hold values from -2.5 to 2.5
- dirichlet_blocks: bfloat16 [4, 8, 16, 128, 128], P('cluster', 'member'), may hold values from -1 to 2.5, as said below
- coarse_inverse: float32 [24, 24], replicated, may hold values from -1 to 1, as said below
Outputs:
- multipliers: float32 [4, 8, 64, 2, 1024], P('cluster', 'member')
- residual: float32 [4, 8, 64, 2, 1024], P('cluster', 'member')
The draws below stay inside these ranges and needn't reach their ends.
Inputs may be any that keep to these rules, and one draw needn't show every extreme that they name: `dual_operator`: symmetric. `dirichlet_blocks`: each block is symmetric. `coarse_inverse`: symmetric. `index_map`: each subdomain's row names every position once.
All inputs are finite; a program needn't handle non-finite values.
Results may differ from the reference program's by a relative error of at most 0.0038.
Values sent between devices are 32-bit elements; how exact they have to be, the bound alone decides.
No kernel may reach another device: no remote copies, remote signals or barrier semaphores. Data moves between devices by JAX's collectives and lax.ppermute only.
A program may use at most 64 MiB of HBM per device.

```python
import math
import jax
import jax.numpy as jnp
from jax import lax

DUAL = 2048
FACE = 1024
BLOCK = 128
NBLOCK = 16
MODES = 6
LOADS = 64
ITERS = 2
CLUSTERS = 4
MEMBERS = 8
COARSE = 24


def rough_draw(key, extent):
    return jax.random.truncated_normal(key, -4.0, 4.0, extent, jnp.float32)


def stiffness_draw(key):
    exponent = jax.random.uniform(jax.random.fold_in(key, 17), (CLUSTERS, MEMBERS), jnp.float32, 0.0, 1.0)
    return jnp.exp(exponent * math.log(10.0))


def one_order(subkey):
    return jax.random.permutation(subkey, DUAL)


def order_draw(key):
    keys = jax.random.split(jax.random.fold_in(key, 21), CLUSTERS * MEMBERS)
    orders = jax.vmap(one_order)(keys)
    return orders.astype(jnp.int32).reshape(CLUSTERS, MEMBERS, DUAL)


def shared_modes(key):
    return rough_draw(jax.random.fold_in(key, 23), (MODES, DUAL))


def basis_draw(key):
    orders = order_draw(key)
    aligned = jnp.take(shared_modes(key), orders, axis=1)
    aligned = jnp.moveaxis(aligned, 0, 2)
    own_part = rough_draw(jax.random.fold_in(key, 7), (CLUSTERS, MEMBERS, MODES, DUAL))
    return (0.8 * aligned + 0.6 * own_part) * (1.0 / math.sqrt(MODES))


def symmetric_draw(key, extent, order):
    sample = rough_draw(key, extent)
    return (sample + jnp.swapaxes(sample, -1, -2)) * (1.0 / math.sqrt(2.0 * order))


def draw_dual_operator(key, part):
    noise_part = symmetric_draw(jax.random.fold_in(key, 3), (DUAL, DUAL), DUAL)
    modes = shared_modes(key)
    strong_part = jnp.zeros((DUAL, DUAL), jnp.float32)
    for mode in range(MODES):
        strong_part = strong_part + modes[mode][:, None] * modes[mode][None, :]
    total = 1.5 * jnp.eye(DUAL, dtype=jnp.float32) + 0.5 * noise_part + 12.0 / DUAL * strong_part
    return total.astype(jnp.bfloat16)


def draw_index_map(key, part):
    return order_draw(key)


def draw_stiffness(key, part):
    return stiffness_draw(key)


def draw_dirichlet_blocks(key, part):
    noise_part = symmetric_draw(jax.random.fold_in(key, 5), (CLUSTERS, MEMBERS, NBLOCK, BLOCK, BLOCK), BLOCK)
    modulus = stiffness_draw(key).reshape(CLUSTERS, MEMBERS, 1, 1, 1)
    return (0.18 * modulus * (jnp.eye(BLOCK, dtype=jnp.float32) + 0.4 * noise_part)).astype(jnp.bfloat16)


def draw_coarse_inverse(key, part):
    magnitude = MODES / (MEMBERS * DUAL)
    noise_part = symmetric_draw(jax.random.fold_in(key, 11), (COARSE, COARSE), COARSE)
    return (jnp.eye(COARSE, dtype=jnp.float32) + 0.3 * noise_part) * magnitude


def draw_coarse_basis(key, part):
    return basis_draw(key)


def draw_dual_load(key, part):
    basis_rows = basis_draw(key)
    amplitude = rough_draw(jax.random.fold_in(key, 9), (CLUSTERS, MODES, LOADS))
    coarse = jnp.einsum('ckr,cmkl->cmrl', amplitude, basis_rows).reshape(CLUSTERS, MEMBERS, LOADS, 2, FACE)
    rough_part = rough_draw(jax.random.fold_in(key, 13), (CLUSTERS, MEMBERS, LOADS, 2, FACE))
    chain_ramp = jnp.linspace(0.6, 1.8, CLUSTERS * MEMBERS, dtype=jnp.float32).reshape(CLUSTERS, MEMBERS, 1, 1, 1)
    return (coarse + rough_part) * chain_ramp


def setup_inputs(seed: int = 0) -> dict:
    splits = jax.random.split(jax.random.key(seed), 8)
    return {
        "dual_load": draw_dual_load(jax.random.fold_in(splits[7], 71), 0),
        "dual_operator": draw_dual_operator(jax.random.fold_in(splits[7], 71), 0),
        "index_map": draw_index_map(jax.random.fold_in(splits[7], 71), 0),
        "stiffness": draw_stiffness(jax.random.fold_in(splits[7], 71), 0),
        "coarse_basis": draw_coarse_basis(jax.random.fold_in(splits[7], 71), 0),
        "dirichlet_blocks": draw_dirichlet_blocks(jax.random.fold_in(splits[7], 71), 0),
        "coarse_inverse": draw_coarse_inverse(jax.random.fold_in(splits[7], 71), 0),
    }


def assemble(part):
    zero = jnp.zeros_like(part[:1, :, 0])
    from_prev = jnp.concatenate([zero, part[:-1, :, 1]], axis=0)
    from_next = jnp.concatenate([part[1:, :, 0], zero], axis=0)
    return part + jnp.stack([from_prev, from_next], axis=2)


def reference(dual_load, dual_operator, index_map, stiffness, coarse_basis, dirichlet_blocks, coarse_inverse):
    exact_precision = lax.Precision.HIGHEST
    count = CLUSTERS * MEMBERS
    position = jnp.arange(count, dtype=jnp.int32)
    low_side = jnp.where(position > 0, 0.5, 1.0)
    high_side = jnp.where(position < count - 1, 0.5, 1.0)
    weights = jnp.stack([low_side, high_side], axis=1).astype(jnp.float32)[:, None, :, None]

    def inner(left, right):
        return jnp.sum(weights * left * right, axis=(0, 2, 3))

    def project(vector):
        folded = vector.reshape(CLUSTERS, MEMBERS, LOADS, DUAL)
        totals = jnp.einsum("cmrl,cmkl->rck", folded, coarse_basis, precision=exact_precision)
        totals = totals.reshape(LOADS, COARSE)
        amounts = jnp.dot(totals, coarse_inverse.T, precision=exact_precision)
        amounts = amounts.reshape(LOADS, CLUSTERS, MODES)
        spread = jnp.einsum("rck,cmkl->cmrl", amounts, coarse_basis, precision=exact_precision)
        return vector - assemble(spread.reshape(count, LOADS, 2, FACE))

    block_table = dirichlet_blocks.reshape(count, NBLOCK, BLOCK, BLOCK).astype(jnp.float32)
    operator_wide = dual_operator.astype(jnp.float32)

    def precondition(vector):
        scaled = (weights * vector).astype(jnp.bfloat16).reshape(count, LOADS, NBLOCK, BLOCK)
        blocked = jnp.einsum("srnj,snij->srni", scaled.astype(jnp.float32), block_table, precision=exact_precision)
        return assemble(weights * blocked.reshape(count, LOADS, 2, FACE))

    def subdomain_operator(inputs):
        flattened, ordering, modulus = inputs
        inverse = jnp.zeros((DUAL,), jnp.int32).at[ordering].set(jnp.arange(DUAL, dtype=jnp.int32))
        local_order = jnp.take(flattened, inverse, axis=1).astype(jnp.float32)
        product = jnp.dot(local_order, operator_wide, precision=exact_precision)
        return (1.0 / modulus) * jnp.take(product, ordering, axis=1)

    def apply(vector):
        rounded = vector.astype(jnp.bfloat16).reshape(count, LOADS, DUAL)
        local_image = lax.map(subdomain_operator, (rounded, index_map.reshape(count, DUAL).astype(jnp.int32), stiffness.reshape(count)))
        return assemble(local_image.reshape(count, LOADS, 2, FACE))

    residual = assemble(dual_load.reshape(count, LOADS, 2, FACE))
    multipliers = jnp.zeros_like(residual)
    direction = residual
    rho_prev = None
    for sweep in range(ITERS):
        projected = project(residual)
        search = project(precondition(projected))
        rho_now = inner(projected, search)
        if sweep == 0:
            direction = search
        else:
            direction = search + (rho_now / rho_prev)[None, :, None, None] * direction
        rho_prev = rho_now
        applied = apply(direction)
        step_size = (rho_now / inner(direction, applied))[None, :, None, None]
        multipliers = multipliers + step_size * direction
        residual = residual - step_size * applied
    return multipliers.reshape(dual_load.shape), residual.reshape(dual_load.shape)
```

```python
import functools

import jax
import jax.numpy as jnp
import numpy as np
from jax import lax
from jax.experimental import pallas as pl
from jax.experimental.pallas import tpu as pltpu
from jax.sharding import PartitionSpec as P

AXES = ("cluster", "member")
F32 = jnp.float32
BF16 = jnp.bfloat16
EXACT = lax.Precision.HIGHEST
KP = 8
TILE = 512


def dot(left, right):
    return jnp.dot(left, right, preferred_element_type=F32)


def dot_rows(left, right):
    return lax.dot_general(
        left, right, (((1,), (1,)), ((), ())), precision=EXACT, preferred_element_type=F32
    )


def dot_modes(amounts, rows):
    return lax.dot_general(
        amounts, rows, (((0,), (0,)), ((), ())), precision=EXACT, preferred_element_type=F32
    )


def two_parts(value):
    high = value.astype(BF16)
    return high, (value - high.astype(F32)).astype(BF16)


def chain_table(clusters, members):
    count = clusters * members
    ints, floats = [], []

    def side(pos):
        cluster, member = divmod(pos, members)
        other = cluster
        if member == 0:
            other = cluster - 1
        elif member == members - 1:
            other = cluster + 1
        return cluster, min(max(other, 0), clusters - 1)

    for pos in range(count):
        row, near = [pos % 2], []
        row += side(pos)
        for partner in (pos ^ 1, pos - 1 if pos % 2 == 0 else pos + 1):
            real = 0 <= partner < count
            row += side(partner if real else pos)
            near.append((0.5 if real else 1.0, float(real and partner // members == pos // members)))
        ints.append(row)
        floats.append([near[0][0], near[1][0], near[0][1], near[1][1]])
    return np.array(ints, np.int32), np.array(floats, np.float32)


def pack_kernel(modes, ints, load, basis, blocks, out_a, out_b):
    loads, _, face = load.shape
    half = blocks.shape[0] // 2
    size = blocks.shape[1]
    odd = ints[0] == 1
    row = lax.broadcasted_iota(jnp.int32, (size, size), 0)
    col = lax.broadcasted_iota(jnp.int32, (size, size), 1)
    load_0, load_1 = load[:, 0, :], load[:, 1, :]
    basis_0, basis_1 = basis[:, :face], basis[:, face:]
    low = loads + KP
    mid = size // 2
    for out, first in ((out_a, odd), (out_b, jnp.logical_not(odd))):
        out[:loads, :] = jnp.where(first, load_0, load_1)
        out[loads:low, :] = jnp.zeros((KP, face), F32)
        out[loads : loads + modes, :] = jnp.where(first, basis_0, basis_1)
        base = jnp.where(first, 0, half)
        for pair in range(half // 2):
            upper = blocks[base + 2 * pair].astype(F32)
            lower = blocks[base + 2 * pair + 1].astype(F32)
            both = jnp.where(row <= col, upper, lower)
            left = pair * size
            right = (half // 2 + pair) * size
            out[low : low + mid, left : left + size] = both[:mid]
            out[low : low + mid, right : right + size] = both[mid:]
            diagonal = jnp.sum(jnp.where(row == col, lower, 0.0), axis=0, keepdims=True)
            out[loads + modes : loads + modes + 1, left : left + size] = diagonal


def order_kernel(position_rows, position_cols, pick, place):
    rows, count = pick.shape
    here = lax.broadcasted_iota(jnp.int32, (rows, count), 1)
    pick[...] = jnp.where(position_rows[...] == here, 1.0, 0.0).astype(BF16)
    start = pl.program_id(0) * rows
    here = lax.broadcasted_iota(jnp.int32, (rows, count), 0) + start
    place[...] = jnp.where(position_cols[...] == here, 1.0, 0.0).astype(BF16)


def operator_step(step, tiles, rows, pick, operator, place, first, second, third, finish):
    @pl.when(step < tiles)
    def _():
        cols = pl.ds(pl.multiple_of(step * TILE, TILE), TILE)
        second[:, cols] = dot(first[...], pick[...]).astype(BF16)

    @pl.when((step >= tiles) & (step < 2 * tiles))
    def _():
        cols = pl.ds(pl.multiple_of((step - tiles) * TILE, TILE), TILE)
        product = dot(second[...], operator[...])
        high, low = two_parts(product[:rows] + product[rows:])
        third[:rows, cols] = high
        third[rows:, cols] = low

    @pl.when(step >= 2 * tiles)
    def _():
        product = dot(third[...], place[...])
        finish(step - 2 * tiles, product[:rows] + product[rows:])


def store_image(tile, value, tiles, image_a, image_b):
    half = tiles // 2

    @pl.when(tile < half)
    def _():
        image_a[:, pl.ds(pl.multiple_of(tile * TILE, TILE), TILE)] = value

    @pl.when(tile >= half)
    def _():
        image_b[:, pl.ds(pl.multiple_of((tile - half) * TILE, TILE), TILE)] = value


def smooth_block(value, weight, block_pair):
    rows = value.shape[0]
    high, low = two_parts(weight * value)
    left = jnp.concatenate(
        [jnp.concatenate([high, high], axis=1), jnp.concatenate([low, low], axis=1)], axis=0
    )
    product = dot(left, block_pair)
    return weight * (product[:rows] + product[rows:])


def first_kernel(
    modes, tiles,
    ints, floats, pay_a, pay_b, got_a, got_b, blocks, pick, operator, place,
    residual, smooth, coarse, pairs, image_a, image_b, terms,
    own_basis, first, second, third,
):
    step = pl.program_id(0)
    loads, slots = residual.shape
    face = slots // 2
    count = pairs.shape[0]
    half = count // 2
    size = pairs.shape[2]
    rows = loads + 4 * KP
    low_row = loads + KP
    mid = size // 2

    @pl.when(step == 0)
    def _():
        odd = ints[0] == 1
        row = lax.broadcasted_iota(jnp.int32, (size, size), 0)
        col = lax.broadcasted_iota(jnp.int32, (size, size), 1)
        real = lax.broadcasted_iota(jnp.int32, (KP, face), 0) < modes
        for side, pay, got in ((0, pay_a, got_a), (1, pay_b, got_b)):
            cols = slice(side * face, (side + 1) * face)
            residual[:, cols] = pay[:loads, :] + got[:loads, :]
            mine = jnp.where(real, pay[loads:low_row, :], 0.0)
            theirs = jnp.where(real, got[loads:low_row, :], 0.0)
            same = floats[2 + side]
            own_basis[:, cols] = mine
            coarse[:KP, cols] = mine + same * theirs
            coarse[KP : 2 * KP, cols] = (1.0 - same) * theirs
            base = jnp.where(odd, side * half, (1 - side) * half)
            for pair in range(half // 2):
                left = pair * size
                right = (half // 2 + pair) * size
                both = jnp.concatenate(
                    [
                        got[low_row : low_row + mid, left : left + size],
                        got[low_row : low_row + mid, right : right + size],
                    ],
                    axis=0,
                )
                turned = both.T
                diagonal = got[loads + modes : loads + modes + 1, left : left + size]
                upper = jnp.where(row <= col, both, turned)
                lower = jnp.where(row > col, both, jnp.where(row < col, turned, diagonal))
                for k, theirs_block in ((2 * pair, upper), (2 * pair + 1, lower)):
                    pairs[side * half + k, :size, :] = blocks[base + k]
                    pairs[side * half + k, size:, :] = theirs_block.astype(BF16)
        for block in range(count):
            cols = slice(block * size, (block + 1) * size)
            weight = floats[0] if block < half else floats[1]
            modes_here = coarse[: 2 * KP, cols]
            value = jnp.concatenate([residual[:, cols], modes_here], axis=0)
            result = smooth_block(value, weight, pairs[block])
            smooth[:, cols] = result[:loads]
            coarse[2 * KP :, cols] = result[loads:]
            high, low = two_parts(
                jnp.concatenate([result[:loads], modes_here, result[loads:]], axis=0)
            )
            first[:rows, cols] = high
            first[rows:, cols] = low
        vectors = jnp.concatenate([residual[...], smooth[...]], axis=0)
        terms[0] = dot_rows(own_basis[...], vectors)

    def finish(tile, value):
        store_image(tile, floats[4] * value, tiles, image_a, image_b)

    operator_step(
        step, tiles, rows, pick, operator, place, first, second, third, finish
    )

    @pl.when(step == 3 * tiles - 1)
    def _():
        energy = dot_rows(coarse[:, :face], image_a[...]) + dot_rows(coarse[:, face:], image_b[...])
        shared = dot_rows(own_basis[...], coarse[2 * KP :, :])
        terms[1, :, :loads] = energy[:KP, :loads]
        terms[1, :, loads:] = energy[KP : 2 * KP, :loads]
        terms[2, :, :loads] = energy[2 * KP : 3 * KP, :loads]
        terms[2, :, loads:] = energy[3 * KP :, :loads]
        for i in range(2):
            for j in range(2):
                at = (2 * i + j) * 4 * KP
                basis_rows = energy[i * KP : (i + 1) * KP]
                smooth_rows = energy[(2 + i) * KP : (3 + i) * KP]
                basis_cols = slice(loads + j * KP, loads + (j + 1) * KP)
                smooth_cols = slice(loads + (2 + j) * KP, loads + (3 + j) * KP)
                terms[3, :, at : at + KP] = basis_rows[:, basis_cols]
                terms[3, :, at + KP : at + 2 * KP] = basis_rows[:, smooth_cols]
                terms[3, :, at + 2 * KP : at + 3 * KP] = smooth_rows[:, smooth_cols]
                last = shared[:, j * KP : (j + 1) * KP] if i == 0 else jnp.zeros((KP, KP), F32)
                terms[3, :, at + 3 * KP : at + 4 * KP] = last


def coarse_solves(clusters, members, loads, terms, inverse):
    def total(c, kind):
        value = terms[c * members, kind]
        for m in range(1, members):
            value = value + terms[c * members + m, kind]
        return value

    def begin(c, kind):
        return terms[c * members, kind]

    def end(c, kind):
        return terms[c * members + members - 1, kind]

    span = 4 * KP
    lanes = terms.shape[-1]
    totals = [total(c, 0) for c in range(clusters)]
    load_side = [v[:, :loads] for v in totals]
    smooth_side = [v[:, loads:] for v in totals]

    def images(kind):
        found = []
        for c in range(clusters):
            value = total(c, kind)[:, :loads]
            if c + 1 < clusters:
                value = value + begin(c + 1, kind)[:, loads:]
            if c > 0:
                value = value + end(c - 1, kind)[:, loads:]
            found.append(value)
        return found

    centre, below, above = [], [], []
    for c in range(clusters):
        value, under, over = total(c, 3), begin(c, 3), end(c, 3)
        if c + 1 < clusters:
            value = value + pltpu.roll(begin(c + 1, 3), lanes - 3 * span, 1)
            over = over + pltpu.roll(begin(c + 1, 3), lanes - span, 1)
        if c > 0:
            value = value + pltpu.roll(end(c - 1, 3), lanes - 3 * span, 1)
            under = under + pltpu.roll(end(c - 1, 3), lanes - span, 1)
        centre.append(value)
        below.append(under)
        above.append(over)

    def block_times(block, amounts):
        value = block[:, 0:1] * amounts[0:1]
        for k in range(1, KP):
            value = value + block[:, k : k + 1] * amounts[k : k + 1]
        return value

    def times(kind, amounts):
        found = []
        for c in range(clusters):
            near, far = slice(kind * KP, (kind + 1) * KP), slice(span + kind * KP, span + (kind + 1) * KP)
            value = block_times(centre[c][:, near], amounts[c])
            if c > 0:
                value = value + block_times(below[c][:, far], amounts[c - 1])
            if c + 1 < clusters:
                value = value + block_times(above[c][:, far], amounts[c + 1])
            found.append(value)
        return found

    turned_centre = [v.T for v in centre]
    turned_below = [v.T for v in below]
    turned_above = [v.T for v in above]

    def turned_times(kind, amounts):
        found = []
        near, far = slice(kind * KP, (kind + 1) * KP), slice(span + kind * KP, span + (kind + 1) * KP)
        for c in range(clusters):
            value = block_times(turned_centre[c][near], amounts[c])
            if c > 0:
                value = value + block_times(turned_above[c - 1][far], amounts[c - 1])
            if c + 1 < clusters:
                value = value + block_times(turned_below[c + 1][far], amounts[c + 1])
            found.append(value)
        return found

    def solve(parts):
        value = jnp.dot(
            inverse[...], jnp.concatenate(parts, axis=0), precision=EXACT, preferred_element_type=F32
        )
        return [value[c * KP : (c + 1) * KP] for c in range(clusters)]

    def less(left, *others):
        found = list(left)
        for other in others:
            found = [p - q for p, q in zip(found, other)]
        return found

    load_amounts = solve(load_side)
    smooth_amounts = solve(less(smooth_side, times(3, load_amounts)))
    image_amounts = solve(less(images(1), times(1, load_amounts), times(0, smooth_amounts)))
    image_side = less(images(2), times(2, load_amounts), turned_times(1, smooth_amounts))
    smooth_image_amounts = solve(less(image_side, times(3, image_amounts)))
    return load_amounts, smooth_amounts, image_amounts, smooth_image_amounts


def second_kernel(
    clusters, members, tiles,
    ints, floats, terms, inverse, residual, smooth, coarse, pairs, image_a, image_b, got_a, got_b,
    pick, operator, place,
    search, applied, change, next_a, next_b, scalars,
    amounts, columns, first, second, third,
):
    step = pl.program_id(0)
    loads, slots = residual.shape
    face = slots // 2
    count = pairs.shape[0]
    half = count // 2
    size = pairs.shape[2]
    lane = lax.broadcasted_iota(jnp.int32, columns.shape, 1)

    def weighted(left, right):
        product = left * right
        near = jnp.sum(product[:, :face], axis=1, keepdims=True)
        far = jnp.sum(product[:, face:], axis=1, keepdims=True)
        return floats[0] * near + floats[1] * far

    @pl.when(step == 0)
    def _():
        solved = coarse_solves(clusters, members, loads, terms, inverse)
        for kind, parts in enumerate(solved):
            for c, part in enumerate(parts):
                amounts[kind, c] = part

        def local(kind, place_of):
            return [amounts[kind, ints[place_of]], amounts[kind, ints[place_of + 1]]]

        own = jnp.concatenate(local(1, 1) + local(0, 1), axis=0)
        image_own = jnp.concatenate(local(3, 1) + local(2, 1), axis=0)
        projected = residual[...] - dot_modes(own[2 * KP :], coarse[: 2 * KP, :])
        direction = smooth[...] - dot_modes(own, coarse[...])
        search[...] = direction
        for side, image, got in ((0, image_a, got_a), (1, image_b, got_b)):
            theirs = local(1, 3 + 2 * side) + local(0, 3 + 2 * side)
            mixed = jnp.concatenate([own] + theirs, axis=0)
            rows = jnp.concatenate([image[loads:, :], got[loads:, :]], axis=0)
            applied[:, side * face : (side + 1) * face] = (
                image[:loads, :] + got[:loads, :] - dot_modes(mixed, rows)
            )
        image_projected = applied[...] - dot_modes(image_own[2 * KP :], coarse[: 2 * KP, :])
        for block in range(count):
            cols = slice(block * size, (block + 1) * size)
            weight = floats[0] if block < half else floats[1]
            change[:, cols] = smooth_block(applied[:, cols], weight, pairs[block])
        changed = change[...] - dot_modes(image_own, coarse[...])
        change[...] = changed
        high, low = two_parts(changed)
        first[:loads, :] = high
        first[loads:, :] = low
        found = [
            weighted(projected, direction),
            weighted(direction, applied[...]),
            weighted(projected, changed) + weighted(image_projected, direction),
            weighted(image_projected, changed),
        ]
        value = jnp.zeros(columns.shape, F32)
        for k, column in enumerate(found):
            value = jnp.where(lane == k, column, value)
        columns[...] = value

    def finish(tile, value):
        store_image(tile, floats[4] * value, tiles, next_a, next_b)

    operator_step(
        step, tiles, loads, pick, operator, place, first, second, third, finish
    )

    @pl.when(step == 3 * tiles - 1)
    def _():
        value = columns[...]
        for k, vector in ((4, search), (5, change)):
            column = jnp.sum(vector[:, :face] * next_a[...], axis=1, keepdims=True)
            column = column + jnp.sum(vector[:, face:] * next_b[...], axis=1, keepdims=True)
            value = jnp.where(lane == k, column, value)
        turned = value.T
        scalars[...] = turned[:8, :]


def last_kernel(
    ints, scalars, residual, search, applied, change, next_a, next_b, got_a, got_b, out_m, out_r
):
    loads, slots = residual.shape
    face = slots // 2
    total = jnp.sum(scalars[...], axis=0)
    rho = total[0:1]
    gamma = total[1:2]
    alpha = rho / gamma
    rho_next = rho - alpha * total[2:3] + alpha * alpha * total[3:4]
    grow = 1.0 + rho_next / rho
    energy = grow * grow * gamma - 2.0 * grow * alpha * total[4:5] + alpha * alpha * total[5:6]
    alpha_next = rho_next / energy
    lengths = jnp.concatenate(
        [alpha + alpha_next * grow, alpha_next * alpha, jnp.zeros((6, rho.shape[1]), F32)], axis=0
    )
    turned = jnp.concatenate([lengths, jnp.zeros((120, rho.shape[1]), F32)], axis=0).T
    along, against = turned[:loads, 0:1], turned[:loads, 1:2]
    sides = []
    for side, own, got in ((0, next_a, got_a), (1, next_b, got_b)):
        cols = slice(side * face, (side + 1) * face)
        sides.append(
            (
                along * search[:, cols] - against * change[:, cols],
                residual[:, cols] - along * applied[:, cols] + against * (own[...] + got[...]),
            )
        )
    odd = ints[0] == 1
    for k, out in ((0, out_m), (1, out_r)):
        out[:, 0, :] = jnp.where(odd, sides[0][k], sides[1][k])
        out[:, 1, :] = jnp.where(odd, sides[1][k], sides[0][k])


VMEM = pl.BlockSpec(memory_space=pltpu.VMEM)
SMEM = pl.BlockSpec(memory_space=pltpu.SMEM)


def shaped(shape, dtype=F32):
    return jax.ShapeDtypeStruct(shape, dtype)


def whole(shape):
    return pl.BlockSpec(shape, lambda i: (0,) * len(shape))


def per_device(
    dual_load, dual_operator, index_map, stiffness, coarse_basis, dirichlet_blocks, coarse_inverse
):
    loads, _, face = dual_load.shape[2:]
    slots = 2 * face
    modes = coarse_basis.shape[2]
    block_count, size, _ = dirichlet_blocks.shape[2:]
    clusters, members = lax.axis_size("cluster"), lax.axis_size("member")
    devices = clusters * members
    position = lax.axis_index("cluster") * members + lax.axis_index("member")
    int_table, float_table = chain_table(clusters, members)
    ints = lax.dynamic_index_in_dim(jnp.asarray(int_table), position, 0, keepdims=False)
    floats = lax.dynamic_index_in_dim(jnp.asarray(float_table), position, 0, keepdims=False)
    floats = jnp.concatenate([floats, (1.0 / stiffness).reshape(1)])
    load = dual_load.reshape(loads, 2, face)
    basis = coarse_basis.reshape(modes, slots)
    blocks = dirichlet_blocks.reshape(block_count, size, size)

    evens = [(i, i + 1) for i in range(0, devices - 1, 2)]
    odds = [(i, i + 1) for i in range(1, devices - 1, 2)]
    evens = evens + [(j, i) for i, j in evens]
    odds = odds + [(j, i) for i, j in odds]

    def swap(side_a, side_b):
        from_b = lax.ppermute(side_b, AXES, odds)
        from_a = lax.ppermute(side_a, AXES, evens)
        return from_a, from_b

    def share(payload):
        sent = jnp.broadcast_to(payload[None], (devices,) + payload.shape)
        return lax.all_to_all(sent, AXES, 0, 0, tiled=True)

    packed = shaped((loads + KP + size // 2, face))
    pay_a, pay_b = pl.pallas_call(
        functools.partial(pack_kernel, modes),
        out_shape=(packed, packed),
        in_specs=[SMEM, VMEM, VMEM, VMEM],
        out_specs=(VMEM, VMEM),
    )(ints, load, basis, blocks)
    got_a, got_b = swap(pay_a, pay_b)

    by_face = index_map.reshape(2, face)
    flipped = jnp.where(ints[0] == 1, by_face, by_face[::-1]).reshape(slots)
    step_rows = slots // 8
    pick, place = pl.pallas_call(
        order_kernel,
        grid=(8,),
        out_shape=(shaped((slots, slots), BF16), shaped((slots, slots), BF16)),
        in_specs=[pl.BlockSpec((step_rows, 1), lambda i: (i, 0)), whole((1, slots))],
        out_specs=(
            pl.BlockSpec((step_rows, slots), lambda i: (i, 0)),
            pl.BlockSpec((step_rows, slots), lambda i: (i, 0)),
        ),
    )(flipped.reshape(slots, 1), flipped.reshape(1, slots))

    padded = jnp.pad(
        coarse_inverse.reshape(clusters, modes, clusters, modes),
        ((0, 0), (0, KP - modes), (0, 0), (0, KP - modes)),
    ).reshape(clusters * KP, clusters * KP)

    tiles = slots // TILE
    tile_specs = [
        pl.BlockSpec((slots, TILE), lambda i: (0, jnp.clip(i, 0, tiles - 1))),
        pl.BlockSpec((slots, TILE), lambda i: (0, jnp.clip(i - tiles, 0, tiles - 1))),
        pl.BlockSpec((slots, TILE), lambda i: (0, jnp.clip(i - 2 * tiles, 0, tiles - 1))),
    ]
    params = pltpu.CompilerParams(
        dimension_semantics=("arbitrary",), vmem_limit_bytes=48 * 1024 * 1024
    )
    rows = loads + 4 * KP
    pair_shape = (block_count, 2 * size, size)
    residual, smooth, coarse, pairs, image_a, image_b, terms = pl.pallas_call(
        functools.partial(first_kernel, modes, tiles),
        grid=(3 * tiles,),
        out_shape=(
            shaped((loads, slots)),
            shaped((loads, slots)),
            shaped((4 * KP, slots)),
            shaped(pair_shape, BF16),
            shaped((rows, face)),
            shaped((rows, face)),
            shaped((4, KP, 2 * loads)),
        ),
        in_specs=[SMEM, SMEM] + [whole(packed.shape)] * 4 + [whole(blocks.shape)] + tile_specs,
        out_specs=(
            whole((loads, slots)),
            whole((loads, slots)),
            whole((4 * KP, slots)),
            whole(pair_shape),
            whole((rows, face)),
            whole((rows, face)),
            whole((4, KP, 2 * loads)),
        ),
        scratch_shapes=[pltpu.VMEM((KP, slots), F32)] + [pltpu.VMEM((2 * rows, slots), BF16)] * 3,
        compiler_params=params,
    )(ints, floats, pay_a, pay_b, got_a, got_b, blocks, pick, dual_operator, place)

    got_a, got_b = swap(image_a, image_b)
    terms = share(terms)

    vector = whole((loads, slots))
    half_vector = whole((loads, face))
    search, applied, change, next_a, next_b, scalars = pl.pallas_call(
        functools.partial(second_kernel, clusters, members, tiles),
        grid=(3 * tiles,),
        out_shape=(
            shaped((loads, slots)),
            shaped((loads, slots)),
            shaped((loads, slots)),
            shaped((loads, face)),
            shaped((loads, face)),
            shaped((8, loads)),
        ),
        in_specs=[
            SMEM, SMEM, whole(terms.shape), whole(padded.shape), vector, vector,
            whole((4 * KP, slots)), whole(pair_shape),
        ]
        + [whole((rows, face))] * 4
        + tile_specs,
        out_specs=(vector, vector, vector, half_vector, half_vector, whole((8, loads))),
        scratch_shapes=[
            pltpu.VMEM((4, clusters, KP, loads), F32),
            pltpu.VMEM((loads, 128), F32),
        ]
        + [pltpu.VMEM((2 * loads, slots), BF16)] * 3,
        compiler_params=params,
    )(
        ints, floats, terms, padded, residual, smooth, coarse, pairs,
        image_a, image_b, got_a, got_b, pick, dual_operator, place,
    )

    got_a, got_b = swap(next_a, next_b)
    scalars = share(scalars)

    out_m, out_r = pl.pallas_call(
        last_kernel,
        out_shape=(shaped((loads, 2, face)), shaped((loads, 2, face))),
        in_specs=[SMEM] + [VMEM] * 9,
        out_specs=(VMEM, VMEM),
        compiler_params=pltpu.CompilerParams(vmem_limit_bytes=48 * 1024 * 1024),
    )(ints, scalars, residual, search, applied, change, next_a, next_b, got_a, got_b)
    return out_m.reshape(dual_load.shape), out_r.reshape(dual_load.shape)


def solution(mesh):
    in_specs = (
        P("cluster", "member", None, None, None),
        P(),
        P("cluster", "member", None),
        P("cluster", "member"),
        P("cluster", "member", None, None),
        P("cluster", "member", None, None, None),
        P(),
    )
    out_specs = (P("cluster", "member", None, None, None), P("cluster", "member", None, None, None))
    return jax.shard_map(
        per_device, mesh=mesh, in_specs=in_specs, out_specs=out_specs, check_vma=False
    )
```

```python
import functools
from typing import NamedTuple

import jax
import jax.numpy as jnp
from jax import lax
from jax.experimental import pallas as pl
from jax.experimental.pallas import tpu as pltpu
from jax.sharding import PartitionSpec as P

AXES = ("cluster", "member")
F32 = jnp.float32
BF16 = jnp.bfloat16
EXACT = lax.Precision.HIGHEST
KP = 8
TILE = 1024


def dot(left, right):
    return jnp.dot(left, right, preferred_element_type=F32)


def dot_rows(left, right):
    return lax.dot_general(left, right, (((1,), (1,)), ((), ())), preferred_element_type=F32)


def two_parts(value):
    high = value.astype(BF16)
    return high, (value - high.astype(F32)).astype(BF16)


def stacked(value):
    return jnp.concatenate(two_parts(value), axis=0)


def folded(value, rows, cols):
    value = value[:rows] + value[rows:]
    return value[:, :cols] + value[:, cols:]


def three_rows(value):
    high, low = two_parts(value)
    return jnp.concatenate([high, low, high], axis=0)


def dot_modes(amounts, rows):
    high, low = two_parts(amounts)
    left = jnp.concatenate([high, high, low], axis=0)
    return lax.dot_general(left, rows, (((0,), (0,)), ((), ())), preferred_element_type=F32)


class Chain(NamedTuple):
    odd: jax.Array
    own: tuple
    near: tuple
    weights: tuple
    same: tuple


def chain(clusters, members):
    count = clusters * members
    position = lax.axis_index("cluster") * members + lax.axis_index("member")
    parity = lax.rem(position, 2)

    def reach(pos):
        cluster, member = lax.div(pos, members), lax.rem(pos, members)
        other = cluster + jnp.where(member == members - 1, 1, jnp.where(member == 0, -1, 0))
        return cluster, jnp.clip(other, 0, clusters - 1)

    own = reach(position)
    near, weights, same = [], [], []
    for partner in (position + 1 - 2 * parity, position - 1 + 2 * parity):
        real = (partner >= 0) & (partner < count)
        there = reach(jnp.clip(partner, 0, count - 1))
        near.append(there)
        weights.append(jnp.where(real, 0.5, 1.0))
        same.append(jnp.where(real & (there[0] == own[0]), 1.0, 0.0))
    return Chain(parity == 1, own, tuple(near), tuple(weights), tuple(same))


def pack_kernel(
    extent,
    far_load, far_basis, far_blocks,
    out_a, out_b, mine,
    load, basis, blocks, arrived,
):
    copies = [
        pltpu.make_async_copy(source, target, arrived.at[k])
        for k, (source, target) in enumerate(
            ((far_load, load), (far_blocks, blocks), (far_basis, basis))
        )
    ]
    for copy in copies:
        copy.start()
    loads, _, face = load.shape
    modes = basis.shape[0]
    half = blocks.shape[0] // 2
    size = blocks.shape[1]
    odd = chain(*extent).odd
    row = lax.broadcasted_iota(jnp.int32, (size, size), 0)
    col = lax.broadcasted_iota(jnp.int32, (size, size), 1)
    mid = size // 2
    low = loads + mid
    copies[0].wait()
    load_0, load_1 = load[:, 0, :], load[:, 1, :]
    out_a[:loads, :] = jnp.where(odd, load_0, load_1)
    out_b[:loads, :] = jnp.where(odd, load_1, load_0)
    for copy in copies[1:]:
        copy.wait()
    for side, out, first in ((0, out_a, odd), (1, out_b, jnp.logical_not(odd))):
        out[low:, :] = jnp.zeros((KP, face), F32)
        for k in range(modes):
            mode = basis[k]
            out[low + k : low + k + 1, :] = jnp.where(first, mode[:, :face], mode[:, face:])
        base = jnp.where(first, 0, half)
        for pair in range(half // 2):
            mine[side * half + 2 * pair] = blocks[base + 2 * pair]
            mine[side * half + 2 * pair + 1] = blocks[base + 2 * pair + 1]
            upper = blocks[base + 2 * pair].astype(F32)
            lower = blocks[base + 2 * pair + 1].astype(F32)
            both = jnp.where(row <= col, upper, lower)
            left = pair * size
            right = (half // 2 + pair) * size
            out[loads:low, left : left + size] = both[:mid]
            out[loads:low, right : right + size] = both[mid:]
            diagonal = jnp.sum(jnp.where(row == col, lower, 0.0), axis=0, keepdims=True)
            out[low + modes : low + modes + 1, left : left + size] = diagonal


def order_kernel(
    extent,
    far_index, far_operator, stiffness,
    pick, place, operator, softness,
    index, arrived,
):
    copies = [
        pltpu.make_async_copy(far_index, index, arrived.at[0]),
        pltpu.make_async_copy(far_operator, operator, arrived.at[1]),
    ]
    for copy in copies:
        copy.start()
    slots = pick.shape[0]
    face = slots // 2
    rows = 128
    odd = chain(*extent).odd
    lane = lax.broadcasted_iota(jnp.int32, (rows, slots), 1)
    depth = lax.broadcasted_iota(jnp.int32, (rows, slots), 0)
    one, zero = jnp.ones((), F32), jnp.zeros((), F32)
    softness[...] = 1.0 / stiffness[...]
    copies[0].wait()
    index_0, index_1 = index[:, :face], index[:, face:]
    wanted = jnp.concatenate(
        [jnp.where(odd, index_0, index_1), jnp.where(odd, index_1, index_0)], axis=1
    )
    for start in range(0, slots, rows):
        here = jnp.broadcast_to(wanted[:, start : start + rows].astype(F32), (rows, rows)).T
        target = jnp.concatenate([here] * (slots // rows), axis=1).astype(jnp.int32)
        pick[start : start + rows, :] = jnp.where(target == lane, one, zero).astype(BF16)
        place[start : start + rows, :] = jnp.where(wanted == depth + start, one, zero).astype(BF16)
    copies[1].wait()


def merge_kernel(keep, got, out):
    kinds, depth, lanes = keep.shape
    rows = got.shape[0] - depth
    for kind in range(kinds):
        value = keep[kind] + got[rows:, kind * lanes : (kind + 1) * lanes]
        out[:, kind * depth : (kind + 1) * depth, :] = jnp.broadcast_to(
            value[None], (out.shape[0], depth, lanes)
        )


def operator_apply(rows, scale, pick, operator, place, first, second, third, image_a, image_b):
    slots = first.shape[1]
    face = slots // 2

    @pl.loop(0, slots // TILE)
    def _(tile):
        cols = pl.ds(pl.multiple_of(tile * TILE, TILE), TILE)
        second[:, cols] = dot(first[...], pick[:, cols]).astype(BF16)

    @pl.loop(0, slots // TILE)
    def _(tile):
        cols = pl.ds(pl.multiple_of(tile * TILE, TILE), TILE)
        product = dot(second[...], operator[:, cols])
        high, low = two_parts(product[:rows] + product[rows:])
        third[:rows, cols] = high
        third[rows:, cols] = low

    for side, image in ((0, image_a), (1, image_b)):
        product = dot(third[...], place[:, side * face : (side + 1) * face])
        image[:rows, :] = scale * (product[:rows] + product[rows:])


def smooth_block(value, weight, block_pair):
    rows = value.shape[0]
    high, low = two_parts(weight * value)
    left = jnp.concatenate(
        [jnp.concatenate([high, high], axis=1), jnp.concatenate([low, low], axis=1)], axis=0
    )
    product = dot(left, block_pair)
    return weight * (product[:rows] + product[rows:])


def first_kernel(
    extent, modes,
    softness, pay_a, pay_b, got_a, got_b, blocks, pick, operator, place,
    residual, smooth, coarse, pairs, image_a, image_b, keep,
    first, second, third, terms,
):
    loads, slots = residual.shape
    face = slots // 2
    count = pairs.shape[0]
    half = count // 2
    size = pairs.shape[2]
    rows = loads + 4 * KP
    mid = size // 2
    low = loads + mid
    here = chain(*extent)
    odd = here.odd
    row = lax.broadcasted_iota(jnp.int32, (size, size), 0)
    col = lax.broadcasted_iota(jnp.int32, (size, size), 1)
    real = lax.broadcasted_iota(jnp.int32, (KP, face), 0) < modes
    own_basis, span = [], []
    for side, pay, got in ((0, pay_a, got_a), (1, pay_b, got_b)):
        cols = slice(side * face, (side + 1) * face)
        residual[:, cols] = pay[:loads, :] + got[:loads, :]
        mine = jnp.where(real, pay[low:, :], 0.0)
        theirs = jnp.where(real, got[low:, :], 0.0)
        same = here.same[side]
        own_basis.append(mine)
        span.append(jnp.concatenate([mine + same * theirs, (1.0 - same) * theirs], axis=0))
        for pair in range(half // 2):
            left = pair * size
            right = (half // 2 + pair) * size
            both = jnp.concatenate(
                [got[loads:low, left : left + size], got[loads:low, right : right + size]], axis=0
            )
            turned = both.T
            diagonal = got[low + modes : low + modes + 1, left : left + size]
            upper = jnp.where(row <= col, both, turned)
            lower = jnp.where(row > col, both, jnp.where(row < col, turned, diagonal))
            for k, theirs_block in ((2 * pair, upper), (2 * pair + 1, lower)):
                pairs[side * half + k, :size, :] = blocks[side * half + k]
                pairs[side * half + k, size:, :] = theirs_block.astype(BF16)
    for block in range(count):
        side, k = divmod(block, half)
        cols = slice(block * size, (block + 1) * size)
        modes_here = span[side][:, k * size : (k + 1) * size]
        value = jnp.concatenate([residual[:, cols], modes_here], axis=0)
        result = smooth_block(value, here.weights[side], pairs[block])
        smooth[:, cols] = result[:loads]
        high, low = two_parts(jnp.concatenate([result[:loads], modes_here, result[loads:]], axis=0))
        first[:rows, cols] = high
        first[rows:, cols] = low
        coarse[: 4 * KP, cols] = high[loads:]
        coarse[4 * KP : 8 * KP, cols] = low[loads:]
        coarse[8 * KP :, cols] = high[loads:]

    operator_apply(
        rows, softness[...], pick, operator, place, first, second, third, image_a, image_b
    )

    basis = stacked(jnp.concatenate(own_basis, axis=1))
    load_side = folded(dot_rows(basis, stacked(residual[...])), KP, loads)
    smooth_side = folded(dot_rows(basis, first[...]), KP, rows)
    shared = smooth_side[:, loads + 2 * KP :]
    energy = jnp.zeros((8 * KP, 2 * rows), F32)
    for side, image in ((0, image_a), (1, image_b)):
        cols = slice(side * face, (side + 1) * face)
        energy = energy + dot_rows(coarse[: 8 * KP, cols], stacked(image[:rows, :]))
    energy = folded(energy, 4 * KP, rows)
    terms[0, :, :loads] = load_side
    terms[0, :, loads:] = smooth_side[:, :loads]
    terms[1, :, :loads] = energy[:KP, :loads]
    terms[1, :, loads:] = energy[KP : 2 * KP, :loads]
    terms[2, :, :loads] = energy[2 * KP : 3 * KP, :loads]
    terms[2, :, loads:] = energy[3 * KP :, :loads]
    for i in range(2):
        for j in range(2):
            at = (2 * i + j) * 4 * KP
            basis_rows = energy[i * KP : (i + 1) * KP]
            smooth_rows = energy[(2 + i) * KP : (3 + i) * KP]
            basis_cols = slice(loads + j * KP, loads + (j + 1) * KP)
            smooth_cols = slice(loads + (2 + j) * KP, loads + (3 + j) * KP)
            terms[3, :, at : at + KP] = basis_rows[:, basis_cols]
            terms[3, :, at + KP : at + 2 * KP] = basis_rows[:, smooth_cols]
            terms[3, :, at + 2 * KP : at + 3 * KP] = smooth_rows[:, smooth_cols]
            last = shared[:, j * KP : (j + 1) * KP] if i == 0 else jnp.zeros((KP, KP), F32)
            terms[3, :, at + 3 * KP : at + 4 * KP] = last
    keep[...] = jnp.where(odd, terms[2:], terms[:2])
    image_a[rows:, :] = jnp.zeros((KP, face), F32)
    for kind in range(2):
        image_a[rows:, kind * 2 * loads : (kind + 1) * 2 * loads] = jnp.where(
            odd, terms[kind], terms[2 + kind]
        )


def coarse_solves(clusters, members, loads, odd, terms, other_terms, inverse):
    def pick_kind(kind, mine, theirs):
        return jnp.where(odd, theirs, mine) if kind < 2 else jnp.where(odd, mine, theirs)

    def rows_of(kind):
        return slice(kind % 2 * KP, kind % 2 * KP + KP)

    def total(c, kind):
        pairs = members // 2
        found = [ref[c * pairs, rows_of(kind)] for ref in (terms, other_terms)]
        for m in range(1, pairs):
            found = [
                v + ref[c * pairs + m, rows_of(kind)]
                for v, ref in zip(found, (terms, other_terms))
            ]
        return pick_kind(kind, *found)

    def one(pair, kind):
        return pick_kind(kind, terms[pair, rows_of(kind)], other_terms[pair, rows_of(kind)])

    def begin(c, kind):
        return one(c * members // 2, kind)

    def end(c, kind):
        return one((c + 1) * members // 2 - 1, kind)

    span = 4 * KP
    lanes = terms.shape[-1]
    totals = [total(c, 0) for c in range(clusters)]
    load_side = [v[:, :loads] for v in totals]
    smooth_side = [v[:, loads:] for v in totals]

    def images(kind):
        found = []
        for c in range(clusters):
            value = total(c, kind)[:, :loads]
            if c + 1 < clusters:
                value = value + begin(c + 1, kind)[:, loads:]
            if c > 0:
                value = value + end(c - 1, kind)[:, loads:]
            found.append(value)
        return found

    centre, below, above = [], [], []
    for c in range(clusters):
        value, under, over = total(c, 3), begin(c, 3), end(c, 3)
        if c + 1 < clusters:
            value = value + pltpu.roll(begin(c + 1, 3), lanes - 3 * span, 1)
            over = over + pltpu.roll(begin(c + 1, 3), lanes - span, 1)
        if c > 0:
            value = value + pltpu.roll(end(c - 1, 3), lanes - 3 * span, 1)
            under = under + pltpu.roll(end(c - 1, 3), lanes - span, 1)
        centre.append(value)
        below.append(under)
        above.append(over)

    def block_times(block, amounts):
        value = block[:, 0:1] * amounts[0:1]
        for k in range(1, KP):
            value = value + block[:, k : k + 1] * amounts[k : k + 1]
        return value

    def times(kind, amounts):
        found = []
        for c in range(clusters):
            near, far = slice(kind * KP, (kind + 1) * KP), slice(span + kind * KP, span + (kind + 1) * KP)
            value = block_times(centre[c][:, near], amounts[c])
            if c > 0:
                value = value + block_times(below[c][:, far], amounts[c - 1])
            if c + 1 < clusters:
                value = value + block_times(above[c][:, far], amounts[c + 1])
            found.append(value)
        return found

    turned_centre = [v.T for v in centre]
    turned_below = [v.T for v in below]
    turned_above = [v.T for v in above]

    def turned_times(kind, amounts):
        found = []
        near, far = slice(kind * KP, (kind + 1) * KP), slice(span + kind * KP, span + (kind + 1) * KP)
        for c in range(clusters):
            value = block_times(turned_centre[c][near], amounts[c])
            if c > 0:
                value = value + block_times(turned_above[c - 1][far], amounts[c - 1])
            if c + 1 < clusters:
                value = value + block_times(turned_below[c + 1][far], amounts[c + 1])
            found.append(value)
        return found

    modes = inverse.shape[0] // clusters
    row = lax.broadcasted_iota(jnp.int32, (clusters * KP, clusters * modes), 0)
    col = lax.broadcasted_iota(jnp.int32, (clusters * KP, clusters * modes), 1)
    mode = row % KP
    spread = jnp.where((mode < modes) & (col == row // KP * modes + mode), 1.0, 0.0)
    padded = jnp.dot(spread, inverse[...], precision=EXACT, preferred_element_type=F32)
    padded = lax.dot_general(
        padded, spread, (((1,), (1,)), ((), ())), precision=EXACT, preferred_element_type=F32
    )

    def solve(parts):
        value = jnp.dot(
            padded, jnp.concatenate(parts, axis=0), precision=EXACT, preferred_element_type=F32
        )
        return [value[c * KP : (c + 1) * KP] for c in range(clusters)]

    def less(left, *others):
        found = list(left)
        for other in others:
            found = [p - q for p, q in zip(found, other)]
        return found

    load_amounts = solve(load_side)
    smooth_amounts = solve(less(smooth_side, times(3, load_amounts)))
    image_amounts = solve(less(images(1), times(1, load_amounts), times(0, smooth_amounts)))
    image_side = less(images(2), times(2, load_amounts), turned_times(1, smooth_amounts))
    smooth_image_amounts = solve(less(image_side, times(3, image_amounts)))
    return load_amounts, smooth_amounts, image_amounts, smooth_image_amounts


def second_kernel(
    extent,
    softness, terms, other_terms, inverse, residual, smooth, coarse, pairs, image_a, image_b, got_a, got_b,
    pick, operator, place,
    search, applied, change, next_a, next_b, scalars,
    amounts, first, second, third,
):
    loads, slots = residual.shape
    face = slots // 2
    count = pairs.shape[0]
    half = count // 2
    size = pairs.shape[2]
    clusters, members = extent
    here = chain(*extent)

    def weighted(left, right):
        product = left * right
        near = jnp.sum(product[:, :face], axis=1, keepdims=True)
        far = jnp.sum(product[:, face:], axis=1, keepdims=True)
        return here.weights[0] * near + here.weights[1] * far

    solved = coarse_solves(clusters, members, loads, here.odd, terms, other_terms, inverse)
    for kind, parts in enumerate(solved):
        for c, part in enumerate(parts):
            amounts[kind, c] = part

    def local(kind, reached):
        return [amounts[kind, c] for c in reached]

    none = [jnp.zeros((2 * KP, loads), F32)]
    own = jnp.concatenate(local(1, here.own) + local(0, here.own), axis=0)
    image_own = jnp.concatenate(local(3, here.own) + local(2, here.own), axis=0)
    own_basis = jnp.concatenate(local(0, here.own) + none, axis=0)
    image_own_basis = jnp.concatenate(local(2, here.own) + none, axis=0)
    projected = residual[...] - dot_modes(own_basis, coarse[...])
    direction = smooth[...] - dot_modes(own, coarse[...])
    search[...] = direction
    for side, image, got in ((0, image_a, got_a), (1, image_b, got_b)):
        theirs = local(1, here.near[side]) + local(0, here.near[side])
        mixed = jnp.concatenate([own] + theirs, axis=0)
        rows = slice(loads, loads + 4 * KP)
        rows = three_rows(jnp.concatenate([image[rows, :], got[rows, :]], axis=0))
        applied[:, side * face : (side + 1) * face] = (
            image[:loads, :] + got[:loads, :] - dot_modes(mixed, rows)
        )
    image_projected = applied[...] - dot_modes(image_own_basis, coarse[...])
    for block in range(count):
        cols = slice(block * size, (block + 1) * size)
        weight = here.weights[block // half]
        change[:, cols] = smooth_block(applied[:, cols], weight, pairs[block])
    changed = change[...] - dot_modes(image_own, coarse[...])
    change[...] = changed
    high, low = two_parts(changed)
    first[:loads, :] = high
    first[loads:, :] = low
    found = [
        weighted(projected, direction),
        weighted(direction, applied[...]),
        weighted(projected, changed) + weighted(image_projected, direction),
        weighted(image_projected, changed),
    ]

    operator_apply(
        loads, softness[...], pick, operator, place, first, second, third, next_a, next_b
    )

    for vector in (search, change):
        column = jnp.sum(vector[:, :face] * next_a[...], axis=1, keepdims=True)
        column = column + jnp.sum(vector[:, face:] * next_b[...], axis=1, keepdims=True)
        found.append(column)
    lane = lax.broadcasted_iota(jnp.int32, (loads, 128), 1)
    value = jnp.zeros(lane.shape, F32)
    for k, column in enumerate(found):
        value = jnp.where(lane == k, column, value)
    turned = value.T
    scalars[:, :loads] = turned[:4, :]
    scalars[:, loads:] = turned[4:8, :]


def last_kernel(
    extent, scalars, residual, search, applied, change, next_a, next_b, got_a, got_b, out_m, out_r
):
    loads, slots = residual.shape
    face = slots // 2
    total = jnp.sum(scalars[...], axis=0)
    total = jnp.concatenate([total[:, :loads], total[:, loads:]], axis=0)
    rho = total[0:1]
    gamma = total[1:2]
    alpha = rho / gamma
    rho_next = rho - alpha * total[2:3] + alpha * alpha * total[3:4]
    grow = 1.0 + rho_next / rho
    energy = grow * grow * gamma - 2.0 * grow * alpha * total[4:5] + alpha * alpha * total[5:6]
    alpha_next = rho_next / energy
    lengths = jnp.concatenate(
        [alpha + alpha_next * grow, alpha_next * alpha, jnp.zeros((6, rho.shape[1]), F32)], axis=0
    )
    turned = jnp.concatenate([lengths, jnp.zeros((120, rho.shape[1]), F32)], axis=0).T
    along, against = turned[:loads, 0:1], turned[:loads, 1:2]
    sides = []
    for side, own, got in ((0, next_a, got_a), (1, next_b, got_b)):
        cols = slice(side * face, (side + 1) * face)
        sides.append(
            (
                along * search[:, cols] - against * change[:, cols],
                residual[:, cols] - along * applied[:, cols] + against * (own[...] + got[...]),
            )
        )
    odd = chain(*extent).odd
    for k, out in ((0, out_m), (1, out_r)):
        out[:, 0, :] = jnp.where(odd, sides[0][k], sides[1][k])
        out[:, 1, :] = jnp.where(odd, sides[1][k], sides[0][k])


VMEM = pl.BlockSpec(memory_space=pltpu.VMEM)
HBM = pl.BlockSpec(memory_space=pltpu.HBM)


def shaped(shape, dtype=F32):
    return jax.ShapeDtypeStruct(shape, dtype)


def in_hbm(value):
    return pltpu.with_memory_space_constraint(value, pltpu.HBM)


def per_device(
    dual_load, dual_operator, index_map, stiffness, coarse_basis, dirichlet_blocks, coarse_inverse
):
    loads, _, face = dual_load.shape[2:]
    slots = 2 * face
    modes = coarse_basis.shape[2]
    block_count, size, _ = dirichlet_blocks.shape[2:]
    clusters, members = lax.axis_size("cluster"), lax.axis_size("member")
    devices = clusters * members
    extent = clusters, members
    load = dual_load.reshape(loads, 2, face)
    basis = coarse_basis.reshape(modes, 1, slots)
    blocks = dirichlet_blocks.reshape(block_count, size, size)

    evens = [(i, i + 1) for i in range(0, devices - 1, 2)]
    odds = [(i, i + 1) for i in range(1, devices - 1, 2)]
    evens = evens + [(j, i) for i, j in evens]
    odds = odds + [(j, i) for i, j in odds]

    def swap(side_a, side_b):
        from_b = lax.ppermute(side_b, AXES, odds)
        from_a = lax.ppermute(side_a, AXES, evens)
        return from_a, from_b

    def share(copies, groups=None):
        return lax.all_to_all(copies, AXES, 0, 0, axis_index_groups=groups, tiled=True)

    def params(mebibytes):
        return pltpu.CompilerParams(vmem_limit_bytes=mebibytes * 1024 * 1024)

    half_vector = shaped((loads, face))
    vector = shaped((loads, slots))
    packed = shaped((loads + size // 2 + KP, face))
    pay_a, pay_b, mine = pl.pallas_call(
        functools.partial(pack_kernel, extent),
        out_shape=(packed, packed, shaped(blocks.shape, BF16)),
        in_specs=[HBM] * 3,
        out_specs=(VMEM,) * 3,
        scratch_shapes=[
            pltpu.VMEM(load.shape, F32),
            pltpu.VMEM(basis.shape, F32),
            pltpu.VMEM(blocks.shape, BF16),
            pltpu.SemaphoreType.DMA((3,)),
        ],
        compiler_params=params(8),
    )(*[in_hbm(v) for v in (load, basis, blocks)])
    got_a, got_b = swap(pay_a, pay_b)

    ordering = shaped((slots, slots), BF16)
    pick, place, operator, softness = pl.pallas_call(
        functools.partial(order_kernel, extent),
        out_shape=(ordering, ordering, ordering, shaped((1, 1))),
        in_specs=[HBM, HBM, VMEM],
        out_specs=(VMEM,) * 4,
        scratch_shapes=[pltpu.VMEM((1, slots), jnp.int32), pltpu.SemaphoreType.DMA((2,))],
        compiler_params=params(8),
    )(in_hbm(index_map.reshape(1, slots)), in_hbm(dual_operator), stiffness)
    pick, operator, place = [
        pltpu.with_memory_space_constraint(v, pltpu.VMEM) for v in (pick, operator, place)
    ]

    rows = loads + 4 * KP
    residual, smooth, coarse, pairs, image_a, image_b, keep = pl.pallas_call(
        functools.partial(first_kernel, extent, modes),
        out_shape=(
            vector,
            vector,
            shaped((12 * KP, slots), BF16),
            shaped((block_count, 2 * size, size), BF16),
            shaped((rows + KP, face)),
            shaped((rows, face)),
            shaped((2, KP, 2 * loads)),
        ),
        in_specs=[VMEM] * 9,
        out_specs=(VMEM,) * 7,
        scratch_shapes=[pltpu.VMEM((2 * rows, slots), BF16)] * 3
        + [pltpu.VMEM((4, KP, 2 * loads), F32)],
        compiler_params=params(20),
    )(softness, pay_a, pay_b, got_a, got_b, mine, pick, operator, place)

    got_a, got_b = swap(image_a, image_b)
    terms = pl.pallas_call(
        merge_kernel,
        out_shape=shaped((devices // 2, 2 * KP, 2 * loads)),
        in_specs=[VMEM] * 2,
        out_specs=VMEM,
        compiler_params=params(8),
    )(keep, got_a)
    terms = share(terms, [list(range(k, devices, 2)) for k in range(2)])
    other_terms = lax.ppermute(terms, AXES, evens)

    search, applied, change, next_a, next_b, scalars = pl.pallas_call(
        functools.partial(second_kernel, extent),
        out_shape=(vector, vector, vector, half_vector, half_vector, shaped((4, 2 * loads))),
        in_specs=[VMEM] * 15,
        out_specs=(VMEM,) * 6,
        scratch_shapes=[pltpu.VMEM((4, clusters, KP, loads), F32)]
        + [pltpu.VMEM((2 * loads, slots), BF16)] * 3,
        compiler_params=params(20),
    )(
        softness, terms, other_terms, coarse_inverse, residual, smooth, coarse, pairs,
        image_a, image_b, got_a, got_b, pick, operator, place,
    )

    got_a, got_b = swap(next_a, next_b)
    scalars = share(jnp.broadcast_to(scalars[None], (devices,) + scalars.shape))

    out_m, out_r = pl.pallas_call(
        functools.partial(last_kernel, extent),
        out_shape=(shaped((loads, 2, face)), shaped((loads, 2, face))),
        in_specs=[VMEM] * 9,
        out_specs=(VMEM, VMEM),
        compiler_params=params(20),
    )(scalars, residual, search, applied, change, next_a, next_b, got_a, got_b)
    return out_m.reshape(dual_load.shape), out_r.reshape(dual_load.shape)


def solution(mesh):
    in_specs = (
        P("cluster", "member", None, None, None),
        P(),
        P("cluster", "member", None),
        P("cluster", "member"),
        P("cluster", "member", None, None),
        P("cluster", "member", None, None, None),
        P(),
    )
    out_specs = (P("cluster", "member", None, None, None), P("cluster", "member", None, None, None))
    return jax.shard_map(
        per_device, mesh=mesh, in_specs=in_specs, out_specs=out_specs, check_vma=False
    )
```

```python
import functools
from typing import NamedTuple

import jax
import jax.numpy as jnp
from jax import lax
from jax.experimental import pallas as pl
from jax.experimental.pallas import tpu as pltpu
from jax.sharding import PartitionSpec as P

AXES = ("cluster", "member")
F32 = jnp.float32
BF16 = jnp.bfloat16
EXACT = lax.Precision.HIGHEST
KP = 8
TILE = 1024


def dot(left, right):
    return jnp.dot(left, right, preferred_element_type=F32)


def dot_rows(left, right):
    return lax.dot_general(left, right, (((1,), (1,)), ((), ())), preferred_element_type=F32)


def two_parts(value):
    high = value.astype(BF16)
    return high, (value - high.astype(F32)).astype(BF16)


def stacked(value):
    return jnp.concatenate(two_parts(value), axis=0)


def folded(value, rows, cols):
    value = value[:rows] + value[rows:]
    return value[:, :cols] + value[:, cols:]


def three_rows(value):
    high, low = two_parts(value)
    return jnp.concatenate([high, low, high], axis=0)


def dot_modes(amounts, rows):
    high, low = two_parts(amounts)
    left = jnp.concatenate([high, high, low], axis=0)
    return lax.dot_general(left, rows, (((0,), (0,)), ((), ())), preferred_element_type=F32)


class Chain(NamedTuple):
    odd: jax.Array
    own: tuple
    near: tuple
    weights: tuple
    same: tuple


def chain(clusters, members):
    count = clusters * members
    position = lax.axis_index("cluster") * members + lax.axis_index("member")
    parity = lax.rem(position, 2)

    def reach(pos):
        cluster, member = lax.div(pos, members), lax.rem(pos, members)
        other = cluster + jnp.where(member == members - 1, 1, jnp.where(member == 0, -1, 0))
        return cluster, jnp.clip(other, 0, clusters - 1)

    own = reach(position)
    near, weights, same = [], [], []
    for partner in (position + 1 - 2 * parity, position - 1 + 2 * parity):
        real = (partner >= 0) & (partner < count)
        there = reach(jnp.clip(partner, 0, count - 1))
        near.append(there)
        weights.append(jnp.where(real, 0.5, 1.0))
        same.append(jnp.where(real & (there[0] == own[0]), 1.0, 0.0))
    return Chain(parity == 1, own, tuple(near), tuple(weights), tuple(same))


def pack_side(first, load, basis, blocks, out, mine):
    loads, _, face = load.shape
    modes = basis.shape[0]
    half = blocks.shape[0] // 2
    size = blocks.shape[1]
    row = lax.broadcasted_iota(jnp.int32, (size, size), 0)
    col = lax.broadcasted_iota(jnp.int32, (size, size), 1)
    mid = size // 2
    low = mid + KP
    out[mid:low, :] = jnp.zeros((KP, face), F32)
    for k in range(modes):
        mode = basis[k]
        out[mid + k : mid + k + 1, :] = jnp.where(first, mode[:, :face], mode[:, face:])
    base = jnp.where(first, 0, half)
    for pair in range(half // 2):
        one, two = blocks[base + 2 * pair], blocks[base + 2 * pair + 1]
        mine[2 * pair] = one
        mine[2 * pair + 1] = two
        upper, lower = one.astype(F32), two.astype(F32)
        both = jnp.where(row <= col, upper, lower)
        left = pair * size
        right = (half // 2 + pair) * size
        out[:mid, left : left + size] = both[:mid]
        out[:mid, right : right + size] = both[mid:]
        diagonal = jnp.sum(jnp.where(row == col, lower, 0.0), axis=0, keepdims=True)
        out[mid + modes : mid + modes + 1, left : left + size] = diagonal
    out[low:, :] = jnp.where(first, load[:, 0, :], load[:, 1, :])


def pack_kernel(
    extent,
    far_load, far_basis, far_blocks,
    out_a, out_b, mine_a, mine_b,
    load, basis, blocks, arrived,
):
    copies = [
        pltpu.make_async_copy(source, target, arrived.at[k])
        for k, (source, target) in enumerate(
            ((far_blocks, blocks), (far_load, load), (far_basis, basis))
        )
    ]
    for copy in copies:
        copy.start()
    for copy in copies:
        copy.wait()
    odd = chain(*extent).odd
    pack_side(jnp.logical_not(odd), load, basis, blocks, out_b, mine_b)
    pack_side(odd, load, basis, blocks, out_a, mine_a)


def order_kernel(
    extent,
    far_index, stiffness, far_operator,
    pick, place, operator, softness,
    index, arrived,
):
    copies = [
        pltpu.make_async_copy(far_index, index, arrived.at[0]),
        pltpu.make_async_copy(far_operator, operator, arrived.at[1]),
    ]
    for copy in copies:
        copy.start()
    slots = pick.shape[0]
    face = slots // 2
    rows = 128
    odd = chain(*extent).odd
    softness[...] = 1.0 / stiffness[...]
    copies[0].wait()
    lane = lax.broadcasted_iota(jnp.int32, (rows, slots), 1).astype(jnp.int16)
    depth = lax.broadcasted_iota(jnp.int32, (rows, slots), 0).astype(jnp.int16)
    one, zero = jnp.ones((), BF16), jnp.zeros((), BF16)
    index_0, index_1 = index[:, :face], index[:, face:]
    wanted = jnp.concatenate(
        [jnp.where(odd, index_0, index_1), jnp.where(odd, index_1, index_0)], axis=1
    )
    every = jnp.broadcast_to(wanted, (rows, slots)).astype(jnp.int16)
    for start in range(0, slots, rows):
        here = jnp.broadcast_to(wanted[:, start : start + rows].astype(F32), (rows, rows)).T
        here = here.astype(jnp.int32).astype(jnp.int16)
        target = jnp.concatenate([here] * (slots // rows), axis=1)
        pick[start : start + rows, :] = jnp.where(target == lane, one, zero)
        place[start : start + rows, :] = jnp.where(every - jnp.int16(start) == depth, one, zero)
    copies[1].wait()


def merge_kernel(keep, got, out):
    kinds, depth, lanes = keep.shape
    rows = got.shape[0] - depth
    for kind in range(kinds):
        value = keep[kind] + got[rows:, kind * lanes : (kind + 1) * lanes]
        out[:, kind * depth : (kind + 1) * depth, :] = jnp.broadcast_to(
            value[None], (out.shape[0], depth, lanes)
        )


def apply_rest(rows, scale, operator, place, second, third, image_a, image_b):
    slots = second.shape[1]
    face = slots // 2

    @pl.loop(0, slots // TILE)
    def _(tile):
        cols = pl.ds(pl.multiple_of(tile * TILE, TILE), TILE)
        product = dot(second[...], operator[:, cols])
        high, low = two_parts(product[:rows] + product[rows:])
        third[:rows, cols] = high
        third[rows:, cols] = low

    for side, image in ((0, image_a), (1, image_b)):
        product = dot(third[...], place[:, side * face : (side + 1) * face])
        image[:rows, :] = scale * (product[:rows] + product[rows:])


def smooth_block(value, weight, block_pair):
    rows = value.shape[0]
    high, low = two_parts(weight * value)
    left = jnp.concatenate(
        [jnp.concatenate([high, high], axis=1), jnp.concatenate([low, low], axis=1)], axis=0
    )
    product = dot(left, block_pair)
    return weight * (product[:rows] + product[rows:])


def side_part(
    modes, at, weight, same, pay, got, blocks, residual, smooth, coarse, own_basis, pairs, first
):
    half, size, _ = blocks.shape
    face = half * size
    loads = pay.shape[0] - size // 2 - KP
    rows = loads + 4 * KP
    mid = size // 2
    low = mid + KP
    cols = slice(at, at + face)
    row = lax.broadcasted_iota(jnp.int32, (size, size), 0)
    col = lax.broadcasted_iota(jnp.int32, (size, size), 1)
    real = lax.broadcasted_iota(jnp.int32, (KP, face), 0) < modes
    mine = jnp.where(real, pay[mid:low, :], 0.0)
    theirs = jnp.where(real, got[mid:low, :], 0.0)
    own_basis[:, cols] = stacked(mine)
    span = jnp.concatenate([mine + same * theirs, (1.0 - same) * theirs], axis=0)
    for pair in range(half // 2):
        left = pair * size
        right = (half // 2 + pair) * size
        both = jnp.concatenate(
            [got[:mid, left : left + size], got[:mid, right : right + size]], axis=0
        )
        turned = both.T
        diagonal = got[mid + modes : mid + modes + 1, left : left + size]
        upper = jnp.where(row <= col, both, turned)
        lower = jnp.where(row > col, both, jnp.where(row < col, turned, diagonal))
        for k, theirs_block in ((2 * pair, upper), (2 * pair + 1, lower)):
            block_pair = jnp.concatenate([blocks[k], theirs_block.astype(BF16)], axis=0)
            pairs[k] = block_pair
            there = slice(k * size, (k + 1) * size)
            cols = slice(at + k * size, at + (k + 1) * size)
            value = pay[low:, there] + got[low:, there]
            modes_here = span[:, there]
            result = smooth_block(
                jnp.concatenate([value, modes_here], axis=0), weight, block_pair
            )
            residual[:, cols] = value
            smooth[:, cols] = result[:loads]
            high, low_part = two_parts(
                jnp.concatenate([result[:loads], modes_here, result[loads:]], axis=0)
            )
            first[:rows, cols] = high
            first[rows:, cols] = low_part
            coarse[: 4 * KP, cols] = high[loads:]
            coarse[4 * KP : 8 * KP, cols] = low_part[loads:]
            coarse[8 * KP :, cols] = high[loads:]


def near_kernel(
    extent, modes,
    pay, got, blocks, pick,
    residual, smooth, coarse, own_basis, pairs, first, second,
):
    here = chain(*extent)
    side_part(
        modes, 0, here.weights[0], here.same[0], pay, got, blocks,
        residual, smooth, coarse, own_basis, pairs, first,
    )
    slots = second.shape[1]
    face = first.shape[1]

    @pl.loop(0, slots // TILE)
    def _(tile):
        cols = pl.ds(pl.multiple_of(tile * TILE, TILE), TILE)
        second[:, cols] = dot(first[...], pick[:face, cols]).astype(BF16)


def first_kernel(
    extent, modes,
    softness, pay, got, blocks,
    residual_a, smooth_a, coarse_a, own_basis_a, first_a, second_a,
    pick, operator, place,
    residual, smooth, coarse, pairs, image_a, image_b, keep,
    own_basis, first, second, third, terms,
):
    loads, slots = residual.shape
    face = slots // 2
    rows = loads + 4 * KP
    here = chain(*extent)
    side_part(
        modes, face, here.weights[1], here.same[1], pay, got, blocks,
        residual, smooth, coarse, own_basis, pairs, first,
    )

    @pl.loop(0, slots // TILE)
    def _(tile):
        cols = pl.ds(pl.multiple_of(tile * TILE, TILE), TILE)
        product = dot(first[:, face:], pick[face:, cols]) + second_a[:, cols].astype(F32)
        second[:, cols] = product.astype(BF16)

    for whole, part in (
        (residual, residual_a), (smooth, smooth_a), (coarse, coarse_a),
        (own_basis, own_basis_a), (first, first_a),
    ):
        whole[:, :face] = part[...]
    apply_rest(rows, softness[...], operator, place, second, third, image_a, image_b)

    vectors = jnp.concatenate([stacked(residual[...]), first[...]], axis=0)
    sides = dot_rows(own_basis[...], vectors)
    load_side = folded(sides[:, : 2 * loads], KP, loads)
    smooth_side = folded(sides[:, 2 * loads :], KP, rows)
    shared = smooth_side[:, loads + 2 * KP :]
    energy = jnp.zeros((8 * KP, 2 * rows), F32)
    for side, image in ((0, image_a), (1, image_b)):
        cols = slice(side * face, (side + 1) * face)
        energy = energy + dot_rows(coarse[: 8 * KP, cols], stacked(image[:rows, :]))
    energy = folded(energy, 4 * KP, rows)
    terms[0, :, :loads] = load_side
    terms[0, :, loads:] = smooth_side[:, :loads]
    terms[1, :, :loads] = energy[:KP, :loads]
    terms[1, :, loads:] = energy[KP : 2 * KP, :loads]
    terms[2, :, :loads] = energy[2 * KP : 3 * KP, :loads]
    terms[2, :, loads:] = energy[3 * KP :, :loads]
    for i in range(2):
        for j in range(2):
            at = (2 * i + j) * 4 * KP
            basis_rows = energy[i * KP : (i + 1) * KP]
            smooth_rows = energy[(2 + i) * KP : (3 + i) * KP]
            basis_cols = slice(loads + j * KP, loads + (j + 1) * KP)
            smooth_cols = slice(loads + (2 + j) * KP, loads + (3 + j) * KP)
            terms[3, :, at : at + KP] = basis_rows[:, basis_cols]
            terms[3, :, at + KP : at + 2 * KP] = basis_rows[:, smooth_cols]
            terms[3, :, at + 2 * KP : at + 3 * KP] = smooth_rows[:, smooth_cols]
            last = shared[:, j * KP : (j + 1) * KP] if i == 0 else jnp.zeros((KP, KP), F32)
            terms[3, :, at + 3 * KP : at + 4 * KP] = last
    keep[...] = jnp.where(here.odd, terms[2:], terms[:2])
    image_a[rows:, :] = jnp.zeros((KP, face), F32)
    for kind in range(2):
        image_a[rows:, kind * 2 * loads : (kind + 1) * 2 * loads] = jnp.where(
            here.odd, terms[kind], terms[2 + kind]
        )


def coarse_solves(clusters, members, loads, odd, terms, other_terms, inverse):
    def pick_kind(kind, mine, theirs):
        return jnp.where(odd, theirs, mine) if kind < 2 else jnp.where(odd, mine, theirs)

    def rows_of(kind):
        return slice(kind % 2 * KP, kind % 2 * KP + KP)

    def total(c, kind):
        pairs = members // 2
        found = [ref[c * pairs, rows_of(kind)] for ref in (terms, other_terms)]
        for m in range(1, pairs):
            found = [
                v + ref[c * pairs + m, rows_of(kind)]
                for v, ref in zip(found, (terms, other_terms))
            ]
        return pick_kind(kind, *found)

    def one(pair, kind):
        return pick_kind(kind, terms[pair, rows_of(kind)], other_terms[pair, rows_of(kind)])

    def begin(c, kind):
        return one(c * members // 2, kind)

    def end(c, kind):
        return one((c + 1) * members // 2 - 1, kind)

    span = 4 * KP
    lanes = terms.shape[-1]
    totals = [total(c, 0) for c in range(clusters)]
    load_side = [v[:, :loads] for v in totals]
    smooth_side = [v[:, loads:] for v in totals]

    def images(kind):
        found = []
        for c in range(clusters):
            value = total(c, kind)[:, :loads]
            if c + 1 < clusters:
                value = value + begin(c + 1, kind)[:, loads:]
            if c > 0:
                value = value + end(c - 1, kind)[:, loads:]
            found.append(value)
        return found

    centre, below, above = [], [], []
    for c in range(clusters):
        value, under, over = total(c, 3), begin(c, 3), end(c, 3)
        if c + 1 < clusters:
            value = value + pltpu.roll(begin(c + 1, 3), lanes - 3 * span, 1)
            over = over + pltpu.roll(begin(c + 1, 3), lanes - span, 1)
        if c > 0:
            value = value + pltpu.roll(end(c - 1, 3), lanes - 3 * span, 1)
            under = under + pltpu.roll(end(c - 1, 3), lanes - span, 1)
        centre.append(value)
        below.append(under)
        above.append(over)

    def block_times(block, amounts):
        value = block[:, 0:1] * amounts[0:1]
        for k in range(1, KP):
            value = value + block[:, k : k + 1] * amounts[k : k + 1]
        return value

    def times(kind, amounts):
        found = []
        for c in range(clusters):
            near, far = slice(kind * KP, (kind + 1) * KP), slice(span + kind * KP, span + (kind + 1) * KP)
            value = block_times(centre[c][:, near], amounts[c])
            if c > 0:
                value = value + block_times(below[c][:, far], amounts[c - 1])
            if c + 1 < clusters:
                value = value + block_times(above[c][:, far], amounts[c + 1])
            found.append(value)
        return found

    turned_centre = [v.T for v in centre]
    turned_below = [v.T for v in below]
    turned_above = [v.T for v in above]

    def turned_times(kind, amounts):
        found = []
        near, far = slice(kind * KP, (kind + 1) * KP), slice(span + kind * KP, span + (kind + 1) * KP)
        for c in range(clusters):
            value = block_times(turned_centre[c][near], amounts[c])
            if c > 0:
                value = value + block_times(turned_above[c - 1][far], amounts[c - 1])
            if c + 1 < clusters:
                value = value + block_times(turned_below[c + 1][far], amounts[c + 1])
            found.append(value)
        return found

    modes = inverse.shape[0] // clusters
    row = lax.broadcasted_iota(jnp.int32, (clusters * KP, clusters * modes), 0)
    col = lax.broadcasted_iota(jnp.int32, (clusters * KP, clusters * modes), 1)
    mode = row % KP
    spread = jnp.where((mode < modes) & (col == row // KP * modes + mode), 1.0, 0.0)
    padded = jnp.dot(spread, inverse[...], precision=EXACT, preferred_element_type=F32)
    padded = lax.dot_general(
        padded, spread, (((1,), (1,)), ((), ())), precision=EXACT, preferred_element_type=F32
    )

    def solve(parts):
        value = jnp.dot(
            padded, jnp.concatenate(parts, axis=0), precision=EXACT, preferred_element_type=F32
        )
        return [value[c * KP : (c + 1) * KP] for c in range(clusters)]

    def less(left, *others):
        found = list(left)
        for other in others:
            found = [p - q for p, q in zip(found, other)]
        return found

    load_amounts = solve(load_side)
    smooth_amounts = solve(less(smooth_side, times(3, load_amounts)))
    image_amounts = solve(less(images(1), times(1, load_amounts), times(0, smooth_amounts)))
    image_side = less(images(2), times(2, load_amounts), turned_times(1, smooth_amounts))
    smooth_image_amounts = solve(less(image_side, times(3, image_amounts)))
    return load_amounts, smooth_amounts, image_amounts, smooth_image_amounts


def second_kernel(
    extent,
    softness, terms, other_terms, inverse, residual, smooth, coarse, pairs_a, pairs_b,
    image_a, image_b, got_a, got_b,
    pick, operator, place,
    search, applied, change, next_a, next_b, scalars,
    amounts, first, second, third,
):
    loads, slots = residual.shape
    face = slots // 2
    half, _, size = pairs_a.shape
    clusters, members = extent
    here = chain(*extent)

    def weighted(left, right):
        product = left * right
        near = jnp.sum(product[:, :face], axis=1, keepdims=True)
        far = jnp.sum(product[:, face:], axis=1, keepdims=True)
        return here.weights[0] * near + here.weights[1] * far

    solved = coarse_solves(clusters, members, loads, here.odd, terms, other_terms, inverse)
    for kind, parts in enumerate(solved):
        for c, part in enumerate(parts):
            amounts[kind, c] = part

    def local(kind, reached):
        return [amounts[kind, c] for c in reached]

    none = [jnp.zeros((2 * KP, loads), F32)]
    own = jnp.concatenate(local(1, here.own) + local(0, here.own), axis=0)
    image_own = jnp.concatenate(local(3, here.own) + local(2, here.own), axis=0)
    own_basis = jnp.concatenate(local(0, here.own) + none, axis=0)
    image_own_basis = jnp.concatenate(local(2, here.own) + none, axis=0)
    projected = residual[...] - dot_modes(own_basis, coarse[...])
    direction = smooth[...] - dot_modes(own, coarse[...])
    search[...] = direction
    for side, image, got in ((0, image_a, got_a), (1, image_b, got_b)):
        theirs = local(1, here.near[side]) + local(0, here.near[side])
        mixed = jnp.concatenate([own] + theirs, axis=0)
        rows = slice(loads, loads + 4 * KP)
        rows = three_rows(jnp.concatenate([image[rows, :], got[rows, :]], axis=0))
        applied[:, side * face : (side + 1) * face] = (
            image[:loads, :] + got[:loads, :] - dot_modes(mixed, rows)
        )
    image_projected = applied[...] - dot_modes(image_own_basis, coarse[...])
    for side, pairs in ((0, pairs_a), (1, pairs_b)):
        for k in range(half):
            cols = slice(side * face + k * size, side * face + (k + 1) * size)
            change[:, cols] = smooth_block(applied[:, cols], here.weights[side], pairs[k])
    changed = change[...] - dot_modes(image_own, coarse[...])
    change[...] = changed
    high, low = two_parts(changed)
    first[:loads, :] = high
    first[loads:, :] = low
    found = [
        weighted(projected, direction),
        weighted(direction, applied[...]),
        weighted(projected, changed) + weighted(image_projected, direction),
        weighted(image_projected, changed),
    ]

    @pl.loop(0, slots // TILE)
    def _(tile):
        cols = pl.ds(pl.multiple_of(tile * TILE, TILE), TILE)
        second[:, cols] = dot(first[...], pick[:, cols]).astype(BF16)

    apply_rest(loads, softness[...], operator, place, second, third, next_a, next_b)

    for vector in (search, change):
        column = jnp.sum(vector[:, :face] * next_a[...], axis=1, keepdims=True)
        column = column + jnp.sum(vector[:, face:] * next_b[...], axis=1, keepdims=True)
        found.append(column)
    lane = lax.broadcasted_iota(jnp.int32, (loads, 128), 1)
    value = jnp.zeros(lane.shape, F32)
    for k, column in enumerate(found):
        value = jnp.where(lane == k, column, value)
    turned = value.T
    scalars[:, :loads] = turned[:4, :]
    scalars[:, loads:] = turned[4:8, :]


def last_kernel(
    extent, scalars, residual, search, applied, change, next_a, next_b, got_a, got_b, out_m, out_r
):
    loads, slots = residual.shape
    face = slots // 2
    total = jnp.sum(scalars[...], axis=0)
    total = jnp.concatenate([total[:, :loads], total[:, loads:]], axis=0)
    rho = total[0:1]
    gamma = total[1:2]
    alpha = rho / gamma
    rho_next = rho - alpha * total[2:3] + alpha * alpha * total[3:4]
    grow = 1.0 + rho_next / rho
    energy = grow * grow * gamma - 2.0 * grow * alpha * total[4:5] + alpha * alpha * total[5:6]
    alpha_next = rho_next / energy
    lengths = jnp.concatenate(
        [alpha + alpha_next * grow, alpha_next * alpha, jnp.zeros((6, rho.shape[1]), F32)], axis=0
    )
    turned = jnp.concatenate([lengths, jnp.zeros((120, rho.shape[1]), F32)], axis=0).T
    along, against = turned[:loads, 0:1], turned[:loads, 1:2]
    sides = []
    for side, own, got in ((0, next_a, got_a), (1, next_b, got_b)):
        cols = slice(side * face, (side + 1) * face)
        sides.append(
            (
                along * search[:, cols] - against * change[:, cols],
                residual[:, cols] - along * applied[:, cols] + against * (own[...] + got[...]),
            )
        )
    odd = chain(*extent).odd
    for k, out in ((0, out_m), (1, out_r)):
        out[:, 0, :] = jnp.where(odd, sides[0][k], sides[1][k])
        out[:, 1, :] = jnp.where(odd, sides[1][k], sides[0][k])


VMEM = pl.BlockSpec(memory_space=pltpu.VMEM)
HBM = pl.BlockSpec(memory_space=pltpu.HBM)


def shaped(shape, dtype=F32):
    return jax.ShapeDtypeStruct(shape, dtype)


def in_hbm(value):
    return pltpu.with_memory_space_constraint(value, pltpu.HBM)


def per_device(
    dual_load, dual_operator, index_map, stiffness, coarse_basis, dirichlet_blocks, coarse_inverse
):
    loads, _, face = dual_load.shape[2:]
    slots = 2 * face
    modes = coarse_basis.shape[2]
    block_count, size, _ = dirichlet_blocks.shape[2:]
    clusters, members = lax.axis_size("cluster"), lax.axis_size("member")
    devices = clusters * members
    extent = clusters, members
    load = dual_load.reshape(loads, 2, face)
    basis = coarse_basis.reshape(modes, 1, slots)
    blocks = dirichlet_blocks.reshape(block_count, size, size)

    evens = [(i, i + 1) for i in range(0, devices - 1, 2)]
    odds = [(i, i + 1) for i in range(1, devices - 1, 2)]
    evens = evens + [(j, i) for i, j in evens]
    odds = odds + [(j, i) for i, j in odds]

    def swap(side_a, side_b):
        from_b = lax.ppermute(side_b, AXES, odds)
        from_a = lax.ppermute(side_a, AXES, evens)
        return from_a, from_b

    def share(copies, groups=None):
        return lax.all_to_all(copies, AXES, 0, 0, axis_index_groups=groups, tiled=True)

    def params(mebibytes):
        return pltpu.CompilerParams(vmem_limit_bytes=mebibytes * 1024 * 1024)

    half_vector = shaped((loads, face))
    vector = shaped((loads, slots))
    half = block_count // 2
    packed = shaped((size // 2 + KP + loads, face))
    side_blocks = shaped((half, size, size), BF16)
    pay_a, pay_b, mine_a, mine_b = pl.pallas_call(
        functools.partial(pack_kernel, extent),
        out_shape=(packed, packed, side_blocks, side_blocks),
        in_specs=[HBM] * 3,
        out_specs=(VMEM,) * 4,
        scratch_shapes=[
            pltpu.VMEM(load.shape, F32),
            pltpu.VMEM(basis.shape, F32),
            pltpu.VMEM(blocks.shape, BF16),
            pltpu.SemaphoreType.DMA((3,)),
        ],
        compiler_params=params(8),
    )(*[in_hbm(v) for v in (load, basis, blocks)])
    got_a, got_b = swap(pay_a, pay_b)

    ordering = shaped((slots, slots), BF16)
    pick, place, operator, softness = pl.pallas_call(
        functools.partial(order_kernel, extent),
        out_shape=(ordering, ordering, ordering, shaped((1, 1))),
        in_specs=[HBM, VMEM, HBM],
        out_specs=(VMEM,) * 4,
        scratch_shapes=[pltpu.VMEM((1, slots), jnp.int32), pltpu.SemaphoreType.DMA((2,))],
        compiler_params=params(8),
    )(in_hbm(index_map.reshape(1, slots)), stiffness, in_hbm(dual_operator))
    pick, operator, place = [
        pltpu.with_memory_space_constraint(v, pltpu.VMEM) for v in (pick, operator, place)
    ]

    rows = loads + 4 * KP
    side_pairs = shaped((half, 2 * size, size), BF16)
    residual_a, smooth_a, coarse_a, own_basis_a, pairs_a, first_a, second_a = pl.pallas_call(
        functools.partial(near_kernel, extent, modes),
        out_shape=(
            half_vector,
            half_vector,
            shaped((12 * KP, face), BF16),
            shaped((2 * KP, face), BF16),
            side_pairs,
            shaped((2 * rows, face), BF16),
            shaped((2 * rows, slots), BF16),
        ),
        in_specs=[VMEM] * 4,
        out_specs=(VMEM,) * 7,
        compiler_params=params(8),
    )(pay_a, got_a, mine_a, pick)
    residual, smooth, coarse, pairs_b, image_a, image_b, keep = pl.pallas_call(
        functools.partial(first_kernel, extent, modes),
        out_shape=(
            vector,
            vector,
            shaped((12 * KP, slots), BF16),
            side_pairs,
            shaped((rows + KP, face)),
            shaped((rows, face)),
            shaped((2, KP, 2 * loads)),
        ),
        in_specs=[VMEM] * 13,
        out_specs=(VMEM,) * 7,
        scratch_shapes=[pltpu.VMEM((2 * KP, slots), BF16)]
        + [pltpu.VMEM((2 * rows, slots), BF16)] * 3
        + [pltpu.VMEM((4, KP, 2 * loads), F32)],
        compiler_params=params(12),
    )(
        softness, pay_b, got_b, mine_b, residual_a, smooth_a, coarse_a, own_basis_a, first_a,
        second_a, pick, operator, place,
    )

    got_a, got_b = swap(image_a, image_b)
    terms = pl.pallas_call(
        merge_kernel,
        out_shape=shaped((devices // 2, 2 * KP, 2 * loads)),
        in_specs=[VMEM] * 2,
        out_specs=VMEM,
        compiler_params=params(8),
    )(keep, got_a)
    terms = share(terms, [list(range(k, devices, 2)) for k in range(2)])
    other_terms = lax.ppermute(terms, AXES, evens)

    search, applied, change, next_a, next_b, scalars = pl.pallas_call(
        functools.partial(second_kernel, extent),
        out_shape=(vector, vector, vector, half_vector, half_vector, shaped((4, 2 * loads))),
        in_specs=[VMEM] * 16,
        out_specs=(VMEM,) * 6,
        scratch_shapes=[pltpu.VMEM((4, clusters, KP, loads), F32)]
        + [pltpu.VMEM((2 * loads, slots), BF16)] * 3,
        compiler_params=params(12),
    )(
        softness, terms, other_terms, coarse_inverse, residual, smooth, coarse, pairs_a, pairs_b,
        image_a, image_b, got_a, got_b, pick, operator, place,
    )

    got_a, got_b = swap(next_a, next_b)
    scalars = share(jnp.broadcast_to(scalars[None], (devices,) + scalars.shape))

    out_m, out_r = pl.pallas_call(
        functools.partial(last_kernel, extent),
        out_shape=(shaped((loads, 2, face)), shaped((loads, 2, face))),
        in_specs=[VMEM] * 9,
        out_specs=(VMEM, VMEM),
        compiler_params=params(12),
    )(scalars, residual, search, applied, change, next_a, next_b, got_a, got_b)
    return out_m.reshape(dual_load.shape), out_r.reshape(dual_load.shape)


def solution(mesh):
    in_specs = (
        P("cluster", "member", None, None, None),
        P(),
        P("cluster", "member", None),
        P("cluster", "member"),
        P("cluster", "member", None, None),
        P("cluster", "member", None, None, None),
        P(),
    )
    out_specs = (P("cluster", "member", None, None, None), P("cluster", "member", None, None, None))
    return jax.shard_map(
        per_device, mesh=mesh, in_specs=in_specs, out_specs=out_specs, check_vma=False
    )
```

```python
import functools
from typing import NamedTuple

import jax
import jax.numpy as jnp
from jax import lax
from jax.experimental import pallas as pl
from jax.experimental.pallas import tpu as pltpu
from jax.sharding import PartitionSpec as P

AXES = ("cluster", "member")
F32 = jnp.float32
BF16 = jnp.bfloat16
EXACT = lax.Precision.HIGHEST
SLICE = 4
KP = 8
TILE = 1024


def dot(left, right):
    return jnp.dot(left, right, preferred_element_type=F32)


def dot_rows(left, right):
    return lax.dot_general(left, right, (((1,), (1,)), ((), ())), preferred_element_type=F32)


def two_parts(value):
    high = value.astype(BF16)
    return high, (value - high.astype(F32)).astype(BF16)


def stacked(value):
    return jnp.concatenate(two_parts(value), axis=0)


def folded(value, rows, cols):
    value = value[:rows] + value[rows:]
    return value[:, :cols] + value[:, cols:]


def three_rows(value):
    high, low = two_parts(value)
    return jnp.concatenate([high, low, high], axis=0)


def dot_modes(amounts, rows):
    high, low = two_parts(amounts)
    left = jnp.concatenate([high, high, low], axis=0)
    return lax.dot_general(left, rows, (((0,), (0,)), ((), ())), preferred_element_type=F32)


class Chain(NamedTuple):
    odd: jax.Array
    own: tuple
    near: tuple
    weights: tuple
    same: tuple


def chain(clusters, members):
    count = clusters * members
    position = lax.axis_index("cluster") * members + lax.axis_index("member")
    parity = lax.rem(position, 2)

    def reach(pos):
        cluster, member = lax.div(pos, members), lax.rem(pos, members)
        other = cluster + jnp.where(member == members - 1, 1, jnp.where(member == 0, -1, 0))
        return cluster, jnp.clip(other, 0, clusters - 1)

    own = reach(position)
    near, weights, same = [], [], []
    for partner in (position + 1 - 2 * parity, position - 1 + 2 * parity):
        real = (partner >= 0) & (partner < count)
        there = reach(jnp.clip(partner, 0, count - 1))
        near.append(there)
        weights.append(jnp.where(real, 0.5, 1.0))
        same.append(jnp.where(real & (there[0] == own[0]), 1.0, 0.0))
    return Chain(parity == 1, own, tuple(near), tuple(weights), tuple(same))


def pack_side(first, load, basis, blocks, out, mine):
    loads, _, face = load.shape
    modes = basis.shape[0]
    half = blocks.shape[0] // 2
    size = blocks.shape[1]
    row = lax.broadcasted_iota(jnp.int32, (size, size), 0)
    col = lax.broadcasted_iota(jnp.int32, (size, size), 1)
    mid = size // 2
    low = mid + KP
    out[mid:low, :] = jnp.zeros((KP, face), F32)
    for k in range(modes):
        mode = basis[k]
        out[mid + k : mid + k + 1, :] = jnp.where(first, mode[:, :face], mode[:, face:])
    base = jnp.where(first, 0, half)
    for pair in range(half // 2):
        one, two = blocks[base + 2 * pair], blocks[base + 2 * pair + 1]
        mine[2 * pair] = one
        mine[2 * pair + 1] = two
        upper, lower = one.astype(F32), two.astype(F32)
        both = jnp.where(row <= col, upper, lower)
        left = pair * size
        right = (half // 2 + pair) * size
        out[:mid, left : left + size] = both[:mid]
        out[:mid, right : right + size] = both[mid:]
        diagonal = jnp.sum(jnp.where(row == col, lower, 0.0), axis=0, keepdims=True)
        out[mid + modes : mid + modes + 1, left : left + size] = diagonal
    out[low:, :] = jnp.where(first, load[:, 0, :], load[:, 1, :])


def pack_kernel(
    extent,
    far_load, far_basis, far_blocks,
    out_a, out_b, mine_a, mine_b,
    load, basis, blocks, arrived,
):
    copies = [
        pltpu.make_async_copy(source, target, arrived.at[k])
        for k, (source, target) in enumerate(
            ((far_blocks, blocks), (far_load, load), (far_basis, basis))
        )
    ]
    for copy in copies:
        copy.start()
    for copy in copies:
        copy.wait()
    odd = chain(*extent).odd
    pack_side(jnp.logical_not(odd), load, basis, blocks, out_b, mine_b)
    pack_side(odd, load, basis, blocks, out_a, mine_a)


def order_kernel(
    extent,
    far_index, stiffness, far_operator,
    pick, place, operator, softness,
    index, arrived,
):
    copies = [
        pltpu.make_async_copy(far_index, index, arrived.at[0]),
        pltpu.make_async_copy(far_operator, operator, arrived.at[1]),
    ]
    for copy in copies:
        copy.start()
    slots = pick.shape[0]
    face = slots // 2
    rows = 128
    odd = chain(*extent).odd
    softness[...] = 1.0 / stiffness[...]
    copies[0].wait()
    lane = lax.broadcasted_iota(jnp.int32, (rows, slots), 1).astype(jnp.int16)
    depth = lax.broadcasted_iota(jnp.int32, (rows, slots), 0).astype(jnp.int16)
    one, zero = jnp.ones((), BF16), jnp.zeros((), BF16)
    index_0, index_1 = index[:, :face], index[:, face:]
    wanted = jnp.concatenate(
        [jnp.where(odd, index_0, index_1), jnp.where(odd, index_1, index_0)], axis=1
    )
    every = jnp.broadcast_to(wanted, (rows, slots)).astype(jnp.int16)
    for start in range(0, slots, rows):
        here = jnp.broadcast_to(wanted[:, start : start + rows].astype(F32), (rows, rows)).T
        here = here.astype(jnp.int32).astype(jnp.int16)
        target = jnp.concatenate([here] * (slots // rows), axis=1)
        pick[start : start + rows, :] = jnp.where(target == lane, one, zero)
        place[start : start + rows, :] = jnp.where(every - jnp.int16(start) == depth, one, zero)
    copies[1].wait()


def merge_kernel(keep, got, out):
    kinds, depth, lanes = keep.shape
    rows = got.shape[0] - depth
    modes = out.shape[1] * SLICE // kinds
    values = [keep[k] + got[rows:, k * lanes : (k + 1) * lanes] for k in range(kinds)]
    value = jnp.concatenate([v[:modes] for v in values], axis=0)
    for part in range(out.shape[1]):
        piece = value[part * SLICE : (part + 1) * SLICE]
        out[:, part] = jnp.broadcast_to(piece[None], (out.shape[0],) + piece.shape)


def fold_kernel(clusters, members, terms, out):
    for c in range(clusters):
        for parity in range(2):
            for part in range(terms.shape[1]):
                begin = terms[c * members + parity, part]
                end = terms[(c + 1) * members - 2 + parity, part]
                value = begin
                for m in range(2, members, 2):
                    value = value + terms[c * members + m + parity, part]
                for k, result in enumerate((value, begin, end)):
                    out[(c * 2 + parity) * 3 + k, part * SLICE : (part + 1) * SLICE] = result


def apply_rest(rows, scale, operator, place, second, third, image_a, image_b):
    slots = second.shape[1]
    face = slots // 2

    @pl.loop(0, slots // TILE)
    def _(tile):
        cols = pl.ds(pl.multiple_of(tile * TILE, TILE), TILE)
        product = dot(second[...], operator[:, cols])
        high, low = two_parts(product[:rows] + product[rows:])
        third[:rows, cols] = high
        third[rows:, cols] = low

    for side, image in ((0, image_a), (1, image_b)):
        product = dot(third[...], place[:, side * face : (side + 1) * face])
        image[:rows, :] = scale * (product[:rows] + product[rows:])


def smooth_block(value, weight, block_pair):
    rows = value.shape[0]
    high, low = two_parts(weight * value)
    left = jnp.concatenate(
        [jnp.concatenate([high, high], axis=1), jnp.concatenate([low, low], axis=1)], axis=0
    )
    product = dot(left, block_pair)
    return weight * (product[:rows] + product[rows:])


def side_part(
    modes, at, weight, same, pay, got, blocks, residual, smooth, coarse, own_basis, pairs, first
):
    half, size, _ = blocks.shape
    face = half * size
    loads = pay.shape[0] - size // 2 - KP
    rows = loads + 4 * KP
    mid = size // 2
    low = mid + KP
    cols = slice(at, at + face)
    row = lax.broadcasted_iota(jnp.int32, (size, size), 0)
    col = lax.broadcasted_iota(jnp.int32, (size, size), 1)
    real = lax.broadcasted_iota(jnp.int32, (KP, face), 0) < modes
    mine = jnp.where(real, pay[mid:low, :], 0.0)
    theirs = jnp.where(real, got[mid:low, :], 0.0)
    own_basis[:, cols] = stacked(mine)
    span = jnp.concatenate([mine + same * theirs, (1.0 - same) * theirs], axis=0)
    for pair in range(half // 2):
        left = pair * size
        right = (half // 2 + pair) * size
        both = jnp.concatenate(
            [got[:mid, left : left + size], got[:mid, right : right + size]], axis=0
        )
        turned = both.T
        diagonal = got[mid + modes : mid + modes + 1, left : left + size]
        upper = jnp.where(row <= col, both, turned)
        lower = jnp.where(row > col, both, jnp.where(row < col, turned, diagonal))
        for k, theirs_block in ((2 * pair, upper), (2 * pair + 1, lower)):
            block_pair = jnp.concatenate([blocks[k], theirs_block.astype(BF16)], axis=0)
            pairs[k] = block_pair
            there = slice(k * size, (k + 1) * size)
            cols = slice(at + k * size, at + (k + 1) * size)
            value = pay[low:, there] + got[low:, there]
            modes_here = span[:, there]
            result = smooth_block(
                jnp.concatenate([value, modes_here], axis=0), weight, block_pair
            )
            residual[:, cols] = value
            smooth[:, cols] = result[:loads]
            high, low_part = two_parts(
                jnp.concatenate([result[:loads], modes_here, result[loads:]], axis=0)
            )
            first[:rows, cols] = high
            first[rows:, cols] = low_part
            coarse[: 4 * KP, cols] = high[loads:]
            coarse[4 * KP : 8 * KP, cols] = low_part[loads:]
            coarse[8 * KP :, cols] = high[loads:]


def near_kernel(
    extent, modes,
    pay, got, blocks, pick,
    residual, smooth, coarse, own_basis, pairs, first, second,
):
    here = chain(*extent)
    side_part(
        modes, 0, here.weights[0], here.same[0], pay, got, blocks,
        residual, smooth, coarse, own_basis, pairs, first,
    )
    slots = second.shape[1]
    face = first.shape[1]

    @pl.loop(0, slots // TILE)
    def _(tile):
        cols = pl.ds(pl.multiple_of(tile * TILE, TILE), TILE)
        second[:, cols] = dot(first[...], pick[:face, cols]).astype(BF16)


def first_kernel(
    extent, modes,
    softness, pay, got, blocks,
    residual_a, smooth_a, coarse_a, own_basis_a, first_a, second_a,
    pick, operator, place,
    residual, smooth, coarse, pairs, image_a, image_b, keep,
    own_basis, first, second, third, terms,
):
    loads, slots = residual.shape
    face = slots // 2
    rows = loads + 4 * KP
    here = chain(*extent)
    side_part(
        modes, face, here.weights[1], here.same[1], pay, got, blocks,
        residual, smooth, coarse, own_basis, pairs, first,
    )

    @pl.loop(0, slots // TILE)
    def _(tile):
        cols = pl.ds(pl.multiple_of(tile * TILE, TILE), TILE)
        product = dot(first[:, face:], pick[face:, cols]) + second_a[:, cols].astype(F32)
        second[:, cols] = product.astype(BF16)

    for whole, part in (
        (residual, residual_a), (smooth, smooth_a), (coarse, coarse_a),
        (own_basis, own_basis_a), (first, first_a),
    ):
        whole[:, :face] = part[...]
    apply_rest(rows, softness[...], operator, place, second, third, image_a, image_b)

    vectors = jnp.concatenate([stacked(residual[...]), first[...]], axis=0)
    sides = dot_rows(own_basis[...], vectors)
    load_side = folded(sides[:, : 2 * loads], KP, loads)
    smooth_side = folded(sides[:, 2 * loads :], KP, rows)
    shared = smooth_side[:, loads + 2 * KP :]
    energy = jnp.zeros((8 * KP, 2 * rows), F32)
    for side, image in ((0, image_a), (1, image_b)):
        cols = slice(side * face, (side + 1) * face)
        energy = energy + dot_rows(coarse[: 8 * KP, cols], stacked(image[:rows, :]))
    energy = folded(energy, 4 * KP, rows)
    terms[0, :, :loads] = load_side
    terms[0, :, loads:] = smooth_side[:, :loads]
    terms[1, :, :loads] = energy[:KP, :loads]
    terms[1, :, loads:] = energy[KP : 2 * KP, :loads]
    terms[2, :, :loads] = energy[2 * KP : 3 * KP, :loads]
    terms[2, :, loads:] = energy[3 * KP :, :loads]
    for i in range(2):
        for j in range(2):
            at = (2 * i + j) * 4 * KP
            basis_rows = energy[i * KP : (i + 1) * KP]
            smooth_rows = energy[(2 + i) * KP : (3 + i) * KP]
            basis_cols = slice(loads + j * KP, loads + (j + 1) * KP)
            smooth_cols = slice(loads + (2 + j) * KP, loads + (3 + j) * KP)
            terms[3, :, at : at + KP] = basis_rows[:, basis_cols]
            terms[3, :, at + KP : at + 2 * KP] = basis_rows[:, smooth_cols]
            terms[3, :, at + 2 * KP : at + 3 * KP] = smooth_rows[:, smooth_cols]
            last = shared[:, j * KP : (j + 1) * KP] if i == 0 else jnp.zeros((KP, KP), F32)
            terms[3, :, at + 3 * KP : at + 4 * KP] = last
    keep[...] = jnp.where(here.odd, terms[2:], terms[:2])
    image_a[rows:, :] = jnp.zeros((KP, face), F32)
    for kind in range(2):
        image_a[rows:, kind * 2 * loads : (kind + 1) * 2 * loads] = jnp.where(
            here.odd, terms[kind], terms[2 + kind]
        )


def coarse_solves(clusters, loads, terms, inverse):
    modes = inverse.shape[0] // clusters

    def one_kind(c, kind, which):
        value = terms[(c * 2 + kind // 2) * 3 + which]
        value = value[kind % 2 * modes : (kind % 2 + 1) * modes]
        return jnp.concatenate([value, jnp.zeros((KP - modes, value.shape[1]), F32)], axis=0)

    def total(c, kind):
        return one_kind(c, kind, 0)

    def begin(c, kind):
        return one_kind(c, kind, 1)

    def end(c, kind):
        return one_kind(c, kind, 2)

    span = 4 * KP
    lanes = terms.shape[-1]
    totals = [total(c, 0) for c in range(clusters)]
    load_side = [v[:, :loads] for v in totals]
    smooth_side = [v[:, loads:] for v in totals]

    def images(kind):
        found = []
        for c in range(clusters):
            value = total(c, kind)[:, :loads]
            if c + 1 < clusters:
                value = value + begin(c + 1, kind)[:, loads:]
            if c > 0:
                value = value + end(c - 1, kind)[:, loads:]
            found.append(value)
        return found

    centre, below, above = [], [], []
    for c in range(clusters):
        value, under, over = total(c, 3), begin(c, 3), end(c, 3)
        if c + 1 < clusters:
            value = value + pltpu.roll(begin(c + 1, 3), lanes - 3 * span, 1)
            over = over + pltpu.roll(begin(c + 1, 3), lanes - span, 1)
        if c > 0:
            value = value + pltpu.roll(end(c - 1, 3), lanes - 3 * span, 1)
            under = under + pltpu.roll(end(c - 1, 3), lanes - span, 1)
        centre.append(value)
        below.append(under)
        above.append(over)

    def block_times(block, amounts):
        value = block[:, 0:1] * amounts[0:1]
        for k in range(1, KP):
            value = value + block[:, k : k + 1] * amounts[k : k + 1]
        return value

    def times(kind, amounts):
        found = []
        for c in range(clusters):
            near, far = slice(kind * KP, (kind + 1) * KP), slice(span + kind * KP, span + (kind + 1) * KP)
            value = block_times(centre[c][:, near], amounts[c])
            if c > 0:
                value = value + block_times(below[c][:, far], amounts[c - 1])
            if c + 1 < clusters:
                value = value + block_times(above[c][:, far], amounts[c + 1])
            found.append(value)
        return found

    turned_centre = [v.T for v in centre]
    turned_below = [v.T for v in below]
    turned_above = [v.T for v in above]

    def turned_times(kind, amounts):
        found = []
        near, far = slice(kind * KP, (kind + 1) * KP), slice(span + kind * KP, span + (kind + 1) * KP)
        for c in range(clusters):
            value = block_times(turned_centre[c][near], amounts[c])
            if c > 0:
                value = value + block_times(turned_above[c - 1][far], amounts[c - 1])
            if c + 1 < clusters:
                value = value + block_times(turned_below[c + 1][far], amounts[c + 1])
            found.append(value)
        return found

    row = lax.broadcasted_iota(jnp.int32, (clusters * KP, clusters * modes), 0)
    col = lax.broadcasted_iota(jnp.int32, (clusters * KP, clusters * modes), 1)
    mode = row % KP
    spread = jnp.where((mode < modes) & (col == row // KP * modes + mode), 1.0, 0.0)
    padded = jnp.dot(spread, inverse[...], precision=EXACT, preferred_element_type=F32)
    padded = lax.dot_general(
        padded, spread, (((1,), (1,)), ((), ())), precision=EXACT, preferred_element_type=F32
    )

    def solve(parts):
        value = jnp.dot(
            padded, jnp.concatenate(parts, axis=0), precision=EXACT, preferred_element_type=F32
        )
        return [value[c * KP : (c + 1) * KP] for c in range(clusters)]

    def less(left, *others):
        found = list(left)
        for other in others:
            found = [p - q for p, q in zip(found, other)]
        return found

    load_amounts = solve(load_side)
    smooth_amounts = solve(less(smooth_side, times(3, load_amounts)))
    image_amounts = solve(less(images(1), times(1, load_amounts), times(0, smooth_amounts)))
    image_side = less(images(2), times(2, load_amounts), turned_times(1, smooth_amounts))
    smooth_image_amounts = solve(less(image_side, times(3, image_amounts)))
    return load_amounts, smooth_amounts, image_amounts, smooth_image_amounts


def second_kernel(
    extent,
    softness, terms, inverse, residual, smooth, coarse, pairs_a, pairs_b,
    image_a, image_b, got_a, got_b,
    pick, operator, place,
    search, applied, change, next_a, next_b, scalars,
    amounts, first, second, third,
):
    loads, slots = residual.shape
    face = slots // 2
    half, _, size = pairs_a.shape
    clusters, _ = extent
    here = chain(*extent)

    def weighted(left, right):
        product = left * right
        near = jnp.sum(product[:, :face], axis=1, keepdims=True)
        far = jnp.sum(product[:, face:], axis=1, keepdims=True)
        return here.weights[0] * near + here.weights[1] * far

    solved = coarse_solves(clusters, loads, terms, inverse)
    for kind, parts in enumerate(solved):
        for c, part in enumerate(parts):
            amounts[kind, c] = part

    def local(kind, reached):
        return [amounts[kind, c] for c in reached]

    none = [jnp.zeros((2 * KP, loads), F32)]
    own = jnp.concatenate(local(1, here.own) + local(0, here.own), axis=0)
    image_own = jnp.concatenate(local(3, here.own) + local(2, here.own), axis=0)
    own_basis = jnp.concatenate(local(0, here.own) + none, axis=0)
    image_own_basis = jnp.concatenate(local(2, here.own) + none, axis=0)
    projected = residual[...] - dot_modes(own_basis, coarse[...])
    direction = smooth[...] - dot_modes(own, coarse[...])
    search[...] = direction
    for side, image, got in ((0, image_a, got_a), (1, image_b, got_b)):
        theirs = local(1, here.near[side]) + local(0, here.near[side])
        mixed = jnp.concatenate([own] + theirs, axis=0)
        rows = slice(loads, loads + 4 * KP)
        rows = three_rows(jnp.concatenate([image[rows, :], got[rows, :]], axis=0))
        applied[:, side * face : (side + 1) * face] = (
            image[:loads, :] + got[:loads, :] - dot_modes(mixed, rows)
        )
    image_projected = applied[...] - dot_modes(image_own_basis, coarse[...])
    for side, pairs in ((0, pairs_a), (1, pairs_b)):
        for k in range(half):
            cols = slice(side * face + k * size, side * face + (k + 1) * size)
            change[:, cols] = smooth_block(applied[:, cols], here.weights[side], pairs[k])
    changed = change[...] - dot_modes(image_own, coarse[...])
    change[...] = changed
    high, low = two_parts(changed)
    first[:loads, :] = high
    first[loads:, :] = low
    found = [
        weighted(projected, direction),
        weighted(direction, applied[...]),
        weighted(projected, changed) + weighted(image_projected, direction),
        weighted(image_projected, changed),
    ]

    @pl.loop(0, slots // TILE)
    def _(tile):
        cols = pl.ds(pl.multiple_of(tile * TILE, TILE), TILE)
        second[:, cols] = dot(first[...], pick[:, cols]).astype(BF16)

    apply_rest(loads, softness[...], operator, place, second, third, next_a, next_b)

    for vector in (search, change):
        column = jnp.sum(vector[:, :face] * next_a[...], axis=1, keepdims=True)
        column = column + jnp.sum(vector[:, face:] * next_b[...], axis=1, keepdims=True)
        found.append(column)
    lane = lax.broadcasted_iota(jnp.int32, (loads, 128), 1)
    value = jnp.zeros(lane.shape, F32)
    for k, column in enumerate(found):
        value = jnp.where(lane == k, column, value)
    turned = value.T
    scalars[:, :loads] = turned[:4, :]
    scalars[:, loads:] = turned[4:8, :]


def last_kernel(
    extent, scalars, residual, search, applied, change, next_a, next_b, got_a, got_b, out_m, out_r
):
    loads, slots = residual.shape
    face = slots // 2
    total = jnp.sum(scalars[...], axis=0)
    total = jnp.concatenate([total[:, :loads], total[:, loads:]], axis=0)
    rho = total[0:1]
    gamma = total[1:2]
    alpha = rho / gamma
    rho_next = rho - alpha * total[2:3] + alpha * alpha * total[3:4]
    grow = 1.0 + rho_next / rho
    energy = grow * grow * gamma - 2.0 * grow * alpha * total[4:5] + alpha * alpha * total[5:6]
    alpha_next = rho_next / energy
    lengths = jnp.concatenate(
        [alpha + alpha_next * grow, alpha_next * alpha, jnp.zeros((6, rho.shape[1]), F32)], axis=0
    )
    turned = jnp.concatenate([lengths, jnp.zeros((120, rho.shape[1]), F32)], axis=0).T
    along, against = turned[:loads, 0:1], turned[:loads, 1:2]
    sides = []
    for side, own, got in ((0, next_a, got_a), (1, next_b, got_b)):
        cols = slice(side * face, (side + 1) * face)
        sides.append(
            (
                along * search[:, cols] - against * change[:, cols],
                residual[:, cols] - along * applied[:, cols] + against * (own[...] + got[...]),
            )
        )
    odd = chain(*extent).odd
    for k, out in ((0, out_m), (1, out_r)):
        out[:, 0, :] = jnp.where(odd, sides[0][k], sides[1][k])
        out[:, 1, :] = jnp.where(odd, sides[1][k], sides[0][k])


VMEM = pl.BlockSpec(memory_space=pltpu.VMEM)
HBM = pl.BlockSpec(memory_space=pltpu.HBM)


def shaped(shape, dtype=F32):
    return jax.ShapeDtypeStruct(shape, dtype)


def in_hbm(value):
    return pltpu.with_memory_space_constraint(value, pltpu.HBM)


def per_device(
    dual_load, dual_operator, index_map, stiffness, coarse_basis, dirichlet_blocks, coarse_inverse
):
    loads, _, face = dual_load.shape[2:]
    slots = 2 * face
    modes = coarse_basis.shape[2]
    block_count, size, _ = dirichlet_blocks.shape[2:]
    clusters, members = lax.axis_size("cluster"), lax.axis_size("member")
    devices = clusters * members
    extent = clusters, members
    load = dual_load.reshape(loads, 2, face)
    basis = coarse_basis.reshape(modes, 1, slots)
    blocks = dirichlet_blocks.reshape(block_count, size, size)

    evens = [(i, i + 1) for i in range(0, devices - 1, 2)]
    odds = [(i, i + 1) for i in range(1, devices - 1, 2)]
    evens = evens + [(j, i) for i, j in evens]
    odds = odds + [(j, i) for i, j in odds]

    def swap(side_a, side_b):
        from_b = lax.ppermute(side_b, AXES, odds)
        from_a = lax.ppermute(side_a, AXES, evens)
        return from_a, from_b

    def share(copies):
        parts = copies.reshape((-1,) + copies.shape[2:])
        return lax.all_to_all(parts, AXES, 0, 0, tiled=True).reshape(copies.shape)

    def params(mebibytes):
        return pltpu.CompilerParams(vmem_limit_bytes=mebibytes * 1024 * 1024)

    half_vector = shaped((loads, face))
    vector = shaped((loads, slots))
    half = block_count // 2
    packed = shaped((size // 2 + KP + loads, face))
    side_blocks = shaped((half, size, size), BF16)
    pay_a, pay_b, mine_a, mine_b = pl.pallas_call(
        functools.partial(pack_kernel, extent),
        out_shape=(packed, packed, side_blocks, side_blocks),
        in_specs=[HBM] * 3,
        out_specs=(VMEM,) * 4,
        scratch_shapes=[
            pltpu.VMEM(load.shape, F32),
            pltpu.VMEM(basis.shape, F32),
            pltpu.VMEM(blocks.shape, BF16),
            pltpu.SemaphoreType.DMA((3,)),
        ],
        compiler_params=params(8),
    )(*[in_hbm(v) for v in (load, basis, blocks)])
    got_a, got_b = swap(pay_a, pay_b)

    ordering = shaped((slots, slots), BF16)
    pick, place, operator, softness = pl.pallas_call(
        functools.partial(order_kernel, extent),
        out_shape=(ordering, ordering, ordering, shaped((1, 1))),
        in_specs=[HBM, VMEM, HBM],
        out_specs=(VMEM,) * 4,
        scratch_shapes=[pltpu.VMEM((1, slots), jnp.int32), pltpu.SemaphoreType.DMA((2,))],
        compiler_params=params(8),
    )(in_hbm(index_map.reshape(1, slots)), stiffness, in_hbm(dual_operator))
    pick, operator, place = [
        pltpu.with_memory_space_constraint(v, pltpu.VMEM) for v in (pick, operator, place)
    ]

    rows = loads + 4 * KP
    side_pairs = shaped((half, 2 * size, size), BF16)
    residual_a, smooth_a, coarse_a, own_basis_a, pairs_a, first_a, second_a = pl.pallas_call(
        functools.partial(near_kernel, extent, modes),
        out_shape=(
            half_vector,
            half_vector,
            shaped((12 * KP, face), BF16),
            shaped((2 * KP, face), BF16),
            side_pairs,
            shaped((2 * rows, face), BF16),
            shaped((2 * rows, slots), BF16),
        ),
        in_specs=[VMEM] * 4,
        out_specs=(VMEM,) * 7,
        compiler_params=params(8),
    )(pay_a, got_a, mine_a, pick)
    residual, smooth, coarse, pairs_b, image_a, image_b, keep = pl.pallas_call(
        functools.partial(first_kernel, extent, modes),
        out_shape=(
            vector,
            vector,
            shaped((12 * KP, slots), BF16),
            side_pairs,
            shaped((rows + KP, face)),
            shaped((rows, face)),
            shaped((2, KP, 2 * loads)),
        ),
        in_specs=[VMEM] * 13,
        out_specs=(VMEM,) * 7,
        scratch_shapes=[pltpu.VMEM((2 * KP, slots), BF16)]
        + [pltpu.VMEM((2 * rows, slots), BF16)] * 3
        + [pltpu.VMEM((4, KP, 2 * loads), F32)],
        compiler_params=params(12),
    )(
        softness, pay_b, got_b, mine_b, residual_a, smooth_a, coarse_a, own_basis_a, first_a,
        second_a, pick, operator, place,
    )

    got_a, got_b = swap(image_a, image_b)
    terms = pl.pallas_call(
        merge_kernel,
        out_shape=shaped((devices, 2 * modes // SLICE, SLICE, 2 * loads)),
        in_specs=[VMEM] * 2,
        out_specs=VMEM,
        compiler_params=params(8),
    )(keep, got_a)
    terms = pl.pallas_call(
        functools.partial(fold_kernel, clusters, members),
        out_shape=shaped((clusters * 6, 2 * modes, 2 * loads)),
        in_specs=[VMEM],
        out_specs=VMEM,
        compiler_params=params(8),
    )(share(terms))

    search, applied, change, next_a, next_b, scalars = pl.pallas_call(
        functools.partial(second_kernel, extent),
        out_shape=(vector, vector, vector, half_vector, half_vector, shaped((4, 2 * loads))),
        in_specs=[VMEM] * 15,
        out_specs=(VMEM,) * 6,
        scratch_shapes=[pltpu.VMEM((4, clusters, KP, loads), F32)]
        + [pltpu.VMEM((2 * loads, slots), BF16)] * 3,
        compiler_params=params(12),
    )(
        softness, terms, coarse_inverse, residual, smooth, coarse, pairs_a, pairs_b,
        image_a, image_b, got_a, got_b, pick, operator, place,
    )

    got_a, got_b = swap(next_a, next_b)
    scalars = share(jnp.broadcast_to(scalars[None, None], (devices, 1) + scalars.shape))
    scalars = scalars.reshape(devices, 4, 2 * loads)

    out_m, out_r = pl.pallas_call(
        functools.partial(last_kernel, extent),
        out_shape=(shaped((loads, 2, face)), shaped((loads, 2, face))),
        in_specs=[VMEM] * 9,
        out_specs=(VMEM, VMEM),
        compiler_params=params(12),
    )(scalars, residual, search, applied, change, next_a, next_b, got_a, got_b)
    return out_m.reshape(dual_load.shape), out_r.reshape(dual_load.shape)


def solution(mesh):
    in_specs = (
        P("cluster", "member", None, None, None),
        P(),
        P("cluster", "member", None),
        P("cluster", "member"),
        P("cluster", "member", None, None),
        P("cluster", "member", None, None, None),
        P(),
    )
    out_specs = (P("cluster", "member", None, None, None), P("cluster", "member", None, None, None))
    return jax.shard_map(
        per_device, mesh=mesh, in_specs=in_specs, out_specs=out_specs, check_vma=False
    )
```

```python
import functools
from typing import NamedTuple

import jax
import jax.numpy as jnp
from jax import lax
from jax.experimental import pallas as pl
from jax.experimental.pallas import tpu as pltpu
from jax.sharding import PartitionSpec as P

AXES = ("cluster", "member")
F32 = jnp.float32
BF16 = jnp.bfloat16
EXACT = lax.Precision.HIGHEST
SLICE = 4
KP = 8


def dot(left, right):
    return jnp.dot(left, right, preferred_element_type=F32)


def dot_rows(left, right):
    return lax.dot_general(left, right, (((1,), (1,)), ((), ())), preferred_element_type=F32)


def two_parts(value):
    high = value.astype(BF16)
    return high, (value - high.astype(F32)).astype(BF16)


def stacked(value):
    return jnp.concatenate(two_parts(value), axis=0)


def folded(value, rows, cols):
    value = value[:rows] + value[rows:]
    return value[:, :cols] + value[:, cols:]


def three_rows(value):
    high, low = two_parts(value)
    return jnp.concatenate([high, low, high], axis=0)


def dot_modes(amounts, rows):
    high, low = two_parts(amounts)
    left = jnp.concatenate([high, high, low], axis=0)
    return lax.dot_general(left, rows, (((0,), (0,)), ((), ())), preferred_element_type=F32)


class Chain(NamedTuple):
    odd: jax.Array
    own: tuple
    near: tuple
    weights: tuple
    same: tuple


def chain(clusters, members):
    count = clusters * members
    position = lax.axis_index("cluster") * members + lax.axis_index("member")
    parity = lax.rem(position, 2)

    def reach(pos):
        cluster, member = lax.div(pos, members), lax.rem(pos, members)
        other = cluster + jnp.where(member == members - 1, 1, jnp.where(member == 0, -1, 0))
        return cluster, jnp.clip(other, 0, clusters - 1)

    own = reach(position)
    near, weights, same = [], [], []
    for partner in (position + 1 - 2 * parity, position - 1 + 2 * parity):
        real = (partner >= 0) & (partner < count)
        there = reach(jnp.clip(partner, 0, count - 1))
        near.append(there)
        weights.append(jnp.where(real, 0.5, 1.0))
        same.append(jnp.where(real & (there[0] == own[0]), 1.0, 0.0))
    return Chain(parity == 1, own, tuple(near), tuple(weights), tuple(same))


def pack_side(first, load, basis, blocks, out, mine):
    loads, _, face = load.shape
    modes = basis.shape[0]
    half = blocks.shape[0] // 2
    size = blocks.shape[1]
    row = lax.broadcasted_iota(jnp.int32, (size, size), 0)
    col = lax.broadcasted_iota(jnp.int32, (size, size), 1)
    mid = size // 2
    low = mid + KP
    out[mid:low, :] = jnp.zeros((KP, face), F32)
    for k in range(modes):
        mode = basis[k]
        out[mid + k : mid + k + 1, :] = jnp.where(first, mode[:, :face], mode[:, face:])
    base = jnp.where(first, 0, half)
    for pair in range(half // 2):
        one, two = blocks[base + 2 * pair], blocks[base + 2 * pair + 1]
        mine[2 * pair] = one
        mine[2 * pair + 1] = two
        upper, lower = one.astype(F32), two.astype(F32)
        both = jnp.where(row <= col, upper, lower)
        left = pair * size
        right = (half // 2 + pair) * size
        out[:mid, left : left + size] = both[:mid]
        out[:mid, right : right + size] = both[mid:]
        diagonal = jnp.sum(jnp.where(row == col, lower, 0.0), axis=0, keepdims=True)
        out[mid + modes : mid + modes + 1, left : left + size] = diagonal
    out[low:, :] = jnp.where(first, load[:, 0, :], load[:, 1, :])


def pack_kernel(
    extent,
    far_load, far_basis, far_blocks,
    out_a, out_b, mine_a, mine_b,
    load, basis, blocks, arrived,
):
    copies = [
        pltpu.make_async_copy(source, target, arrived.at[k])
        for k, (source, target) in enumerate(
            ((far_blocks, blocks), (far_load, load), (far_basis, basis))
        )
    ]
    for copy in copies:
        copy.start()
    for copy in copies:
        copy.wait()
    odd = chain(*extent).odd
    pack_side(jnp.logical_not(odd), load, basis, blocks, out_b, mine_b)
    pack_side(odd, load, basis, blocks, out_a, mine_a)


def order_kernel(
    extent,
    far_index, stiffness, far_operator,
    pick, place, operator, softness,
    index, arrived,
):
    copies = [
        pltpu.make_async_copy(far_index, index, arrived.at[0]),
        pltpu.make_async_copy(far_operator, operator, arrived.at[1]),
    ]
    for copy in copies:
        copy.start()
    slots = pick.shape[0]
    face = slots // 2
    rows = 128
    odd = chain(*extent).odd
    softness[...] = 1.0 / stiffness[...]
    copies[0].wait()
    lane = lax.broadcasted_iota(jnp.int32, (rows, slots), 1).astype(jnp.int16)
    depth = lax.broadcasted_iota(jnp.int32, (rows, slots), 0).astype(jnp.int16)
    one, zero = jnp.ones((), BF16), jnp.zeros((), BF16)
    index_0, index_1 = index[:, :face], index[:, face:]
    wanted = jnp.concatenate(
        [jnp.where(odd, index_0, index_1), jnp.where(odd, index_1, index_0)], axis=1
    )
    every = jnp.broadcast_to(wanted, (rows, slots)).astype(jnp.int16)
    for start in range(0, slots, rows):
        here = jnp.broadcast_to(wanted[:, start : start + rows].astype(F32), (rows, rows)).T
        here = here.astype(jnp.int32).astype(jnp.int16)
        target = jnp.concatenate([here] * (slots // rows), axis=1)
        pick[start : start + rows, :] = jnp.where(target == lane, one, zero)
        place[start : start + rows, :] = jnp.where(every - jnp.int16(start) == depth, one, zero)
    copies[1].wait()


def merge_kernel(keep, got, out):
    kinds, depth, lanes = keep.shape
    rows = got.shape[0] - depth
    modes = out.shape[1] * SLICE // kinds
    values = [keep[k] + got[rows:, k * lanes : (k + 1) * lanes] for k in range(kinds)]
    value = jnp.concatenate([v[:modes] for v in values], axis=0)
    for part in range(out.shape[1]):
        piece = value[part * SLICE : (part + 1) * SLICE]
        out[:, part] = jnp.broadcast_to(piece[None], (out.shape[0],) + piece.shape)


def fold_kernel(clusters, members, terms, out):
    for c in range(clusters):
        for parity in range(2):
            for part in range(terms.shape[1]):
                begin = terms[c * members + parity, part]
                end = terms[(c + 1) * members - 2 + parity, part]
                value = begin
                for m in range(2, members, 2):
                    value = value + terms[c * members + m + parity, part]
                for k, result in enumerate((value, begin, end)):
                    out[(c * 2 + parity) * 3 + k, part * SLICE : (part + 1) * SLICE] = result


def apply_rest(rows, scale, operator, place, second, third, image_a, image_b):
    slots = second.shape[1]
    face = slots // 2

    product = dot(second[...], operator[...])
    high, low = two_parts(product[:rows] + product[rows:])
    third[:rows, :] = high
    third[rows:, :] = low

    product = dot(third[...], place[...])
    product = scale * (product[:rows] + product[rows:])
    image_a[:rows, :] = product[:, :face]
    image_b[:rows, :] = product[:, face:]


def smooth_block(value, weight, block_pair):
    rows = value.shape[0]
    high, low = two_parts(weight * value)
    left = jnp.concatenate(
        [jnp.concatenate([high, high], axis=1), jnp.concatenate([low, low], axis=1)], axis=0
    )
    product = dot(left, block_pair)
    return weight * (product[:rows] + product[rows:])


def side_part(
    modes, at, weight, same, pay, got, blocks, residual, smooth, coarse, own_basis, pairs, first
):
    half, size, _ = blocks.shape
    face = half * size
    loads = pay.shape[0] - size // 2 - KP
    rows = loads + 4 * KP
    mid = size // 2
    low = mid + KP
    cols = slice(at, at + face)
    row = lax.broadcasted_iota(jnp.int32, (size, size), 0)
    col = lax.broadcasted_iota(jnp.int32, (size, size), 1)
    real = lax.broadcasted_iota(jnp.int32, (KP, face), 0) < modes
    mine = jnp.where(real, pay[mid:low, :], 0.0)
    theirs = jnp.where(real, got[mid:low, :], 0.0)
    own_basis[:, cols] = stacked(mine)
    span = jnp.concatenate([mine + same * theirs, (1.0 - same) * theirs], axis=0)
    for pair in range(half // 2):
        left = pair * size
        right = (half // 2 + pair) * size
        both = jnp.concatenate(
            [got[:mid, left : left + size], got[:mid, right : right + size]], axis=0
        )
        turned = both.T
        diagonal = got[mid + modes : mid + modes + 1, left : left + size]
        upper = jnp.where(row <= col, both, turned)
        lower = jnp.where(row > col, both, jnp.where(row < col, turned, diagonal))
        for k, theirs_block in ((2 * pair, upper), (2 * pair + 1, lower)):
            block_pair = jnp.concatenate([blocks[k], theirs_block.astype(BF16)], axis=0)
            pairs[k] = block_pair
            there = slice(k * size, (k + 1) * size)
            cols = slice(at + k * size, at + (k + 1) * size)
            value = pay[low:, there] + got[low:, there]
            modes_here = span[:, there]
            result = smooth_block(
                jnp.concatenate([value, modes_here], axis=0), weight, block_pair
            )
            residual[:, cols] = value
            smooth[:, cols] = result[:loads]
            high, low_part = two_parts(
                jnp.concatenate([result[:loads], modes_here, result[loads:]], axis=0)
            )
            first[:rows, cols] = high
            first[rows:, cols] = low_part
            coarse[: 4 * KP, cols] = high[loads:]
            coarse[4 * KP : 8 * KP, cols] = low_part[loads:]
            coarse[8 * KP :, cols] = high[loads:]


def near_kernel(
    extent, modes,
    pay, got, blocks, pick,
    residual, smooth, coarse, own_basis, pairs, first, second,
):
    here = chain(*extent)
    side_part(
        modes, 0, here.weights[0], here.same[0], pay, got, blocks,
        residual, smooth, coarse, own_basis, pairs, first,
    )
    face = first.shape[1]

    second[...] = dot(first[...], pick[:face, :]).astype(BF16)


def first_kernel(
    extent, modes,
    softness, pay, got, blocks,
    residual_a, smooth_a, coarse_a, own_basis_a, first_a, second_a,
    pick, operator, place,
    residual, smooth, coarse, pairs, image_a, image_b, keep,
    own_basis, first, second, third, terms,
):
    loads, slots = residual.shape
    face = slots // 2
    rows = loads + 4 * KP
    here = chain(*extent)
    side_part(
        modes, face, here.weights[1], here.same[1], pay, got, blocks,
        residual, smooth, coarse, own_basis, pairs, first,
    )

    product = dot(first[:, face:], pick[face:, :]) + second_a[...].astype(F32)
    second[...] = product.astype(BF16)

    for whole, part in (
        (residual, residual_a), (smooth, smooth_a), (coarse, coarse_a),
        (own_basis, own_basis_a), (first, first_a),
    ):
        whole[:, :face] = part[...]
    apply_rest(rows, softness[...], operator, place, second, third, image_a, image_b)

    vectors = jnp.concatenate([stacked(residual[...]), first[...]], axis=0)
    sides = dot_rows(own_basis[...], vectors)
    load_side = folded(sides[:, : 2 * loads], KP, loads)
    smooth_side = folded(sides[:, 2 * loads :], KP, rows)
    shared = smooth_side[:, loads + 2 * KP :]
    energy = jnp.zeros((8 * KP, 2 * rows), F32)
    for side, image in ((0, image_a), (1, image_b)):
        cols = slice(side * face, (side + 1) * face)
        energy = energy + dot_rows(coarse[: 8 * KP, cols], stacked(image[:rows, :]))
    energy = folded(energy, 4 * KP, rows)
    terms[0, :, :loads] = load_side
    terms[0, :, loads:] = smooth_side[:, :loads]
    terms[1, :, :loads] = energy[:KP, :loads]
    terms[1, :, loads:] = energy[KP : 2 * KP, :loads]
    terms[2, :, :loads] = energy[2 * KP : 3 * KP, :loads]
    terms[2, :, loads:] = energy[3 * KP :, :loads]
    for i in range(2):
        for j in range(2):
            at = (2 * i + j) * 4 * KP
            basis_rows = energy[i * KP : (i + 1) * KP]
            smooth_rows = energy[(2 + i) * KP : (3 + i) * KP]
            basis_cols = slice(loads + j * KP, loads + (j + 1) * KP)
            smooth_cols = slice(loads + (2 + j) * KP, loads + (3 + j) * KP)
            terms[3, :, at : at + KP] = basis_rows[:, basis_cols]
            terms[3, :, at + KP : at + 2 * KP] = basis_rows[:, smooth_cols]
            terms[3, :, at + 2 * KP : at + 3 * KP] = smooth_rows[:, smooth_cols]
            last = shared[:, j * KP : (j + 1) * KP] if i == 0 else jnp.zeros((KP, KP), F32)
            terms[3, :, at + 3 * KP : at + 4 * KP] = last
    keep[...] = jnp.where(here.odd, terms[2:], terms[:2])
    image_a[rows:, :] = jnp.zeros((KP, face), F32)
    for kind in range(2):
        image_a[rows:, kind * 2 * loads : (kind + 1) * 2 * loads] = jnp.where(
            here.odd, terms[kind], terms[2 + kind]
        )


def coarse_solves(clusters, loads, terms, inverse):
    modes = inverse.shape[0] // clusters

    def one_kind(c, kind, which):
        value = terms[(c * 2 + kind // 2) * 3 + which]
        value = value[kind % 2 * modes : (kind % 2 + 1) * modes]
        return jnp.concatenate([value, jnp.zeros((KP - modes, value.shape[1]), F32)], axis=0)

    def total(c, kind):
        return one_kind(c, kind, 0)

    def begin(c, kind):
        return one_kind(c, kind, 1)

    def end(c, kind):
        return one_kind(c, kind, 2)

    span = 4 * KP
    lanes = terms.shape[-1]
    totals = [total(c, 0) for c in range(clusters)]
    load_side = [v[:, :loads] for v in totals]
    smooth_side = [v[:, loads:] for v in totals]

    def images(kind):
        found = []
        for c in range(clusters):
            value = total(c, kind)[:, :loads]
            if c + 1 < clusters:
                value = value + begin(c + 1, kind)[:, loads:]
            if c > 0:
                value = value + end(c - 1, kind)[:, loads:]
            found.append(value)
        return found

    centre, below, above = [], [], []
    for c in range(clusters):
        value, under, over = total(c, 3), begin(c, 3), end(c, 3)
        if c + 1 < clusters:
            value = value + pltpu.roll(begin(c + 1, 3), lanes - 3 * span, 1)
            over = over + pltpu.roll(begin(c + 1, 3), lanes - span, 1)
        if c > 0:
            value = value + pltpu.roll(end(c - 1, 3), lanes - 3 * span, 1)
            under = under + pltpu.roll(end(c - 1, 3), lanes - span, 1)
        centre.append(value)
        below.append(under)
        above.append(over)

    def block_times(block, amounts):
        value = block[:, 0:1] * amounts[0:1]
        for k in range(1, KP):
            value = value + block[:, k : k + 1] * amounts[k : k + 1]
        return value

    def times(kind, amounts):
        found = []
        for c in range(clusters):
            near, far = slice(kind * KP, (kind + 1) * KP), slice(span + kind * KP, span + (kind + 1) * KP)
            value = block_times(centre[c][:, near], amounts[c])
            if c > 0:
                value = value + block_times(below[c][:, far], amounts[c - 1])
            if c + 1 < clusters:
                value = value + block_times(above[c][:, far], amounts[c + 1])
            found.append(value)
        return found

    turned_centre = [v.T for v in centre]
    turned_below = [v.T for v in below]
    turned_above = [v.T for v in above]

    def turned_times(kind, amounts):
        found = []
        near, far = slice(kind * KP, (kind + 1) * KP), slice(span + kind * KP, span + (kind + 1) * KP)
        for c in range(clusters):
            value = block_times(turned_centre[c][near], amounts[c])
            if c > 0:
                value = value + block_times(turned_above[c - 1][far], amounts[c - 1])
            if c + 1 < clusters:
                value = value + block_times(turned_below[c + 1][far], amounts[c + 1])
            found.append(value)
        return found

    row = lax.broadcasted_iota(jnp.int32, (clusters * KP, clusters * modes), 0)
    col = lax.broadcasted_iota(jnp.int32, (clusters * KP, clusters * modes), 1)
    mode = row % KP
    spread = jnp.where((mode < modes) & (col == row // KP * modes + mode), 1.0, 0.0)
    padded = jnp.dot(spread, inverse[...], precision=EXACT, preferred_element_type=F32)
    padded = lax.dot_general(
        padded, spread, (((1,), (1,)), ((), ())), precision=EXACT, preferred_element_type=F32
    )

    def solve(parts):
        value = jnp.dot(
            padded, jnp.concatenate(parts, axis=0), precision=EXACT, preferred_element_type=F32
        )
        return [value[c * KP : (c + 1) * KP] for c in range(clusters)]

    def less(left, *others):
        found = list(left)
        for other in others:
            found = [p - q for p, q in zip(found, other)]
        return found

    load_amounts = solve(load_side)
    smooth_amounts = solve(less(smooth_side, times(3, load_amounts)))
    image_amounts = solve(less(images(1), times(1, load_amounts), times(0, smooth_amounts)))
    image_side = less(images(2), times(2, load_amounts), turned_times(1, smooth_amounts))
    smooth_image_amounts = solve(less(image_side, times(3, image_amounts)))
    return load_amounts, smooth_amounts, image_amounts, smooth_image_amounts


def second_kernel(
    extent,
    softness, terms, inverse, residual, smooth, coarse, pairs_a, pairs_b,
    image_a, image_b, got_a, got_b,
    pick, operator, place,
    search, applied, change, next_a, next_b, scalars,
    amounts, first, second, third,
):
    loads, slots = residual.shape
    face = slots // 2
    half, _, size = pairs_a.shape
    clusters, _ = extent
    here = chain(*extent)

    def weighted(left, right):
        product = left * right
        near = jnp.sum(product[:, :face], axis=1, keepdims=True)
        far = jnp.sum(product[:, face:], axis=1, keepdims=True)
        return here.weights[0] * near + here.weights[1] * far

    solved = coarse_solves(clusters, loads, terms, inverse)
    for kind, parts in enumerate(solved):
        for c, part in enumerate(parts):
            amounts[kind, c] = part

    def local(kind, reached):
        return [amounts[kind, c] for c in reached]

    none = [jnp.zeros((2 * KP, loads), F32)]
    own = jnp.concatenate(local(1, here.own) + local(0, here.own), axis=0)
    image_own = jnp.concatenate(local(3, here.own) + local(2, here.own), axis=0)
    own_basis = jnp.concatenate(local(0, here.own) + none, axis=0)
    image_own_basis = jnp.concatenate(local(2, here.own) + none, axis=0)
    projected = residual[...] - dot_modes(own_basis, coarse[...])
    direction = smooth[...] - dot_modes(own, coarse[...])
    search[...] = direction
    for side, image, got in ((0, image_a, got_a), (1, image_b, got_b)):
        theirs = local(1, here.near[side]) + local(0, here.near[side])
        mixed = jnp.concatenate([own] + theirs, axis=0)
        rows = slice(loads, loads + 4 * KP)
        rows = three_rows(jnp.concatenate([image[rows, :], got[rows, :]], axis=0))
        applied[:, side * face : (side + 1) * face] = (
            image[:loads, :] + got[:loads, :] - dot_modes(mixed, rows)
        )
    image_projected = applied[...] - dot_modes(image_own_basis, coarse[...])
    for side, pairs in ((0, pairs_a), (1, pairs_b)):
        for k in range(half):
            cols = slice(side * face + k * size, side * face + (k + 1) * size)
            change[:, cols] = smooth_block(applied[:, cols], here.weights[side], pairs[k])
    changed = change[...] - dot_modes(image_own, coarse[...])
    change[...] = changed
    high, low = two_parts(changed)
    first[:loads, :] = high
    first[loads:, :] = low
    found = [
        weighted(projected, direction),
        weighted(direction, applied[...]),
        weighted(projected, changed) + weighted(image_projected, direction),
        weighted(image_projected, changed),
    ]

    second[...] = dot(first[...], pick[...]).astype(BF16)

    apply_rest(loads, softness[...], operator, place, second, third, next_a, next_b)

    for vector in (search, change):
        column = jnp.sum(vector[:, :face] * next_a[...], axis=1, keepdims=True)
        column = column + jnp.sum(vector[:, face:] * next_b[...], axis=1, keepdims=True)
        found.append(column)
    lane = lax.broadcasted_iota(jnp.int32, (loads, 128), 1)
    value = jnp.zeros(lane.shape, F32)
    for k, column in enumerate(found):
        value = jnp.where(lane == k, column, value)
    turned = value.T
    scalars[:, :loads] = turned[:4, :]
    scalars[:, loads:] = turned[4:8, :]


def last_kernel(
    extent, scalars, residual, search, applied, change, next_a, next_b, got_a, got_b, out_m, out_r
):
    loads, slots = residual.shape
    face = slots // 2
    total = jnp.sum(scalars[...], axis=0)
    total = jnp.concatenate([total[:, :loads], total[:, loads:]], axis=0)
    rho = total[0:1]
    gamma = total[1:2]
    alpha = rho / gamma
    rho_next = rho - alpha * total[2:3] + alpha * alpha * total[3:4]
    grow = 1.0 + rho_next / rho
    energy = grow * grow * gamma - 2.0 * grow * alpha * total[4:5] + alpha * alpha * total[5:6]
    alpha_next = rho_next / energy
    lengths = jnp.concatenate(
        [alpha + alpha_next * grow, alpha_next * alpha, jnp.zeros((6, rho.shape[1]), F32)], axis=0
    )
    turned = jnp.concatenate([lengths, jnp.zeros((120, rho.shape[1]), F32)], axis=0).T
    along, against = turned[:loads, 0:1], turned[:loads, 1:2]
    sides = []
    for side, own, got in ((0, next_a, got_a), (1, next_b, got_b)):
        cols = slice(side * face, (side + 1) * face)
        sides.append(
            (
                along * search[:, cols] - against * change[:, cols],
                residual[:, cols] - along * applied[:, cols] + against * (own[...] + got[...]),
            )
        )
    odd = chain(*extent).odd
    for k, out in ((0, out_m), (1, out_r)):
        out[:, 0, :] = jnp.where(odd, sides[0][k], sides[1][k])
        out[:, 1, :] = jnp.where(odd, sides[1][k], sides[0][k])


VMEM = pl.BlockSpec(memory_space=pltpu.VMEM)
HBM = pl.BlockSpec(memory_space=pltpu.HBM)


def shaped(shape, dtype=F32):
    return jax.ShapeDtypeStruct(shape, dtype)


def in_hbm(value):
    return pltpu.with_memory_space_constraint(value, pltpu.HBM)


def per_device(
    dual_load, dual_operator, index_map, stiffness, coarse_basis, dirichlet_blocks, coarse_inverse
):
    loads, _, face = dual_load.shape[2:]
    slots = 2 * face
    modes = coarse_basis.shape[2]
    block_count, size, _ = dirichlet_blocks.shape[2:]
    clusters, members = lax.axis_size("cluster"), lax.axis_size("member")
    devices = clusters * members
    extent = clusters, members
    load = dual_load.reshape(loads, 2, face)
    basis = coarse_basis.reshape(modes, 1, slots)
    blocks = dirichlet_blocks.reshape(block_count, size, size)

    evens = [(i, i + 1) for i in range(0, devices - 1, 2)]
    odds = [(i, i + 1) for i in range(1, devices - 1, 2)]
    evens = evens + [(j, i) for i, j in evens]
    odds = odds + [(j, i) for i, j in odds]

    def swap(side_a, side_b):
        from_b = lax.ppermute(side_b, AXES, odds)
        from_a = lax.ppermute(side_a, AXES, evens)
        return from_a, from_b

    def share(copies):
        parts = copies.reshape((-1,) + copies.shape[2:])
        return lax.all_to_all(parts, AXES, 0, 0, tiled=True).reshape(copies.shape)

    def params(mebibytes):
        return pltpu.CompilerParams(vmem_limit_bytes=mebibytes * 1024 * 1024)

    half_vector = shaped((loads, face))
    vector = shaped((loads, slots))
    half = block_count // 2
    packed = shaped((size // 2 + KP + loads, face))
    side_blocks = shaped((half, size, size), BF16)
    pay_a, pay_b, mine_a, mine_b = pl.pallas_call(
        functools.partial(pack_kernel, extent),
        out_shape=(packed, packed, side_blocks, side_blocks),
        in_specs=[HBM] * 3,
        out_specs=(VMEM,) * 4,
        scratch_shapes=[
            pltpu.VMEM(load.shape, F32),
            pltpu.VMEM(basis.shape, F32),
            pltpu.VMEM(blocks.shape, BF16),
            pltpu.SemaphoreType.DMA((3,)),
        ],
        compiler_params=params(8),
    )(*[in_hbm(v) for v in (load, basis, blocks)])
    got_a, got_b = swap(pay_a, pay_b)

    ordering = shaped((slots, slots), BF16)
    pick, place, operator, softness = pl.pallas_call(
        functools.partial(order_kernel, extent),
        out_shape=(ordering, ordering, ordering, shaped((1, 1))),
        in_specs=[HBM, VMEM, HBM],
        out_specs=(VMEM,) * 4,
        scratch_shapes=[pltpu.VMEM((1, slots), jnp.int32), pltpu.SemaphoreType.DMA((2,))],
        compiler_params=params(8),
    )(in_hbm(index_map.reshape(1, slots)), stiffness, in_hbm(dual_operator))
    pick, operator, place = [
        pltpu.with_memory_space_constraint(v, pltpu.VMEM) for v in (pick, operator, place)
    ]

    rows = loads + 4 * KP
    side_pairs = shaped((half, 2 * size, size), BF16)
    residual_a, smooth_a, coarse_a, own_basis_a, pairs_a, first_a, second_a = pl.pallas_call(
        functools.partial(near_kernel, extent, modes),
        out_shape=(
            half_vector,
            half_vector,
            shaped((12 * KP, face), BF16),
            shaped((2 * KP, face), BF16),
            side_pairs,
            shaped((2 * rows, face), BF16),
            shaped((2 * rows, slots), BF16),
        ),
        in_specs=[VMEM] * 4,
        out_specs=(VMEM,) * 7,
        compiler_params=params(8),
    )(pay_a, got_a, mine_a, pick)
    residual, smooth, coarse, pairs_b, image_a, image_b, keep = pl.pallas_call(
        functools.partial(first_kernel, extent, modes),
        out_shape=(
            vector,
            vector,
            shaped((12 * KP, slots), BF16),
            side_pairs,
            shaped((rows + KP, face)),
            shaped((rows, face)),
            shaped((2, KP, 2 * loads)),
        ),
        in_specs=[VMEM] * 13,
        out_specs=(VMEM,) * 7,
        scratch_shapes=[pltpu.VMEM((2 * KP, slots), BF16)]
        + [pltpu.VMEM((2 * rows, slots), BF16)] * 3
        + [pltpu.VMEM((4, KP, 2 * loads), F32)],
        compiler_params=params(12),
    )(
        softness, pay_b, got_b, mine_b, residual_a, smooth_a, coarse_a, own_basis_a, first_a,
        second_a, pick, operator, place,
    )

    got_a, got_b = swap(image_a, image_b)
    terms = pl.pallas_call(
        merge_kernel,
        out_shape=shaped((devices, 2 * modes // SLICE, SLICE, 2 * loads)),
        in_specs=[VMEM] * 2,
        out_specs=VMEM,
        compiler_params=params(8),
    )(keep, got_a)
    terms = pl.pallas_call(
        functools.partial(fold_kernel, clusters, members),
        out_shape=shaped((clusters * 6, 2 * modes, 2 * loads)),
        in_specs=[VMEM],
        out_specs=VMEM,
        compiler_params=params(8),
    )(share(terms))

    search, applied, change, next_a, next_b, scalars = pl.pallas_call(
        functools.partial(second_kernel, extent),
        out_shape=(vector, vector, vector, half_vector, half_vector, shaped((4, 2 * loads))),
        in_specs=[VMEM] * 15,
        out_specs=(VMEM,) * 6,
        scratch_shapes=[pltpu.VMEM((4, clusters, KP, loads), F32)]
        + [pltpu.VMEM((2 * loads, slots), BF16)] * 3,
        compiler_params=params(12),
    )(
        softness, terms, coarse_inverse, residual, smooth, coarse, pairs_a, pairs_b,
        image_a, image_b, got_a, got_b, pick, operator, place,
    )

    got_a, got_b = swap(next_a, next_b)
    scalars = share(jnp.broadcast_to(scalars[None, None], (devices, 1) + scalars.shape))
    scalars = scalars.reshape(devices, 4, 2 * loads)

    out_m, out_r = pl.pallas_call(
        functools.partial(last_kernel, extent),
        out_shape=(shaped((loads, 2, face)), shaped((loads, 2, face))),
        in_specs=[VMEM] * 9,
        out_specs=(VMEM, VMEM),
        compiler_params=params(12),
    )(scalars, residual, search, applied, change, next_a, next_b, got_a, got_b)
    return out_m.reshape(dual_load.shape), out_r.reshape(dual_load.shape)


def solution(mesh):
    in_specs = (
        P("cluster", "member", None, None, None),
        P(),
        P("cluster", "member", None),
        P("cluster", "member"),
        P("cluster", "member", None, None),
        P("cluster", "member", None, None, None),
        P(),
    )
    out_specs = (P("cluster", "member", None, None, None), P("cluster", "member", None, None, None))
    return jax.shard_map(
        per_device, mesh=mesh, in_specs=in_specs, out_specs=out_specs, check_vma=False
    )
```

```python
import functools
from typing import NamedTuple

import jax
import jax.numpy as jnp
from jax import lax
from jax.experimental import pallas as pl
from jax.experimental.pallas import tpu as pltpu
from jax.sharding import PartitionSpec as P

AXES = ("cluster", "member")
F32 = jnp.float32
BF16 = jnp.bfloat16
EXACT = lax.Precision.HIGHEST
SLICE = 4
KP = 8


def dot(left, right):
    return jnp.dot(left, right, preferred_element_type=F32)


def dot_rows(left, right):
    return lax.dot_general(left, right, (((1,), (1,)), ((), ())), preferred_element_type=F32)


def two_parts(value):
    high = value.astype(BF16)
    return high, (value - high.astype(F32)).astype(BF16)


def stacked(value):
    return jnp.concatenate(two_parts(value), axis=0)


def folded(value, rows, cols):
    value = value[:rows] + value[rows:]
    return value[:, :cols] + value[:, cols:]


def three_rows(value):
    high, low = two_parts(value)
    return jnp.concatenate([high, low, high], axis=0)


def dot_modes(amounts, rows):
    high, low = two_parts(amounts)
    left = jnp.concatenate([high, high, low], axis=0)
    return lax.dot_general(left, rows, (((0,), (0,)), ((), ())), preferred_element_type=F32)


class Chain(NamedTuple):
    odd: jax.Array
    own: tuple
    near: tuple
    weights: tuple
    same: tuple


def chain(clusters, members):
    count = clusters * members
    position = lax.axis_index("cluster") * members + lax.axis_index("member")
    parity = lax.rem(position, 2)

    def reach(pos):
        cluster, member = lax.div(pos, members), lax.rem(pos, members)
        other = cluster + jnp.where(member == members - 1, 1, jnp.where(member == 0, -1, 0))
        return cluster, jnp.clip(other, 0, clusters - 1)

    own = reach(position)
    near, weights, same = [], [], []
    for partner in (position + 1 - 2 * parity, position - 1 + 2 * parity):
        real = (partner >= 0) & (partner < count)
        there = reach(jnp.clip(partner, 0, count - 1))
        near.append(there)
        weights.append(jnp.where(real, 0.5, 1.0))
        same.append(jnp.where(real & (there[0] == own[0]), 1.0, 0.0))
    return Chain(parity == 1, own, tuple(near), tuple(weights), tuple(same))


def pack_side(first, load, basis, blocks, out, mine):
    loads, _, face = load.shape
    modes = basis.shape[0]
    half = blocks.shape[0] // 2
    size = blocks.shape[1]
    row = lax.broadcasted_iota(jnp.int32, (size, size), 0)
    col = lax.broadcasted_iota(jnp.int32, (size, size), 1)
    mid = size // 2
    low = mid + KP
    out[mid:low, :] = jnp.zeros((KP, face), F32)
    for k in range(modes):
        mode = basis[k]
        out[mid + k : mid + k + 1, :] = jnp.where(first, mode[:, :face], mode[:, face:])
    base = jnp.where(first, 0, half)
    for pair in range(half // 2):
        one, two = blocks[base + 2 * pair], blocks[base + 2 * pair + 1]
        mine[2 * pair] = one
        mine[2 * pair + 1] = two
        upper, lower = one.astype(F32), two.astype(F32)
        both = jnp.where(row <= col, upper, lower)
        left = pair * size
        right = (half // 2 + pair) * size
        out[:mid, left : left + size] = both[:mid]
        out[:mid, right : right + size] = both[mid:]
        diagonal = jnp.sum(jnp.where(row == col, lower, 0.0), axis=0, keepdims=True)
        out[mid + modes : mid + modes + 1, left : left + size] = diagonal
    out[low:, :] = jnp.where(first, load[:, 0, :], load[:, 1, :])


def pack_kernel(
    extent,
    far_load, far_basis, far_blocks,
    out_a, out_b, mine_a, mine_b,
    load, basis, blocks, arrived,
):
    copies = [
        pltpu.make_async_copy(source, target, arrived.at[k])
        for k, (source, target) in enumerate(
            ((far_blocks, blocks), (far_load, load), (far_basis, basis))
        )
    ]
    for copy in copies:
        copy.start()
    for copy in copies:
        copy.wait()
    odd = chain(*extent).odd
    pack_side(jnp.logical_not(odd), load, basis, blocks, out_b, mine_b)
    pack_side(odd, load, basis, blocks, out_a, mine_a)


def order_kernel(
    extent,
    far_index, stiffness, far_operator,
    pick, place, operator, softness,
    index, arrived,
):
    copies = [
        pltpu.make_async_copy(far_index, index, arrived.at[0]),
        pltpu.make_async_copy(far_operator, operator, arrived.at[1]),
    ]
    for copy in copies:
        copy.start()
    slots = pick.shape[0]
    face = slots // 2
    rows = 128
    odd = chain(*extent).odd
    softness[...] = 1.0 / stiffness[...]
    copies[0].wait()
    lane = lax.broadcasted_iota(jnp.int32, (rows, slots), 1).astype(jnp.int16)
    depth = lax.broadcasted_iota(jnp.int32, (rows, slots), 0).astype(jnp.int16)
    one, zero = jnp.ones((), BF16), jnp.zeros((), BF16)
    index_0, index_1 = index[:, :face], index[:, face:]
    wanted = jnp.concatenate(
        [jnp.where(odd, index_0, index_1), jnp.where(odd, index_1, index_0)], axis=1
    )
    every = jnp.broadcast_to(wanted, (rows, slots)).astype(jnp.int16)
    for start in range(0, slots, rows):
        here = jnp.broadcast_to(wanted[:, start : start + rows].astype(F32), (rows, rows)).T
        here = here.astype(jnp.int32).astype(jnp.int16)
        target = jnp.concatenate([here] * (slots // rows), axis=1)
        pick[start : start + rows, :] = jnp.where(target == lane, one, zero)
        place[start : start + rows, :] = jnp.where(every - jnp.int16(start) == depth, one, zero)
    copies[1].wait()


def merge_kernel(keep, got, out):
    kinds, depth, lanes = keep.shape
    rows = got.shape[0] - depth
    modes = out.shape[1] * SLICE // kinds
    values = [keep[k] + got[rows:, k * lanes : (k + 1) * lanes] for k in range(kinds)]
    value = jnp.concatenate([v[:modes] for v in values], axis=0)
    for part in range(out.shape[1]):
        piece = value[part * SLICE : (part + 1) * SLICE]
        out[:, part] = jnp.broadcast_to(piece[None], (out.shape[0],) + piece.shape)


def fold_kernel(clusters, members, terms, out):
    for c in range(clusters):
        for parity in range(2):
            for part in range(terms.shape[1]):
                begin = terms[c * members + parity, part]
                end = terms[(c + 1) * members - 2 + parity, part]
                value = begin
                for m in range(2, members, 2):
                    value = value + terms[c * members + m + parity, part]
                for k, result in enumerate((value, begin, end)):
                    out[(c * 2 + parity) * 3 + k, part * SLICE : (part + 1) * SLICE] = result


def apply_rest(rows, scale, operator, place, second, third, image_a, image_b):
    slots = second.shape[1]
    face = slots // 2

    product = dot(second[...], operator[...])
    high, low = two_parts(product[:rows] + product[rows:])
    third[:rows, :] = high
    third[rows:, :] = low

    product = dot(third[...], place[...])
    product = scale * (product[:rows] + product[rows:])
    image_a[:rows, :] = product[:, :face]
    image_b[:rows, :] = product[:, face:]


def smooth_block(value, weight, block_pair):
    rows = value.shape[0]
    high, low = two_parts(weight * value)
    left = jnp.concatenate(
        [jnp.concatenate([high, high], axis=1), jnp.concatenate([low, low], axis=1)], axis=0
    )
    product = dot(left, block_pair)
    return weight * (product[:rows] + product[rows:])


def side_part(
    modes, at, weight, same, pay, got, blocks, residual, smooth, coarse, own_basis, pairs, first
):
    half, size, _ = blocks.shape
    face = half * size
    loads = pay.shape[0] - size // 2 - KP
    rows = loads + 4 * KP
    mid = size // 2
    low = mid + KP
    cols = slice(at, at + face)
    row = lax.broadcasted_iota(jnp.int32, (size, size), 0)
    col = lax.broadcasted_iota(jnp.int32, (size, size), 1)
    real = lax.broadcasted_iota(jnp.int32, (KP, face), 0) < modes
    mine = jnp.where(real, pay[mid:low, :], 0.0)
    theirs = jnp.where(real, got[mid:low, :], 0.0)
    own_basis[:, cols] = stacked(mine)
    span = jnp.concatenate([mine + same * theirs, (1.0 - same) * theirs], axis=0)
    for pair in range(half // 2):
        left = pair * size
        right = (half // 2 + pair) * size
        both = jnp.concatenate(
            [got[:mid, left : left + size], got[:mid, right : right + size]], axis=0
        )
        turned = both.T
        diagonal = got[mid + modes : mid + modes + 1, left : left + size]
        upper = jnp.where(row <= col, both, turned)
        lower = jnp.where(row > col, both, jnp.where(row < col, turned, diagonal))
        for k, theirs_block in ((2 * pair, upper), (2 * pair + 1, lower)):
            block_pair = jnp.concatenate([blocks[k], theirs_block.astype(BF16)], axis=0)
            pairs[k] = block_pair
            there = slice(k * size, (k + 1) * size)
            cols = slice(at + k * size, at + (k + 1) * size)
            value = pay[low:, there] + got[low:, there]
            modes_here = span[:, there]
            result = smooth_block(
                jnp.concatenate([value, modes_here], axis=0), weight, block_pair
            )
            residual[:, cols] = value
            smooth[:, cols] = result[:loads]
            high, low_part = two_parts(
                jnp.concatenate([result[:loads], modes_here, result[loads:]], axis=0)
            )
            first[:rows, cols] = high
            first[rows:, cols] = low_part
            coarse[: 4 * KP, cols] = high[loads:]
            coarse[4 * KP : 8 * KP, cols] = low_part[loads:]
            coarse[8 * KP :, cols] = high[loads:]


def near_kernel(
    extent, modes,
    pay, got, blocks, pick,
    residual, smooth, coarse, own_basis, pairs, first, second,
):
    here = chain(*extent)
    side_part(
        modes, 0, here.weights[0], here.same[0], pay, got, blocks,
        residual, smooth, coarse, own_basis, pairs, first,
    )
    face = first.shape[1]

    second[...] = dot(first[...], pick[:face, :]).astype(BF16)


def first_kernel(
    extent, modes,
    softness, pay, got, blocks,
    residual_a, smooth_a, coarse_a, own_basis_a, first_a, second_a,
    pick, operator, place,
    residual, smooth, coarse, pairs, image_a, image_b, keep,
    own_basis, first, second, third, terms,
):
    loads, slots = residual.shape
    face = slots // 2
    rows = loads + 4 * KP
    here = chain(*extent)
    side_part(
        modes, face, here.weights[1], here.same[1], pay, got, blocks,
        residual, smooth, coarse, own_basis, pairs, first,
    )

    product = dot(first[:, face:], pick[face:, :]) + second_a[...].astype(F32)
    second[...] = product.astype(BF16)

    for whole, part in (
        (residual, residual_a), (smooth, smooth_a), (coarse, coarse_a),
        (own_basis, own_basis_a), (first, first_a),
    ):
        whole[:, :face] = part[...]
    apply_rest(rows, softness[...], operator, place, second, third, image_a, image_b)

    vectors = jnp.concatenate([stacked(residual[...]), first[...]], axis=0)
    sides = dot_rows(own_basis[...], vectors)
    load_side = folded(sides[:, : 2 * loads], KP, loads)
    smooth_side = folded(sides[:, 2 * loads :], KP, rows)
    shared = smooth_side[:, loads + 2 * KP :]
    energy = jnp.zeros((8 * KP, 2 * rows), F32)
    for side, image in ((0, image_a), (1, image_b)):
        cols = slice(side * face, (side + 1) * face)
        energy = energy + dot_rows(coarse[: 8 * KP, cols], stacked(image[:rows, :]))
    energy = folded(energy, 4 * KP, rows)
    terms[0, :, :loads] = load_side
    terms[0, :, loads:] = smooth_side[:, :loads]
    terms[1, :, :loads] = energy[:KP, :loads]
    terms[1, :, loads:] = energy[KP : 2 * KP, :loads]
    terms[2, :, :loads] = energy[2 * KP : 3 * KP, :loads]
    terms[2, :, loads:] = energy[3 * KP :, :loads]
    for i in range(2):
        for j in range(2):
            at = (2 * i + j) * 4 * KP
            basis_rows = energy[i * KP : (i + 1) * KP]
            smooth_rows = energy[(2 + i) * KP : (3 + i) * KP]
            basis_cols = slice(loads + j * KP, loads + (j + 1) * KP)
            smooth_cols = slice(loads + (2 + j) * KP, loads + (3 + j) * KP)
            terms[3, :, at : at + KP] = basis_rows[:, basis_cols]
            terms[3, :, at + KP : at + 2 * KP] = basis_rows[:, smooth_cols]
            terms[3, :, at + 2 * KP : at + 3 * KP] = smooth_rows[:, smooth_cols]
            last = shared[:, j * KP : (j + 1) * KP] if i == 0 else jnp.zeros((KP, KP), F32)
            terms[3, :, at + 3 * KP : at + 4 * KP] = last
    keep[...] = jnp.where(here.odd, terms[2:], terms[:2])
    image_a[rows:, :] = jnp.zeros((KP, face), F32)
    for kind in range(2):
        image_a[rows:, kind * 2 * loads : (kind + 1) * 2 * loads] = jnp.where(
            here.odd, terms[kind], terms[2 + kind]
        )


def coarse_solves(clusters, loads, terms, inverse):
    modes = inverse.shape[0] // clusters

    def one_kind(c, kind, which):
        value = terms[(c * 2 + kind // 2) * 3 + which]
        value = value[kind % 2 * modes : (kind % 2 + 1) * modes]
        return jnp.concatenate([value, jnp.zeros((KP - modes, value.shape[1]), F32)], axis=0)

    def total(c, kind):
        return one_kind(c, kind, 0)

    def begin(c, kind):
        return one_kind(c, kind, 1)

    def end(c, kind):
        return one_kind(c, kind, 2)

    span = 4 * KP
    lanes = terms.shape[-1]
    totals = [total(c, 0) for c in range(clusters)]
    load_side = [v[:, :loads] for v in totals]
    smooth_side = [v[:, loads:] for v in totals]

    def images(kind):
        found = []
        for c in range(clusters):
            value = total(c, kind)[:, :loads]
            if c + 1 < clusters:
                value = value + begin(c + 1, kind)[:, loads:]
            if c > 0:
                value = value + end(c - 1, kind)[:, loads:]
            found.append(value)
        return found

    centre, below, above = [], [], []
    for c in range(clusters):
        value, under, over = total(c, 3), begin(c, 3), end(c, 3)
        if c + 1 < clusters:
            value = value + pltpu.roll(begin(c + 1, 3), lanes - 3 * span, 1)
            over = over + pltpu.roll(begin(c + 1, 3), lanes - span, 1)
        if c > 0:
            value = value + pltpu.roll(end(c - 1, 3), lanes - 3 * span, 1)
            under = under + pltpu.roll(end(c - 1, 3), lanes - span, 1)
        centre.append(value)
        below.append(under)
        above.append(over)

    def block_times(block, amounts):
        value = block[:, 0:1] * amounts[0:1]
        for k in range(1, KP):
            value = value + block[:, k : k + 1] * amounts[k : k + 1]
        return value

    def times(kind, amounts):
        found = []
        for c in range(clusters):
            near, far = slice(kind * KP, (kind + 1) * KP), slice(span + kind * KP, span + (kind + 1) * KP)
            value = block_times(centre[c][:, near], amounts[c])
            if c > 0:
                value = value + block_times(below[c][:, far], amounts[c - 1])
            if c + 1 < clusters:
                value = value + block_times(above[c][:, far], amounts[c + 1])
            found.append(value)
        return found

    turned_centre = [v.T for v in centre]
    turned_below = [v.T for v in below]
    turned_above = [v.T for v in above]

    def turned_times(kind, amounts):
        found = []
        near, far = slice(kind * KP, (kind + 1) * KP), slice(span + kind * KP, span + (kind + 1) * KP)
        for c in range(clusters):
            value = block_times(turned_centre[c][near], amounts[c])
            if c > 0:
                value = value + block_times(turned_above[c - 1][far], amounts[c - 1])
            if c + 1 < clusters:
                value = value + block_times(turned_below[c + 1][far], amounts[c + 1])
            found.append(value)
        return found

    row = lax.broadcasted_iota(jnp.int32, (clusters * KP, clusters * modes), 0)
    col = lax.broadcasted_iota(jnp.int32, (clusters * KP, clusters * modes), 1)
    mode = row % KP
    spread = jnp.where((mode < modes) & (col == row // KP * modes + mode), 1.0, 0.0)
    padded = jnp.dot(spread, inverse[...], precision=EXACT, preferred_element_type=F32)
    padded = lax.dot_general(
        padded, spread, (((1,), (1,)), ((), ())), precision=EXACT, preferred_element_type=F32
    )

    def solve(parts):
        value = jnp.dot(
            padded, jnp.concatenate(parts, axis=0), precision=EXACT, preferred_element_type=F32
        )
        return [value[c * KP : (c + 1) * KP] for c in range(clusters)]

    def less(left, *others):
        found = list(left)
        for other in others:
            found = [p - q for p, q in zip(found, other)]
        return found

    load_amounts = solve(load_side)
    smooth_amounts = solve(less(smooth_side, times(3, load_amounts)))
    image_amounts = solve(less(images(1), times(1, load_amounts), times(0, smooth_amounts)))
    image_side = less(images(2), times(2, load_amounts), turned_times(1, smooth_amounts))
    smooth_image_amounts = solve(less(image_side, times(3, image_amounts)))
    return load_amounts, smooth_amounts, image_amounts, smooth_image_amounts


def second_kernel(
    extent,
    softness, terms, inverse, residual, smooth, coarse, pairs_a, pairs_b,
    image_a, image_b, got_a, got_b,
    pick, operator, place,
    search, applied, change, next_a, next_b, scalars,
    amounts, first, second, third,
):
    loads, slots = residual.shape
    face = slots // 2
    half, _, size = pairs_a.shape
    clusters, _ = extent
    here = chain(*extent)

    def weighted(left, right):
        product = left * right
        near = jnp.sum(product[:, :face], axis=1, keepdims=True)
        far = jnp.sum(product[:, face:], axis=1, keepdims=True)
        return here.weights[0] * near + here.weights[1] * far

    solved = coarse_solves(clusters, loads, terms, inverse)
    for kind, parts in enumerate(solved):
        for c, part in enumerate(parts):
            amounts[kind, c] = part

    def local(kind, reached):
        return [amounts[kind, c] for c in reached]

    none = [jnp.zeros((2 * KP, loads), F32)]
    own = jnp.concatenate(local(1, here.own) + local(0, here.own), axis=0)
    image_own = jnp.concatenate(local(3, here.own) + local(2, here.own), axis=0)
    own_basis = jnp.concatenate(local(0, here.own) + none, axis=0)
    image_own_basis = jnp.concatenate(local(2, here.own) + none, axis=0)
    projected = residual[...] - dot_modes(own_basis, coarse[...])
    direction = smooth[...] - dot_modes(own, coarse[...])
    search[...] = direction
    for side, image, got in ((0, image_a, got_a), (1, image_b, got_b)):
        theirs = local(1, here.near[side]) + local(0, here.near[side])
        mixed = jnp.concatenate([own] + theirs, axis=0)
        rows = slice(loads, loads + 4 * KP)
        rows = three_rows(jnp.concatenate([image[rows, :], got[rows, :]], axis=0))
        applied[:, side * face : (side + 1) * face] = (
            image[:loads, :] + got[:loads, :] - dot_modes(mixed, rows)
        )
    image_projected = applied[...] - dot_modes(image_own_basis, coarse[...])
    for side, pairs in ((0, pairs_a), (1, pairs_b)):
        for k in range(half):
            cols = slice(side * face + k * size, side * face + (k + 1) * size)
            change[:, cols] = smooth_block(applied[:, cols], here.weights[side], pairs[k])
    changed = change[...] - dot_modes(image_own, coarse[...])
    change[...] = changed
    high, low = two_parts(changed)
    first[:loads, :] = high
    first[loads:, :] = low
    found = [
        weighted(projected, direction),
        weighted(direction, applied[...]),
        weighted(projected, changed) + weighted(image_projected, direction),
        weighted(image_projected, changed),
    ]

    second[...] = dot(first[...], pick[...]).astype(BF16)

    apply_rest(loads, softness[...], operator, place, second, third, next_a, next_b)

    for vector in (search, change):
        column = jnp.sum(vector[:, :face] * next_a[...], axis=1, keepdims=True)
        column = column + jnp.sum(vector[:, face:] * next_b[...], axis=1, keepdims=True)
        found.append(column)
    lane = lax.broadcasted_iota(jnp.int32, (loads, 128), 1)
    value = jnp.zeros(lane.shape, F32)
    for k, column in enumerate(found):
        value = jnp.where(lane == k, column, value)
    turned = value.T
    scalars[:, :loads] = turned[:4, :]
    scalars[:, loads:] = turned[4:8, :]


def last_kernel(
    extent, scalars, residual, search, applied, change, next_a, next_b, got_a, got_b, out_m, out_r
):
    loads, slots = residual.shape
    face = slots // 2
    total = jnp.sum(scalars[...], axis=0)
    total = jnp.concatenate([total[:, :loads], total[:, loads:]], axis=0)
    rho = total[0:1]
    gamma = total[1:2]
    alpha = rho / gamma
    rho_next = rho - alpha * total[2:3] + alpha * alpha * total[3:4]
    grow = 1.0 + rho_next / rho
    energy = grow * grow * gamma - 2.0 * grow * alpha * total[4:5] + alpha * alpha * total[5:6]
    alpha_next = rho_next / energy
    lengths = jnp.concatenate(
        [alpha + alpha_next * grow, alpha_next * alpha, jnp.zeros((6, rho.shape[1]), F32)], axis=0
    )
    turned = jnp.concatenate([lengths, jnp.zeros((120, rho.shape[1]), F32)], axis=0).T
    along, against = turned[:loads, 0:1], turned[:loads, 1:2]
    sides = []
    for side, own, got in ((0, next_a, got_a), (1, next_b, got_b)):
        cols = slice(side * face, (side + 1) * face)
        sides.append(
            (
                along * search[:, cols] - against * change[:, cols],
                residual[:, cols] - along * applied[:, cols] + against * (own[...] + got[...]),
            )
        )
    odd = chain(*extent).odd
    for k, out in ((0, out_m), (1, out_r)):
        out[:, 0, :] = jnp.where(odd, sides[0][k], sides[1][k])
        out[:, 1, :] = jnp.where(odd, sides[1][k], sides[0][k])


VMEM = pl.BlockSpec(memory_space=pltpu.VMEM)
HBM = pl.BlockSpec(memory_space=pltpu.HBM)


def shaped(shape, dtype=F32):
    return jax.ShapeDtypeStruct(shape, dtype)


def in_hbm(value):
    return pltpu.with_memory_space_constraint(value, pltpu.HBM)


def per_device(
    dual_load, dual_operator, index_map, stiffness, coarse_basis, dirichlet_blocks, coarse_inverse
):
    loads, _, face = dual_load.shape[2:]
    slots = 2 * face
    modes = coarse_basis.shape[2]
    block_count, size, _ = dirichlet_blocks.shape[2:]
    clusters, members = lax.axis_size("cluster"), lax.axis_size("member")
    devices = clusters * members
    extent = clusters, members
    load = dual_load.reshape(loads, 2, face)
    basis = coarse_basis.reshape(modes, 1, slots)
    blocks = dirichlet_blocks.reshape(block_count, size, size)

    evens = [(i, i + 1) for i in range(0, devices - 1, 2)]
    odds = [(i, i + 1) for i in range(1, devices - 1, 2)]
    evens = evens + [(j, i) for i, j in evens]
    odds = odds + [(j, i) for i, j in odds]

    def swap(side_a, side_b):
        from_b = lax.ppermute(side_b, AXES, odds)
        from_a = lax.ppermute(side_a, AXES, evens)
        return from_a, from_b

    def share(copies):
        parts = copies.reshape((-1,) + copies.shape[2:])
        return lax.all_to_all(parts, AXES, 0, 0, tiled=True).reshape(copies.shape)

    def params(mebibytes):
        return pltpu.CompilerParams(vmem_limit_bytes=mebibytes * 1024 * 1024)

    half_vector = shaped((loads, face))
    vector = shaped((loads, slots))
    half = block_count // 2
    packed = shaped((size // 2 + KP + loads, face))
    side_blocks = shaped((half, size, size), BF16)
    pay_a, pay_b, mine_a, mine_b = pl.pallas_call(
        functools.partial(pack_kernel, extent),
        out_shape=(packed, packed, side_blocks, side_blocks),
        in_specs=[HBM] * 3,
        out_specs=(VMEM,) * 4,
        scratch_shapes=[
            pltpu.VMEM(load.shape, F32),
            pltpu.VMEM(basis.shape, F32),
            pltpu.VMEM(blocks.shape, BF16),
            pltpu.SemaphoreType.DMA((3,)),
        ],
        compiler_params=params(8),
    )(*[in_hbm(v) for v in (load, basis, blocks)])
    got_a, got_b = swap(pay_a, pay_b)

    ordering = shaped((slots, slots), BF16)
    pick, place, operator, softness = pl.pallas_call(
        functools.partial(order_kernel, extent),
        out_shape=(ordering, ordering, ordering, shaped((1, 1))),
        in_specs=[HBM, VMEM, HBM],
        out_specs=(VMEM,) * 4,
        scratch_shapes=[pltpu.VMEM((1, slots), jnp.int32), pltpu.SemaphoreType.DMA((2,))],
        cost_estimate=pl.CostEstimate(flops=10**11, transcendentals=0, bytes_accessed=10**8),
        compiler_params=params(8),
    )(in_hbm(index_map.reshape(1, slots)), stiffness, in_hbm(dual_operator))
    pick, operator, place = [
        pltpu.with_memory_space_constraint(v, pltpu.VMEM) for v in (pick, operator, place)
    ]

    rows = loads + 4 * KP
    side_pairs = shaped((half, 2 * size, size), BF16)
    residual_a, smooth_a, coarse_a, own_basis_a, pairs_a, first_a, second_a = pl.pallas_call(
        functools.partial(near_kernel, extent, modes),
        out_shape=(
            half_vector,
            half_vector,
            shaped((12 * KP, face), BF16),
            shaped((2 * KP, face), BF16),
            side_pairs,
            shaped((2 * rows, face), BF16),
            shaped((2 * rows, slots), BF16),
        ),
        in_specs=[VMEM] * 4,
        out_specs=(VMEM,) * 7,
        compiler_params=params(8),
    )(pay_a, got_a, mine_a, pick)
    residual, smooth, coarse, pairs_b, image_a, image_b, keep = pl.pallas_call(
        functools.partial(first_kernel, extent, modes),
        out_shape=(
            vector,
            vector,
            shaped((12 * KP, slots), BF16),
            side_pairs,
            shaped((rows + KP, face)),
            shaped((rows, face)),
            shaped((2, KP, 2 * loads)),
        ),
        in_specs=[VMEM] * 13,
        out_specs=(VMEM,) * 7,
        scratch_shapes=[pltpu.VMEM((2 * KP, slots), BF16)]
        + [pltpu.VMEM((2 * rows, slots), BF16)] * 3
        + [pltpu.VMEM((4, KP, 2 * loads), F32)],
        compiler_params=params(12),
    )(
        softness, pay_b, got_b, mine_b, residual_a, smooth_a, coarse_a, own_basis_a, first_a,
        second_a, pick, operator, place,
    )

    got_a, got_b = swap(image_a, image_b)
    terms = pl.pallas_call(
        merge_kernel,
        out_shape=shaped((devices, 2 * modes // SLICE, SLICE, 2 * loads)),
        in_specs=[VMEM] * 2,
        out_specs=VMEM,
        compiler_params=params(8),
    )(keep, got_a)
    terms = pl.pallas_call(
        functools.partial(fold_kernel, clusters, members),
        out_shape=shaped((clusters * 6, 2 * modes, 2 * loads)),
        in_specs=[VMEM],
        out_specs=VMEM,
        compiler_params=params(8),
    )(share(terms))

    search, applied, change, next_a, next_b, scalars = pl.pallas_call(
        functools.partial(second_kernel, extent),
        out_shape=(vector, vector, vector, half_vector, half_vector, shaped((4, 2 * loads))),
        in_specs=[VMEM] * 15,
        out_specs=(VMEM,) * 6,
        scratch_shapes=[pltpu.VMEM((4, clusters, KP, loads), F32)]
        + [pltpu.VMEM((2 * loads, slots), BF16)] * 3,
        compiler_params=params(12),
    )(
        softness, terms, coarse_inverse, residual, smooth, coarse, pairs_a, pairs_b,
        image_a, image_b, got_a, got_b, pick, operator, place,
    )

    got_a, got_b = swap(next_a, next_b)
    scalars = share(jnp.broadcast_to(scalars[None, None], (devices, 1) + scalars.shape))
    scalars = scalars.reshape(devices, 4, 2 * loads)

    out_m, out_r = pl.pallas_call(
        functools.partial(last_kernel, extent),
        out_shape=(shaped((loads, 2, face)), shaped((loads, 2, face))),
        in_specs=[VMEM] * 9,
        out_specs=(VMEM, VMEM),
        compiler_params=params(12),
    )(scalars, residual, search, applied, change, next_a, next_b, got_a, got_b)
    return out_m.reshape(dual_load.shape), out_r.reshape(dual_load.shape)


def solution(mesh):
    in_specs = (
        P("cluster", "member", None, None, None),
        P(),
        P("cluster", "member", None),
        P("cluster", "member"),
        P("cluster", "member", None, None),
        P("cluster", "member", None, None, None),
        P(),
    )
    out_specs = (P("cluster", "member", None, None, None), P("cluster", "member", None, None, None))
    return jax.shard_map(
        per_device, mesh=mesh, in_specs=in_specs, out_specs=out_specs, check_vma=False
    )
```

```python
import functools
from typing import NamedTuple

import jax
import jax.numpy as jnp
from jax import lax
from jax.experimental import pallas as pl
from jax.experimental.pallas import tpu as pltpu
from jax.sharding import PartitionSpec as P

AXES = ("cluster", "member")
F32 = jnp.float32
BF16 = jnp.bfloat16
EXACT = lax.Precision.HIGHEST
SLICE = 4
KP = 8


def dot(left, right):
    return jnp.dot(left, right, preferred_element_type=F32)


def dot_rows(left, right):
    return lax.dot_general(left, right, (((1,), (1,)), ((), ())), preferred_element_type=F32)


def two_parts(value):
    high = value.astype(BF16)
    return high, (value - high.astype(F32)).astype(BF16)


def stacked(value):
    return jnp.concatenate(two_parts(value), axis=0)


def folded(value, rows, cols):
    value = value[:rows] + value[rows:]
    return value[:, :cols] + value[:, cols:]


def three_rows(value):
    high, low = two_parts(value)
    return jnp.concatenate([high, low, high], axis=0)


def dot_modes(amounts, rows):
    high, low = two_parts(amounts)
    left = jnp.concatenate([high, high, low], axis=0)
    return lax.dot_general(left, rows, (((0,), (0,)), ((), ())), preferred_element_type=F32)


class Chain(NamedTuple):
    odd: jax.Array
    own: tuple
    near: tuple
    weights: tuple
    same: tuple


def chain(clusters, members):
    count = clusters * members
    position = lax.axis_index("cluster") * members + lax.axis_index("member")
    parity = lax.rem(position, 2)

    def reach(pos):
        cluster, member = lax.div(pos, members), lax.rem(pos, members)
        other = cluster + jnp.where(member == members - 1, 1, jnp.where(member == 0, -1, 0))
        return cluster, jnp.clip(other, 0, clusters - 1)

    own = reach(position)
    near, weights, same = [], [], []
    for partner in (position + 1 - 2 * parity, position - 1 + 2 * parity):
        real = (partner >= 0) & (partner < count)
        there = reach(jnp.clip(partner, 0, count - 1))
        near.append(there)
        weights.append(jnp.where(real, 0.5, 1.0))
        same.append(jnp.where(real & (there[0] == own[0]), 1.0, 0.0))
    return Chain(parity == 1, own, tuple(near), tuple(weights), tuple(same))


def pack_side(first, basis, blocks, out):
    face = basis.shape[2] // 2
    modes = basis.shape[0]
    half = blocks.shape[0] // 2
    size = blocks.shape[1]
    row = lax.broadcasted_iota(jnp.int32, (size, size), 0)
    col = lax.broadcasted_iota(jnp.int32, (size, size), 1)
    mid = size // 2
    low = mid + KP
    out[mid:low, :] = jnp.zeros((KP, face), F32)
    for k in range(modes):
        mode = basis[k]
        out[mid + k : mid + k + 1, :] = jnp.where(first, mode[:, :face], mode[:, face:])
    base = jnp.where(first, 0, half)
    for pair in range(half // 2):
        one, two = blocks[base + 2 * pair], blocks[base + 2 * pair + 1]
        upper, lower = one.astype(F32), two.astype(F32)
        both = jnp.where(row <= col, upper, lower)
        left = pair * size
        right = (half // 2 + pair) * size
        out[:mid, left : left + size] = both[:mid]
        out[:mid, right : right + size] = both[mid:]
        diagonal = jnp.sum(jnp.where(row == col, lower, 0.0), axis=0, keepdims=True)
        out[mid + modes : mid + modes + 1, left : left + size] = diagonal


def pack_kernel(
    extent,
    far_load, far_basis, far_blocks,
    out_a, out_b, blocks,
    load, basis, arrived,
):
    copies = [
        pltpu.make_async_copy(source, target, arrived.at[k])
        for k, (source, target) in enumerate(
            ((far_blocks, blocks), (far_basis, basis), (far_load, load))
        )
    ]
    for copy in copies:
        copy.start()
    for copy in copies[:2]:
        copy.wait()
    odd = chain(*extent).odd
    pack_side(jnp.logical_not(odd), basis, blocks, out_b)
    pack_side(odd, basis, blocks, out_a)
    copies[2].wait()
    low = blocks.shape[1] // 2 + KP
    load_0, load_1 = load[:, 0, :], load[:, 1, :]
    out_b[low:, :] = jnp.where(odd, load_1, load_0)
    out_a[low:, :] = jnp.where(odd, load_0, load_1)


def order_kernel(
    extent,
    far_index, stiffness, far_operator,
    pick, place, operator, softness,
    index, arrived,
):
    copies = [
        pltpu.make_async_copy(far_index, index, arrived.at[0]),
        pltpu.make_async_copy(far_operator, operator, arrived.at[1]),
    ]
    for copy in copies:
        copy.start()
    slots = pick.shape[0]
    face = slots // 2
    rows = 128
    odd = chain(*extent).odd
    softness[...] = 1.0 / stiffness[...]
    copies[0].wait()
    lane = lax.broadcasted_iota(jnp.int32, (rows, slots), 1).astype(jnp.int16)
    depth = lax.broadcasted_iota(jnp.int32, (rows, slots), 0).astype(jnp.int16)
    one, zero = jnp.ones((), BF16), jnp.zeros((), BF16)
    index_0, index_1 = index[:, :face], index[:, face:]
    wanted = jnp.concatenate(
        [jnp.where(odd, index_0, index_1), jnp.where(odd, index_1, index_0)], axis=1
    )
    every = jnp.broadcast_to(wanted, (rows, slots)).astype(jnp.int16)
    for start in range(0, slots, rows):
        here = jnp.broadcast_to(wanted[:, start : start + rows].astype(F32), (rows, rows)).T
        here = here.astype(jnp.int32).astype(jnp.int16)
        target = jnp.concatenate([here] * (slots // rows), axis=1)
        pick[start : start + rows, :] = jnp.where(target == lane, one, zero)
        place[start : start + rows, :] = jnp.where(every - jnp.int16(start) == depth, one, zero)
    copies[1].wait()


def merge_kernel(keep, got, out):
    kinds, depth, lanes = keep.shape
    rows = got.shape[0] - depth
    modes = out.shape[1] * SLICE // kinds
    values = [keep[k] + got[rows:, k * lanes : (k + 1) * lanes] for k in range(kinds)]
    value = jnp.concatenate([v[:modes] for v in values], axis=0)
    for part in range(out.shape[1]):
        piece = value[part * SLICE : (part + 1) * SLICE]
        out[:, part] = jnp.broadcast_to(piece[None], (out.shape[0],) + piece.shape)


def fold_kernel(clusters, members, terms, out):
    for c in range(clusters):
        for parity in range(2):
            for part in range(terms.shape[1]):
                begin = terms[c * members + parity, part]
                end = terms[(c + 1) * members - 2 + parity, part]
                value = begin
                for m in range(2, members, 2):
                    value = value + terms[c * members + m + parity, part]
                for k, result in enumerate((value, begin, end)):
                    out[(c * 2 + parity) * 3 + k, part * SLICE : (part + 1) * SLICE] = result


def apply_rest(rows, scale, operator, place, second, third, image_a, image_b):
    slots = second.shape[1]
    face = slots // 2

    product = dot(second[...], operator[...])
    high, low = two_parts(product[:rows] + product[rows:])
    third[:rows, :] = high
    third[rows:, :] = low

    product = dot(third[...], place[...])
    product = scale * (product[:rows] + product[rows:])
    image_a[:rows, :] = product[:, :face]
    image_b[:rows, :] = product[:, face:]


def smooth_block(value, weight, block_pair):
    rows = value.shape[0]
    high, low = two_parts(weight * value)
    left = jnp.concatenate(
        [jnp.concatenate([high, high], axis=1), jnp.concatenate([low, low], axis=1)], axis=0
    )
    product = dot(left, block_pair)
    return weight * (product[:rows] + product[rows:])


def side_part(
    modes, at, weight, same, base, pay, got, blocks, residual, smooth, coarse, own_basis, pairs, first
):
    half, size = blocks.shape[0] // 2, blocks.shape[1]
    face = half * size
    loads = pay.shape[0] - size // 2 - KP
    rows = loads + 4 * KP
    mid = size // 2
    low = mid + KP
    cols = slice(at, at + face)
    row = lax.broadcasted_iota(jnp.int32, (size, size), 0)
    col = lax.broadcasted_iota(jnp.int32, (size, size), 1)
    real = lax.broadcasted_iota(jnp.int32, (KP, face), 0) < modes
    mine = jnp.where(real, pay[mid:low, :], 0.0)
    theirs = jnp.where(real, got[mid:low, :], 0.0)
    own_basis[:, cols] = stacked(mine)
    span = jnp.concatenate([mine + same * theirs, (1.0 - same) * theirs], axis=0)
    for pair in range(half // 2):
        left = pair * size
        right = (half // 2 + pair) * size
        both = jnp.concatenate(
            [got[:mid, left : left + size], got[:mid, right : right + size]], axis=0
        )
        turned = both.T
        diagonal = got[mid + modes : mid + modes + 1, left : left + size]
        upper = jnp.where(row <= col, both, turned)
        lower = jnp.where(row > col, both, jnp.where(row < col, turned, diagonal))
        for k, theirs_block in ((2 * pair, upper), (2 * pair + 1, lower)):
            block_pair = jnp.concatenate([blocks[base + k], theirs_block.astype(BF16)], axis=0)
            pairs[k] = block_pair
            there = slice(k * size, (k + 1) * size)
            cols = slice(at + k * size, at + (k + 1) * size)
            value = pay[low:, there] + got[low:, there]
            modes_here = span[:, there]
            result = smooth_block(
                jnp.concatenate([value, modes_here], axis=0), weight, block_pair
            )
            residual[:, cols] = value
            smooth[:, cols] = result[:loads]
            high, low_part = two_parts(
                jnp.concatenate([result[:loads], modes_here, result[loads:]], axis=0)
            )
            first[:rows, cols] = high
            first[rows:, cols] = low_part
            coarse[: 4 * KP, cols] = high[loads:]
            coarse[4 * KP : 8 * KP, cols] = low_part[loads:]
            coarse[8 * KP :, cols] = high[loads:]


def near_kernel(
    extent, modes,
    pay, got, blocks, pick,
    residual, smooth, coarse, own_basis, pairs, first, second,
):
    here = chain(*extent)
    base = jnp.where(here.odd, 0, blocks.shape[0] // 2)
    side_part(
        modes, 0, here.weights[0], here.same[0], base, pay, got, blocks,
        residual, smooth, coarse, own_basis, pairs, first,
    )
    face = first.shape[1]

    second[...] = dot(first[...], pick[:face, :]).astype(BF16)


def first_kernel(
    extent, modes,
    softness, pay, got, blocks,
    residual_a, smooth_a, coarse_a, own_basis_a, first_a, second_a,
    pick, operator, place,
    residual, smooth, coarse, pairs, image_a, image_b, keep,
    own_basis, first, second, third, terms,
):
    loads, slots = residual.shape
    face = slots // 2
    rows = loads + 4 * KP
    here = chain(*extent)
    base = jnp.where(here.odd, blocks.shape[0] // 2, 0)
    side_part(
        modes, face, here.weights[1], here.same[1], base, pay, got, blocks,
        residual, smooth, coarse, own_basis, pairs, first,
    )

    product = dot(first[:, face:], pick[face:, :]) + second_a[...].astype(F32)
    second[...] = product.astype(BF16)

    for whole, part in (
        (residual, residual_a), (smooth, smooth_a), (coarse, coarse_a),
        (own_basis, own_basis_a), (first, first_a),
    ):
        whole[:, :face] = part[...]
    apply_rest(rows, softness[...], operator, place, second, third, image_a, image_b)

    vectors = jnp.concatenate([stacked(residual[...]), first[...]], axis=0)
    sides = dot_rows(own_basis[...], vectors)
    load_side = folded(sides[:, : 2 * loads], KP, loads)
    smooth_side = folded(sides[:, 2 * loads :], KP, rows)
    shared = smooth_side[:, loads + 2 * KP :]
    energy = jnp.zeros((8 * KP, 2 * rows), F32)
    for side, image in ((0, image_a), (1, image_b)):
        cols = slice(side * face, (side + 1) * face)
        energy = energy + dot_rows(coarse[: 8 * KP, cols], stacked(image[:rows, :]))
    energy = folded(energy, 4 * KP, rows)
    terms[0, :, :loads] = load_side
    terms[0, :, loads:] = smooth_side[:, :loads]
    terms[1, :, :loads] = energy[:KP, :loads]
    terms[1, :, loads:] = energy[KP : 2 * KP, :loads]
    terms[2, :, :loads] = energy[2 * KP : 3 * KP, :loads]
    terms[2, :, loads:] = energy[3 * KP :, :loads]
    for i in range(2):
        for j in range(2):
            at = (2 * i + j) * 4 * KP
            basis_rows = energy[i * KP : (i + 1) * KP]
            smooth_rows = energy[(2 + i) * KP : (3 + i) * KP]
            basis_cols = slice(loads + j * KP, loads + (j + 1) * KP)
            smooth_cols = slice(loads + (2 + j) * KP, loads + (3 + j) * KP)
            terms[3, :, at : at + KP] = basis_rows[:, basis_cols]
            terms[3, :, at + KP : at + 2 * KP] = basis_rows[:, smooth_cols]
            terms[3, :, at + 2 * KP : at + 3 * KP] = smooth_rows[:, smooth_cols]
            last = shared[:, j * KP : (j + 1) * KP] if i == 0 else jnp.zeros((KP, KP), F32)
            terms[3, :, at + 3 * KP : at + 4 * KP] = last
    keep[...] = jnp.where(here.odd, terms[2:], terms[:2])
    image_a[rows:, :] = jnp.zeros((KP, face), F32)
    for kind in range(2):
        image_a[rows:, kind * 2 * loads : (kind + 1) * 2 * loads] = jnp.where(
            here.odd, terms[kind], terms[2 + kind]
        )


def coarse_solves(clusters, loads, terms, inverse):
    modes = inverse.shape[0] // clusters

    def one_kind(c, kind, which):
        value = terms[(c * 2 + kind // 2) * 3 + which]
        value = value[kind % 2 * modes : (kind % 2 + 1) * modes]
        return jnp.concatenate([value, jnp.zeros((KP - modes, value.shape[1]), F32)], axis=0)

    def total(c, kind):
        return one_kind(c, kind, 0)

    def begin(c, kind):
        return one_kind(c, kind, 1)

    def end(c, kind):
        return one_kind(c, kind, 2)

    span = 4 * KP
    lanes = terms.shape[-1]
    totals = [total(c, 0) for c in range(clusters)]
    load_side = [v[:, :loads] for v in totals]
    smooth_side = [v[:, loads:] for v in totals]

    def images(kind):
        found = []
        for c in range(clusters):
            value = total(c, kind)[:, :loads]
            if c + 1 < clusters:
                value = value + begin(c + 1, kind)[:, loads:]
            if c > 0:
                value = value + end(c - 1, kind)[:, loads:]
            found.append(value)
        return found

    centre, below, above = [], [], []
    for c in range(clusters):
        value, under, over = total(c, 3), begin(c, 3), end(c, 3)
        if c + 1 < clusters:
            value = value + pltpu.roll(begin(c + 1, 3), lanes - 3 * span, 1)
            over = over + pltpu.roll(begin(c + 1, 3), lanes - span, 1)
        if c > 0:
            value = value + pltpu.roll(end(c - 1, 3), lanes - 3 * span, 1)
            under = under + pltpu.roll(end(c - 1, 3), lanes - span, 1)
        centre.append(value)
        below.append(under)
        above.append(over)

    def block_times(block, amounts):
        value = block[:, 0:1] * amounts[0:1]
        for k in range(1, KP):
            value = value + block[:, k : k + 1] * amounts[k : k + 1]
        return value

    def times(kind, amounts):
        found = []
        for c in range(clusters):
            near, far = slice(kind * KP, (kind + 1) * KP), slice(span + kind * KP, span + (kind + 1) * KP)
            value = block_times(centre[c][:, near], amounts[c])
            if c > 0:
                value = value + block_times(below[c][:, far], amounts[c - 1])
            if c + 1 < clusters:
                value = value + block_times(above[c][:, far], amounts[c + 1])
            found.append(value)
        return found

    turned_centre = [v.T for v in centre]
    turned_below = [v.T for v in below]
    turned_above = [v.T for v in above]

    def turned_times(kind, amounts):
        found = []
        near, far = slice(kind * KP, (kind + 1) * KP), slice(span + kind * KP, span + (kind + 1) * KP)
        for c in range(clusters):
            value = block_times(turned_centre[c][near], amounts[c])
            if c > 0:
                value = value + block_times(turned_above[c - 1][far], amounts[c - 1])
            if c + 1 < clusters:
                value = value + block_times(turned_below[c + 1][far], amounts[c + 1])
            found.append(value)
        return found

    row = lax.broadcasted_iota(jnp.int32, (clusters * KP, clusters * modes), 0)
    col = lax.broadcasted_iota(jnp.int32, (clusters * KP, clusters * modes), 1)
    mode = row % KP
    spread = jnp.where((mode < modes) & (col == row // KP * modes + mode), 1.0, 0.0)
    padded = jnp.dot(spread, inverse[...], precision=EXACT, preferred_element_type=F32)
    padded = lax.dot_general(
        padded, spread, (((1,), (1,)), ((), ())), precision=EXACT, preferred_element_type=F32
    )

    def solve(parts):
        value = jnp.dot(
            padded, jnp.concatenate(parts, axis=0), precision=EXACT, preferred_element_type=F32
        )
        return [value[c * KP : (c + 1) * KP] for c in range(clusters)]

    def less(left, *others):
        found = list(left)
        for other in others:
            found = [p - q for p, q in zip(found, other)]
        return found

    load_amounts = solve(load_side)
    smooth_amounts = solve(less(smooth_side, times(3, load_amounts)))
    image_amounts = solve(less(images(1), times(1, load_amounts), times(0, smooth_amounts)))
    image_side = less(images(2), times(2, load_amounts), turned_times(1, smooth_amounts))
    smooth_image_amounts = solve(less(image_side, times(3, image_amounts)))
    return load_amounts, smooth_amounts, image_amounts, smooth_image_amounts


def second_kernel(
    extent,
    softness, terms, inverse, residual, smooth, coarse, pairs_a, pairs_b,
    image_a, image_b, got_a, got_b,
    pick, operator, place,
    search, applied, change, next_a, next_b, scalars,
    amounts, first, second, third,
):
    loads, slots = residual.shape
    face = slots // 2
    half, _, size = pairs_a.shape
    clusters, _ = extent
    here = chain(*extent)

    def weighted(left, right):
        product = left * right
        near = jnp.sum(product[:, :face], axis=1, keepdims=True)
        far = jnp.sum(product[:, face:], axis=1, keepdims=True)
        return here.weights[0] * near + here.weights[1] * far

    solved = coarse_solves(clusters, loads, terms, inverse)
    for kind, parts in enumerate(solved):
        for c, part in enumerate(parts):
            amounts[kind, c] = part

    def local(kind, reached):
        return [amounts[kind, c] for c in reached]

    none = [jnp.zeros((2 * KP, loads), F32)]
    own = jnp.concatenate(local(1, here.own) + local(0, here.own), axis=0)
    image_own = jnp.concatenate(local(3, here.own) + local(2, here.own), axis=0)
    own_basis = jnp.concatenate(local(0, here.own) + none, axis=0)
    image_own_basis = jnp.concatenate(local(2, here.own) + none, axis=0)
    projected = residual[...] - dot_modes(own_basis, coarse[...])
    direction = smooth[...] - dot_modes(own, coarse[...])
    search[...] = direction
    for side, image, got in ((0, image_a, got_a), (1, image_b, got_b)):
        theirs = local(1, here.near[side]) + local(0, here.near[side])
        mixed = jnp.concatenate([own] + theirs, axis=0)
        rows = slice(loads, loads + 4 * KP)
        rows = three_rows(jnp.concatenate([image[rows, :], got[rows, :]], axis=0))
        applied[:, side * face : (side + 1) * face] = (
            image[:loads, :] + got[:loads, :] - dot_modes(mixed, rows)
        )
    image_projected = applied[...] - dot_modes(image_own_basis, coarse[...])
    for side, pairs in ((0, pairs_a), (1, pairs_b)):
        for k in range(half):
            cols = slice(side * face + k * size, side * face + (k + 1) * size)
            change[:, cols] = smooth_block(applied[:, cols], here.weights[side], pairs[k])
    changed = change[...] - dot_modes(image_own, coarse[...])
    change[...] = changed
    high, low = two_parts(changed)
    first[:loads, :] = high
    first[loads:, :] = low
    found = [
        weighted(projected, direction),
        weighted(direction, applied[...]),
        weighted(projected, changed) + weighted(image_projected, direction),
        weighted(image_projected, changed),
    ]

    second[...] = dot(first[...], pick[...]).astype(BF16)

    apply_rest(loads, softness[...], operator, place, second, third, next_a, next_b)

    for vector in (search, change):
        column = jnp.sum(vector[:, :face] * next_a[...], axis=1, keepdims=True)
        column = column + jnp.sum(vector[:, face:] * next_b[...], axis=1, keepdims=True)
        found.append(column)
    lane = lax.broadcasted_iota(jnp.int32, (loads, 128), 1)
    value = jnp.zeros(lane.shape, F32)
    for k, column in enumerate(found):
        value = jnp.where(lane == k, column, value)
    turned = value.T
    scalars[:, :loads] = turned[:4, :]
    scalars[:, loads:] = turned[4:8, :]


def last_kernel(
    extent, scalars, residual, search, applied, change, next_a, next_b, got_a, got_b, out_m, out_r
):
    loads, slots = residual.shape
    face = slots // 2
    total = jnp.sum(scalars[...], axis=0)
    total = jnp.concatenate([total[:, :loads], total[:, loads:]], axis=0)
    rho = total[0:1]
    gamma = total[1:2]
    alpha = rho / gamma
    rho_next = rho - alpha * total[2:3] + alpha * alpha * total[3:4]
    grow = 1.0 + rho_next / rho
    energy = grow * grow * gamma - 2.0 * grow * alpha * total[4:5] + alpha * alpha * total[5:6]
    alpha_next = rho_next / energy
    lengths = jnp.concatenate(
        [alpha + alpha_next * grow, alpha_next * alpha, jnp.zeros((6, rho.shape[1]), F32)], axis=0
    )
    turned = jnp.concatenate([lengths, jnp.zeros((120, rho.shape[1]), F32)], axis=0).T
    along, against = turned[:loads, 0:1], turned[:loads, 1:2]
    sides = []
    for side, own, got in ((0, next_a, got_a), (1, next_b, got_b)):
        cols = slice(side * face, (side + 1) * face)
        sides.append(
            (
                along * search[:, cols] - against * change[:, cols],
                residual[:, cols] - along * applied[:, cols] + against * (own[...] + got[...]),
            )
        )
    odd = chain(*extent).odd
    for k, out in ((0, out_m), (1, out_r)):
        out[:, 0, :] = jnp.where(odd, sides[0][k], sides[1][k])
        out[:, 1, :] = jnp.where(odd, sides[1][k], sides[0][k])


VMEM = pl.BlockSpec(memory_space=pltpu.VMEM)
HBM = pl.BlockSpec(memory_space=pltpu.HBM)


def shaped(shape, dtype=F32):
    return jax.ShapeDtypeStruct(shape, dtype)


def in_hbm(value):
    return pltpu.with_memory_space_constraint(value, pltpu.HBM)


def per_device(
    dual_load, dual_operator, index_map, stiffness, coarse_basis, dirichlet_blocks, coarse_inverse
):
    loads, _, face = dual_load.shape[2:]
    slots = 2 * face
    modes = coarse_basis.shape[2]
    block_count, size, _ = dirichlet_blocks.shape[2:]
    clusters, members = lax.axis_size("cluster"), lax.axis_size("member")
    devices = clusters * members
    extent = clusters, members
    load = dual_load.reshape(loads, 2, face)
    basis = coarse_basis.reshape(modes, 1, slots)
    blocks = dirichlet_blocks.reshape(block_count, size, size)

    evens = [(i, i + 1) for i in range(0, devices - 1, 2)]
    odds = [(i, i + 1) for i in range(1, devices - 1, 2)]
    evens = evens + [(j, i) for i, j in evens]
    odds = odds + [(j, i) for i, j in odds]

    def swap(side_a, side_b):
        from_b = lax.ppermute(side_b, AXES, odds)
        from_a = lax.ppermute(side_a, AXES, evens)
        return from_a, from_b

    def share(copies):
        parts = copies.reshape((-1,) + copies.shape[2:])
        return lax.all_to_all(parts, AXES, 0, 0, tiled=True).reshape(copies.shape)

    def params(mebibytes):
        return pltpu.CompilerParams(vmem_limit_bytes=mebibytes * 1024 * 1024)

    half_vector = shaped((loads, face))
    vector = shaped((loads, slots))
    half = block_count // 2
    packed = shaped((size // 2 + KP + loads, face))
    pay_a, pay_b, own_blocks = pl.pallas_call(
        functools.partial(pack_kernel, extent),
        out_shape=(packed, packed, shaped(blocks.shape, BF16)),
        in_specs=[HBM] * 3,
        out_specs=(VMEM,) * 3,
        scratch_shapes=[
            pltpu.VMEM(load.shape, F32),
            pltpu.VMEM(basis.shape, F32),
            pltpu.SemaphoreType.DMA((3,)),
        ],
        compiler_params=params(8),
    )(*[in_hbm(v) for v in (load, basis, blocks)])
    got_a, got_b = swap(pay_a, pay_b)

    ordering = shaped((slots, slots), BF16)
    pick, place, operator, softness = pl.pallas_call(
        functools.partial(order_kernel, extent),
        out_shape=(ordering, ordering, ordering, shaped((1, 1))),
        in_specs=[HBM, VMEM, HBM],
        out_specs=(VMEM,) * 4,
        scratch_shapes=[pltpu.VMEM((1, slots), jnp.int32), pltpu.SemaphoreType.DMA((2,))],
        cost_estimate=pl.CostEstimate(flops=10**11, transcendentals=0, bytes_accessed=10**8),
        compiler_params=params(8),
    )(in_hbm(index_map.reshape(1, slots)), stiffness, in_hbm(dual_operator))
    pick, operator, place = [
        pltpu.with_memory_space_constraint(v, pltpu.VMEM) for v in (pick, operator, place)
    ]

    rows = loads + 4 * KP
    side_pairs = shaped((half, 2 * size, size), BF16)
    residual_a, smooth_a, coarse_a, own_basis_a, pairs_a, first_a, second_a = pl.pallas_call(
        functools.partial(near_kernel, extent, modes),
        out_shape=(
            half_vector,
            half_vector,
            shaped((12 * KP, face), BF16),
            shaped((2 * KP, face), BF16),
            side_pairs,
            shaped((2 * rows, face), BF16),
            shaped((2 * rows, slots), BF16),
        ),
        in_specs=[VMEM] * 4,
        out_specs=(VMEM,) * 7,
        compiler_params=params(8),
    )(pay_a, got_a, own_blocks, pick)
    residual, smooth, coarse, pairs_b, image_a, image_b, keep = pl.pallas_call(
        functools.partial(first_kernel, extent, modes),
        out_shape=(
            vector,
            vector,
            shaped((12 * KP, slots), BF16),
            side_pairs,
            shaped((rows + KP, face)),
            shaped((rows, face)),
            shaped((2, KP, 2 * loads)),
        ),
        in_specs=[VMEM] * 13,
        out_specs=(VMEM,) * 7,
        scratch_shapes=[pltpu.VMEM((2 * KP, slots), BF16)]
        + [pltpu.VMEM((2 * rows, slots), BF16)] * 3
        + [pltpu.VMEM((4, KP, 2 * loads), F32)],
        compiler_params=params(12),
    )(
        softness, pay_b, got_b, own_blocks, residual_a, smooth_a, coarse_a, own_basis_a, first_a,
        second_a, pick, operator, place,
    )

    got_a, got_b = swap(image_a, image_b)
    terms = pl.pallas_call(
        merge_kernel,
        out_shape=shaped((devices, 2 * modes // SLICE, SLICE, 2 * loads)),
        in_specs=[VMEM] * 2,
        out_specs=VMEM,
        compiler_params=params(8),
    )(keep, got_a)
    terms = pl.pallas_call(
        functools.partial(fold_kernel, clusters, members),
        out_shape=shaped((clusters * 6, 2 * modes, 2 * loads)),
        in_specs=[VMEM],
        out_specs=VMEM,
        compiler_params=params(8),
    )(share(terms))

    search, applied, change, next_a, next_b, scalars = pl.pallas_call(
        functools.partial(second_kernel, extent),
        out_shape=(vector, vector, vector, half_vector, half_vector, shaped((4, 2 * loads))),
        in_specs=[VMEM] * 15,
        out_specs=(VMEM,) * 6,
        scratch_shapes=[pltpu.VMEM((4, clusters, KP, loads), F32)]
        + [pltpu.VMEM((2 * loads, slots), BF16)] * 3,
        compiler_params=params(12),
    )(
        softness, terms, coarse_inverse, residual, smooth, coarse, pairs_a, pairs_b,
        image_a, image_b, got_a, got_b, pick, operator, place,
    )

    got_a, got_b = swap(next_a, next_b)
    scalars = share(jnp.broadcast_to(scalars[None, None], (devices, 1) + scalars.shape))
    scalars = scalars.reshape(devices, 4, 2 * loads)

    out_m, out_r = pl.pallas_call(
        functools.partial(last_kernel, extent),
        out_shape=(shaped((loads, 2, face)), shaped((loads, 2, face))),
        in_specs=[VMEM] * 9,
        out_specs=(VMEM, VMEM),
        compiler_params=params(12),
    )(scalars, residual, search, applied, change, next_a, next_b, got_a, got_b)
    return out_m.reshape(dual_load.shape), out_r.reshape(dual_load.shape)


def solution(mesh):
    in_specs = (
        P("cluster", "member", None, None, None),
        P(),
        P("cluster", "member", None),
        P("cluster", "member"),
        P("cluster", "member", None, None),
        P("cluster", "member", None, None, None),
        P(),
    )
    out_specs = (P("cluster", "member", None, None, None), P("cluster", "member", None, None, None))
    return jax.shard_map(
        per_device, mesh=mesh, in_specs=in_specs, out_specs=out_specs, check_vma=False
    )
```

```python
import functools
from typing import NamedTuple

import jax
import jax.numpy as jnp
from jax import lax
from jax.experimental import pallas as pl
from jax.experimental.pallas import tpu as pltpu
from jax.sharding import PartitionSpec as P

AXES = ("cluster", "member")
F32 = jnp.float32
BF16 = jnp.bfloat16
EXACT = lax.Precision.HIGHEST
SLICE = 4
KP = 8


def dot(left, right):
    return jnp.dot(left, right, preferred_element_type=F32)


def dot_rows(left, right):
    return lax.dot_general(left, right, (((1,), (1,)), ((), ())), preferred_element_type=F32)


def two_parts(value):
    high = value.astype(BF16)
    return high, (value - high.astype(F32)).astype(BF16)


def stacked(value):
    return jnp.concatenate(two_parts(value), axis=0)


def folded(value, rows, cols):
    value = value[:rows] + value[rows:]
    return value[:, :cols] + value[:, cols:]


def three_rows(value):
    high, low = two_parts(value)
    return jnp.concatenate([high, low, high], axis=0)


def dot_modes(amounts, rows):
    high, low = two_parts(amounts)
    left = jnp.concatenate([high, high, low], axis=0)
    return lax.dot_general(left, rows, (((0,), (0,)), ((), ())), preferred_element_type=F32)


class Chain(NamedTuple):
    odd: jax.Array
    own: tuple
    near: tuple
    weights: tuple
    same: tuple


def chain(clusters, members):
    count = clusters * members
    position = lax.axis_index("cluster") * members + lax.axis_index("member")
    parity = lax.rem(position, 2)

    def reach(pos):
        cluster, member = lax.div(pos, members), lax.rem(pos, members)
        other = cluster + jnp.where(member == members - 1, 1, jnp.where(member == 0, -1, 0))
        return cluster, jnp.clip(other, 0, clusters - 1)

    own = reach(position)
    near, weights, same = [], [], []
    for partner in (position + 1 - 2 * parity, position - 1 + 2 * parity):
        real = (partner >= 0) & (partner < count)
        there = reach(jnp.clip(partner, 0, count - 1))
        near.append(there)
        weights.append(jnp.where(real, 0.5, 1.0))
        same.append(jnp.where(real & (there[0] == own[0]), 1.0, 0.0))
    return Chain(parity == 1, own, tuple(near), tuple(weights), tuple(same))


def pack_side(first, basis, blocks, out):
    face = basis.shape[2] // 2
    modes = basis.shape[0]
    half = blocks.shape[0] // 2
    size = blocks.shape[1]
    row = lax.broadcasted_iota(jnp.int32, (size, size), 0)
    col = lax.broadcasted_iota(jnp.int32, (size, size), 1)
    mid = size // 2
    low = mid + KP
    out[mid:low, :] = jnp.zeros((KP, face), F32)
    for k in range(modes):
        mode = basis[k]
        out[mid + k : mid + k + 1, :] = jnp.where(first, mode[:, :face], mode[:, face:])
    base = jnp.where(first, 0, half)
    for pair in range(half // 2):
        one, two = blocks[base + 2 * pair], blocks[base + 2 * pair + 1]
        upper, lower = one.astype(F32), two.astype(F32)
        both = jnp.where(row <= col, upper, lower)
        left = pair * size
        right = (half // 2 + pair) * size
        out[:mid, left : left + size] = both[:mid]
        out[:mid, right : right + size] = both[mid:]
        diagonal = jnp.sum(jnp.where(row == col, lower, 0.0), axis=0, keepdims=True)
        out[mid + modes : mid + modes + 1, left : left + size] = diagonal


def pack_kernel(
    extent,
    far_load, far_basis, far_blocks,
    out_a, out_b, blocks,
    load, basis, arrived,
):
    copies = [
        pltpu.make_async_copy(source, target, arrived.at[k])
        for k, (source, target) in enumerate(
            ((far_blocks, blocks), (far_basis, basis), (far_load, load))
        )
    ]
    for copy in copies:
        copy.start()
    for copy in copies[:2]:
        copy.wait()
    odd = chain(*extent).odd
    pack_side(jnp.logical_not(odd), basis, blocks, out_b)
    pack_side(odd, basis, blocks, out_a)
    copies[2].wait()
    low = blocks.shape[1] // 2 + KP
    load_0, load_1 = load[:, 0, :], load[:, 1, :]
    out_b[low:, :] = jnp.where(odd, load_1, load_0)
    out_a[low:, :] = jnp.where(odd, load_0, load_1)


def order_kernel(
    extent,
    far_index, stiffness, far_operator,
    pick, place, operator, softness,
    index, arrived,
):
    copies = [
        pltpu.make_async_copy(far_index, index, arrived.at[0]),
        pltpu.make_async_copy(far_operator, operator, arrived.at[1]),
    ]
    for copy in copies:
        copy.start()
    slots = pick.shape[0]
    face = slots // 2
    rows = 128
    odd = chain(*extent).odd
    softness[...] = 1.0 / stiffness[...]
    copies[0].wait()
    lane = lax.broadcasted_iota(jnp.int32, (rows, slots), 1).astype(jnp.int16)
    depth = lax.broadcasted_iota(jnp.int32, (rows, slots), 0).astype(jnp.int16)
    one, zero = jnp.ones((), BF16), jnp.zeros((), BF16)
    index_0, index_1 = index[:, :face], index[:, face:]
    wanted = jnp.concatenate(
        [jnp.where(odd, index_0, index_1), jnp.where(odd, index_1, index_0)], axis=1
    )
    every = jnp.broadcast_to(wanted, (rows, slots)).astype(jnp.int16)
    for start in range(0, slots, rows):
        here = jnp.broadcast_to(wanted[:, start : start + rows].astype(F32), (rows, rows)).T
        here = here.astype(jnp.int32).astype(jnp.int16)
        target = jnp.concatenate([here] * (slots // rows), axis=1)
        pick[start : start + rows, :] = jnp.where(target == lane, one, zero)
        place[start : start + rows, :] = jnp.where(every - jnp.int16(start) == depth, one, zero)
    copies[1].wait()


def merge_kernel(keep, got, out):
    kinds, depth, lanes = keep.shape
    rows = got.shape[0] - depth
    modes = out.shape[1] * SLICE // kinds
    values = [keep[k] + got[rows:, k * lanes : (k + 1) * lanes] for k in range(kinds)]
    value = jnp.concatenate([v[:modes] for v in values], axis=0)
    for part in range(out.shape[1]):
        piece = value[part * SLICE : (part + 1) * SLICE]
        out[:, part] = jnp.broadcast_to(piece[None], (out.shape[0],) + piece.shape)


def fold_kernel(clusters, members, terms, out):
    for c in range(clusters):
        for parity in range(2):
            for part in range(terms.shape[1]):
                begin = terms[c * members + parity, part]
                end = terms[(c + 1) * members - 2 + parity, part]
                value = begin
                for m in range(2, members, 2):
                    value = value + terms[c * members + m + parity, part]
                for k, result in enumerate((value, begin, end)):
                    out[(c * 2 + parity) * 3 + k, part * SLICE : (part + 1) * SLICE] = result


def apply_rest(rows, scale, operator, place, second, third, image_a, image_b):
    slots = second.shape[1]
    face = slots // 2

    product = dot(second[...], operator[...])
    high, low = two_parts(product[:rows] + product[rows:])
    third[:rows, :] = high
    third[rows:, :] = low

    product = dot(third[...], place[...])
    product = scale * (product[:rows] + product[rows:])
    image_a[:rows, :] = product[:, :face]
    image_b[:rows, :] = product[:, face:]
    return product


def smooth_block(value, weight, block_pair):
    rows = value.shape[0]
    high, low = two_parts(weight * value)
    left = jnp.concatenate(
        [jnp.concatenate([high, high], axis=1), jnp.concatenate([low, low], axis=1)], axis=0
    )
    product = dot(left, block_pair)
    return weight * (product[:rows] + product[rows:])


def side_part(
    modes, at, weight, same, base, pay, got, blocks, residual, smooth, coarse, own_basis, pairs, first
):
    half, size = blocks.shape[0] // 2, blocks.shape[1]
    face = half * size
    loads = pay.shape[0] - size // 2 - KP
    rows = loads + 4 * KP
    mid = size // 2
    low = mid + KP
    cols = slice(at, at + face)
    row = lax.broadcasted_iota(jnp.int32, (size, size), 0)
    col = lax.broadcasted_iota(jnp.int32, (size, size), 1)
    real = lax.broadcasted_iota(jnp.int32, (KP, face), 0) < modes
    mine = jnp.where(real, pay[mid:low, :], 0.0)
    theirs = jnp.where(real, got[mid:low, :], 0.0)
    own_basis[:, cols] = stacked(mine)
    span = jnp.concatenate([mine + same * theirs, (1.0 - same) * theirs], axis=0)
    for pair in range(half // 2):
        left = pair * size
        right = (half // 2 + pair) * size
        both = jnp.concatenate(
            [got[:mid, left : left + size], got[:mid, right : right + size]], axis=0
        )
        turned = both.T
        diagonal = got[mid + modes : mid + modes + 1, left : left + size]
        upper = jnp.where(row <= col, both, turned)
        lower = jnp.where(row > col, both, jnp.where(row < col, turned, diagonal))
        for k, theirs_block in ((2 * pair, upper), (2 * pair + 1, lower)):
            block_pair = jnp.concatenate([blocks[base + k], theirs_block.astype(BF16)], axis=0)
            pairs[k] = block_pair
            there = slice(k * size, (k + 1) * size)
            cols = slice(at + k * size, at + (k + 1) * size)
            value = pay[low:, there] + got[low:, there]
            modes_here = span[:, there]
            result = smooth_block(
                jnp.concatenate([value, modes_here], axis=0), weight, block_pair
            )
            residual[:, cols] = value
            smooth[:, cols] = result[:loads]
            high, low_part = two_parts(
                jnp.concatenate([result[:loads], modes_here, result[loads:]], axis=0)
            )
            first[:rows, cols] = high
            first[rows:, cols] = low_part
            coarse[: 4 * KP, cols] = high[loads:]
            coarse[4 * KP : 8 * KP, cols] = low_part[loads:]
            coarse[8 * KP :, cols] = high[loads:]


def near_kernel(
    extent, modes,
    pay, got, blocks, pick,
    residual, smooth, coarse, own_basis, pairs, first, second,
):
    here = chain(*extent)
    base = jnp.where(here.odd, 0, blocks.shape[0] // 2)
    side_part(
        modes, 0, here.weights[0], here.same[0], base, pay, got, blocks,
        residual, smooth, coarse, own_basis, pairs, first,
    )
    face = first.shape[1]

    second[...] = dot(first[...], pick[:face, :]).astype(BF16)


def first_kernel(
    extent, modes,
    softness, pay, got, blocks,
    residual_a, smooth_a, coarse_a, own_basis_a, first_a, second_a,
    pick, operator, place,
    residual, smooth, coarse, pairs, image_a, image_b, keep,
    own_basis, first, second, third, terms,
):
    loads, slots = residual.shape
    face = slots // 2
    rows = loads + 4 * KP
    here = chain(*extent)
    base = jnp.where(here.odd, blocks.shape[0] // 2, 0)
    side_part(
        modes, face, here.weights[1], here.same[1], base, pay, got, blocks,
        residual, smooth, coarse, own_basis, pairs, first,
    )

    product = dot(first[:, face:], pick[face:, :]) + second_a[...].astype(F32)
    second[...] = product.astype(BF16)

    for whole, part in (
        (residual, residual_a), (smooth, smooth_a), (coarse, coarse_a),
        (own_basis, own_basis_a), (first, first_a),
    ):
        whole[:, :face] = part[...]
    images = apply_rest(
        rows, softness[...], operator, place, second, third, image_a, image_b
    )

    vectors = jnp.concatenate([stacked(residual[...]), first[...]], axis=0)
    sides = dot_rows(own_basis[...], vectors)
    load_side = folded(sides[:, : 2 * loads], KP, loads)
    smooth_side = folded(sides[:, 2 * loads :], KP, rows)
    shared = smooth_side[:, loads + 2 * KP :]
    energy = folded(dot_rows(coarse[: 8 * KP, :], stacked(images)), 4 * KP, rows)
    terms[0, :, :loads] = load_side
    terms[0, :, loads:] = smooth_side[:, :loads]
    terms[1, :, :loads] = energy[:KP, :loads]
    terms[1, :, loads:] = energy[KP : 2 * KP, :loads]
    terms[2, :, :loads] = energy[2 * KP : 3 * KP, :loads]
    terms[2, :, loads:] = energy[3 * KP :, :loads]
    for i in range(2):
        for j in range(2):
            at = (2 * i + j) * 4 * KP
            basis_rows = energy[i * KP : (i + 1) * KP]
            smooth_rows = energy[(2 + i) * KP : (3 + i) * KP]
            basis_cols = slice(loads + j * KP, loads + (j + 1) * KP)
            smooth_cols = slice(loads + (2 + j) * KP, loads + (3 + j) * KP)
            terms[3, :, at : at + KP] = basis_rows[:, basis_cols]
            terms[3, :, at + KP : at + 2 * KP] = basis_rows[:, smooth_cols]
            terms[3, :, at + 2 * KP : at + 3 * KP] = smooth_rows[:, smooth_cols]
            last = shared[:, j * KP : (j + 1) * KP] if i == 0 else jnp.zeros((KP, KP), F32)
            terms[3, :, at + 3 * KP : at + 4 * KP] = last
    keep[...] = jnp.where(here.odd, terms[2:], terms[:2])
    image_a[rows:, :] = jnp.zeros((KP, face), F32)
    for kind in range(2):
        image_a[rows:, kind * 2 * loads : (kind + 1) * 2 * loads] = jnp.where(
            here.odd, terms[kind], terms[2 + kind]
        )


def coarse_solves(clusters, loads, terms, inverse):
    modes = inverse.shape[0] // clusters

    def one_kind(c, kind, which):
        value = terms[(c * 2 + kind // 2) * 3 + which]
        value = value[kind % 2 * modes : (kind % 2 + 1) * modes]
        return jnp.concatenate([value, jnp.zeros((KP - modes, value.shape[1]), F32)], axis=0)

    def total(c, kind):
        return one_kind(c, kind, 0)

    def begin(c, kind):
        return one_kind(c, kind, 1)

    def end(c, kind):
        return one_kind(c, kind, 2)

    span = 4 * KP
    lanes = terms.shape[-1]
    totals = [total(c, 0) for c in range(clusters)]
    load_side = [v[:, :loads] for v in totals]
    smooth_side = [v[:, loads:] for v in totals]

    def images(kind):
        found = []
        for c in range(clusters):
            value = total(c, kind)[:, :loads]
            if c + 1 < clusters:
                value = value + begin(c + 1, kind)[:, loads:]
            if c > 0:
                value = value + end(c - 1, kind)[:, loads:]
            found.append(value)
        return found

    centre, below, above = [], [], []
    for c in range(clusters):
        value, under, over = total(c, 3), begin(c, 3), end(c, 3)
        if c + 1 < clusters:
            value = value + pltpu.roll(begin(c + 1, 3), lanes - 3 * span, 1)
            over = over + pltpu.roll(begin(c + 1, 3), lanes - span, 1)
        if c > 0:
            value = value + pltpu.roll(end(c - 1, 3), lanes - 3 * span, 1)
            under = under + pltpu.roll(end(c - 1, 3), lanes - span, 1)
        centre.append(value)
        below.append(under)
        above.append(over)

    def block_times(block, amounts):
        value = block[:, 0:1] * amounts[0:1]
        for k in range(1, KP):
            value = value + block[:, k : k + 1] * amounts[k : k + 1]
        return value

    def times(kind, amounts):
        found = []
        for c in range(clusters):
            near, far = slice(kind * KP, (kind + 1) * KP), slice(span + kind * KP, span + (kind + 1) * KP)
            value = block_times(centre[c][:, near], amounts[c])
            if c > 0:
                value = value + block_times(below[c][:, far], amounts[c - 1])
            if c + 1 < clusters:
                value = value + block_times(above[c][:, far], amounts[c + 1])
            found.append(value)
        return found

    turned_centre = [v.T for v in centre]
    turned_below = [v.T for v in below]
    turned_above = [v.T for v in above]

    def turned_times(kind, amounts):
        found = []
        near, far = slice(kind * KP, (kind + 1) * KP), slice(span + kind * KP, span + (kind + 1) * KP)
        for c in range(clusters):
            value = block_times(turned_centre[c][near], amounts[c])
            if c > 0:
                value = value + block_times(turned_above[c - 1][far], amounts[c - 1])
            if c + 1 < clusters:
                value = value + block_times(turned_below[c + 1][far], amounts[c + 1])
            found.append(value)
        return found

    row = lax.broadcasted_iota(jnp.int32, (clusters * KP, clusters * modes), 0)
    col = lax.broadcasted_iota(jnp.int32, (clusters * KP, clusters * modes), 1)
    mode = row % KP
    spread = jnp.where((mode < modes) & (col == row // KP * modes + mode), 1.0, 0.0)
    padded = jnp.dot(spread, inverse[...], precision=EXACT, preferred_element_type=F32)
    padded = lax.dot_general(
        padded, spread, (((1,), (1,)), ((), ())), precision=EXACT, preferred_element_type=F32
    )

    def solve(parts):
        value = jnp.dot(
            padded, jnp.concatenate(parts, axis=0), precision=EXACT, preferred_element_type=F32
        )
        return [value[c * KP : (c + 1) * KP] for c in range(clusters)]

    def less(left, *others):
        found = list(left)
        for other in others:
            found = [p - q for p, q in zip(found, other)]
        return found

    load_amounts = solve(load_side)
    smooth_amounts = solve(less(smooth_side, times(3, load_amounts)))
    image_amounts = solve(less(images(1), times(1, load_amounts), times(0, smooth_amounts)))
    image_side = less(images(2), times(2, load_amounts), turned_times(1, smooth_amounts))
    smooth_image_amounts = solve(less(image_side, times(3, image_amounts)))
    return load_amounts, smooth_amounts, image_amounts, smooth_image_amounts


def second_kernel(
    extent,
    softness, terms, inverse, residual, smooth, coarse, pairs_a, pairs_b,
    image_a, image_b, got_a, got_b,
    pick, operator, place,
    search, applied, change, next_a, next_b, scalars,
    amounts, first, second, third,
):
    loads, slots = residual.shape
    face = slots // 2
    half, _, size = pairs_a.shape
    clusters, _ = extent
    here = chain(*extent)

    def weighted(left, right):
        product = left * right
        near = jnp.sum(product[:, :face], axis=1, keepdims=True)
        far = jnp.sum(product[:, face:], axis=1, keepdims=True)
        return here.weights[0] * near + here.weights[1] * far

    solved = coarse_solves(clusters, loads, terms, inverse)
    for kind, parts in enumerate(solved):
        for c, part in enumerate(parts):
            amounts[kind, c] = part

    def local(kind, reached):
        return [amounts[kind, c] for c in reached]

    none = [jnp.zeros((2 * KP, loads), F32)]
    own = jnp.concatenate(local(1, here.own) + local(0, here.own), axis=0)
    image_own = jnp.concatenate(local(3, here.own) + local(2, here.own), axis=0)
    own_basis = jnp.concatenate(local(0, here.own) + none, axis=0)
    image_own_basis = jnp.concatenate(local(2, here.own) + none, axis=0)
    projected = residual[...] - dot_modes(own_basis, coarse[...])
    direction = smooth[...] - dot_modes(own, coarse[...])
    search[...] = direction
    for side, image, got in ((0, image_a, got_a), (1, image_b, got_b)):
        theirs = local(1, here.near[side]) + local(0, here.near[side])
        mixed = jnp.concatenate([own] + theirs, axis=0)
        rows = slice(loads, loads + 4 * KP)
        rows = three_rows(jnp.concatenate([image[rows, :], got[rows, :]], axis=0))
        applied[:, side * face : (side + 1) * face] = (
            image[:loads, :] + got[:loads, :] - dot_modes(mixed, rows)
        )
    image_projected = applied[...] - dot_modes(image_own_basis, coarse[...])
    for side, pairs in ((0, pairs_a), (1, pairs_b)):
        for k in range(half):
            cols = slice(side * face + k * size, side * face + (k + 1) * size)
            change[:, cols] = smooth_block(applied[:, cols], here.weights[side], pairs[k])
    changed = change[...] - dot_modes(image_own, coarse[...])
    change[...] = changed
    high, low = two_parts(changed)
    first[:loads, :] = high
    first[loads:, :] = low
    found = [
        weighted(projected, direction),
        weighted(direction, applied[...]),
        weighted(projected, changed) + weighted(image_projected, direction),
        weighted(image_projected, changed),
    ]

    second[...] = dot(first[...], pick[...]).astype(BF16)

    images = apply_rest(
        loads, softness[...], operator, place, second, third, next_a, next_b
    )
    for vector in (search, change):
        found.append(jnp.sum(vector[...] * images, axis=1, keepdims=True))
    lane = lax.broadcasted_iota(jnp.int32, (loads, 128), 1)
    value = jnp.zeros(lane.shape, F32)
    for k, column in enumerate(found):
        value = jnp.where(lane == k, column, value)
    turned = value.T
    scalars[:, :loads] = turned[:4, :]
    scalars[:, loads:] = turned[4:8, :]


def last_kernel(
    extent, scalars, residual, search, applied, change, next_a, next_b, got_a, got_b, out_m, out_r
):
    loads, slots = residual.shape
    face = slots // 2
    total = jnp.sum(scalars[...], axis=0)
    total = jnp.concatenate([total[:, :loads], total[:, loads:]], axis=0)
    rho = total[0:1]
    gamma = total[1:2]
    alpha = rho / gamma
    rho_next = rho - alpha * total[2:3] + alpha * alpha * total[3:4]
    grow = 1.0 + rho_next / rho
    energy = grow * grow * gamma - 2.0 * grow * alpha * total[4:5] + alpha * alpha * total[5:6]
    alpha_next = rho_next / energy
    lengths = jnp.concatenate(
        [alpha + alpha_next * grow, alpha_next * alpha, jnp.zeros((6, rho.shape[1]), F32)], axis=0
    )
    turned = jnp.concatenate([lengths, jnp.zeros((120, rho.shape[1]), F32)], axis=0).T
    along, against = turned[:loads, 0:1], turned[:loads, 1:2]
    sides = []
    for side, own, got in ((0, next_a, got_a), (1, next_b, got_b)):
        cols = slice(side * face, (side + 1) * face)
        sides.append(
            (
                along * search[:, cols] - against * change[:, cols],
                residual[:, cols] - along * applied[:, cols] + against * (own[...] + got[...]),
            )
        )
    odd = chain(*extent).odd
    for k, out in ((0, out_m), (1, out_r)):
        out[:, 0, :] = jnp.where(odd, sides[0][k], sides[1][k])
        out[:, 1, :] = jnp.where(odd, sides[1][k], sides[0][k])


VMEM = pl.BlockSpec(memory_space=pltpu.VMEM)
HBM = pl.BlockSpec(memory_space=pltpu.HBM)


def shaped(shape, dtype=F32):
    return jax.ShapeDtypeStruct(shape, dtype)


def in_hbm(value):
    return pltpu.with_memory_space_constraint(value, pltpu.HBM)


def per_device(
    dual_load, dual_operator, index_map, stiffness, coarse_basis, dirichlet_blocks, coarse_inverse
):
    loads, _, face = dual_load.shape[2:]
    slots = 2 * face
    modes = coarse_basis.shape[2]
    block_count, size, _ = dirichlet_blocks.shape[2:]
    clusters, members = lax.axis_size("cluster"), lax.axis_size("member")
    devices = clusters * members
    extent = clusters, members
    load = dual_load.reshape(loads, 2, face)
    basis = coarse_basis.reshape(modes, 1, slots)
    blocks = dirichlet_blocks.reshape(block_count, size, size)

    evens = [(i, i + 1) for i in range(0, devices - 1, 2)]
    odds = [(i, i + 1) for i in range(1, devices - 1, 2)]
    evens = evens + [(j, i) for i, j in evens]
    odds = odds + [(j, i) for i, j in odds]

    def swap(side_a, side_b):
        from_b = lax.ppermute(side_b, AXES, odds)
        from_a = lax.ppermute(side_a, AXES, evens)
        return from_a, from_b

    def share(copies):
        parts = copies.reshape((-1,) + copies.shape[2:])
        return lax.all_to_all(parts, AXES, 0, 0, tiled=True).reshape(copies.shape)

    def params(mebibytes):
        return pltpu.CompilerParams(vmem_limit_bytes=mebibytes * 1024 * 1024)

    half_vector = shaped((loads, face))
    vector = shaped((loads, slots))
    half = block_count // 2
    packed = shaped((size // 2 + KP + loads, face))
    pay_a, pay_b, own_blocks = pl.pallas_call(
        functools.partial(pack_kernel, extent),
        out_shape=(packed, packed, shaped(blocks.shape, BF16)),
        in_specs=[HBM] * 3,
        out_specs=(VMEM,) * 3,
        scratch_shapes=[
            pltpu.VMEM(load.shape, F32),
            pltpu.VMEM(basis.shape, F32),
            pltpu.SemaphoreType.DMA((3,)),
        ],
        compiler_params=params(8),
    )(*[in_hbm(v) for v in (load, basis, blocks)])
    got_a, got_b = swap(pay_a, pay_b)

    ordering = shaped((slots, slots), BF16)
    pick, place, operator, softness = pl.pallas_call(
        functools.partial(order_kernel, extent),
        out_shape=(ordering, ordering, ordering, shaped((1, 1))),
        in_specs=[HBM, VMEM, HBM],
        out_specs=(VMEM,) * 4,
        scratch_shapes=[pltpu.VMEM((1, slots), jnp.int32), pltpu.SemaphoreType.DMA((2,))],
        cost_estimate=pl.CostEstimate(flops=10**11, transcendentals=0, bytes_accessed=10**8),
        compiler_params=params(8),
    )(in_hbm(index_map.reshape(1, slots)), stiffness, in_hbm(dual_operator))
    pick, operator, place = [
        pltpu.with_memory_space_constraint(v, pltpu.VMEM) for v in (pick, operator, place)
    ]

    rows = loads + 4 * KP
    side_pairs = shaped((half, 2 * size, size), BF16)
    residual_a, smooth_a, coarse_a, own_basis_a, pairs_a, first_a, second_a = pl.pallas_call(
        functools.partial(near_kernel, extent, modes),
        out_shape=(
            half_vector,
            half_vector,
            shaped((12 * KP, face), BF16),
            shaped((2 * KP, face), BF16),
            side_pairs,
            shaped((2 * rows, face), BF16),
            shaped((2 * rows, slots), BF16),
        ),
        in_specs=[VMEM] * 4,
        out_specs=(VMEM,) * 7,
        compiler_params=params(8),
    )(pay_a, got_a, own_blocks, pick)
    residual, smooth, coarse, pairs_b, image_a, image_b, keep = pl.pallas_call(
        functools.partial(first_kernel, extent, modes),
        out_shape=(
            vector,
            vector,
            shaped((12 * KP, slots), BF16),
            side_pairs,
            shaped((rows + KP, face)),
            shaped((rows, face)),
            shaped((2, KP, 2 * loads)),
        ),
        in_specs=[VMEM] * 13,
        out_specs=(VMEM,) * 7,
        scratch_shapes=[pltpu.VMEM((2 * KP, slots), BF16)]
        + [pltpu.VMEM((2 * rows, slots), BF16)] * 3
        + [pltpu.VMEM((4, KP, 2 * loads), F32)],
        compiler_params=params(12),
    )(
        softness, pay_b, got_b, own_blocks, residual_a, smooth_a, coarse_a, own_basis_a, first_a,
        second_a, pick, operator, place,
    )

    got_a, got_b = swap(image_a, image_b)
    terms = pl.pallas_call(
        merge_kernel,
        out_shape=shaped((devices, 2 * modes // SLICE, SLICE, 2 * loads)),
        in_specs=[VMEM] * 2,
        out_specs=VMEM,
        compiler_params=params(8),
    )(keep, got_a)
    terms = pl.pallas_call(
        functools.partial(fold_kernel, clusters, members),
        out_shape=shaped((clusters * 6, 2 * modes, 2 * loads)),
        in_specs=[VMEM],
        out_specs=VMEM,
        compiler_params=params(8),
    )(share(terms))

    search, applied, change, next_a, next_b, scalars = pl.pallas_call(
        functools.partial(second_kernel, extent),
        out_shape=(vector, vector, vector, half_vector, half_vector, shaped((4, 2 * loads))),
        in_specs=[VMEM] * 15,
        out_specs=(VMEM,) * 6,
        scratch_shapes=[pltpu.VMEM((4, clusters, KP, loads), F32)]
        + [pltpu.VMEM((2 * loads, slots), BF16)] * 3,
        compiler_params=params(12),
    )(
        softness, terms, coarse_inverse, residual, smooth, coarse, pairs_a, pairs_b,
        image_a, image_b, got_a, got_b, pick, operator, place,
    )

    got_a, got_b = swap(next_a, next_b)
    scalars = share(jnp.broadcast_to(scalars[None, None], (devices, 1) + scalars.shape))
    scalars = scalars.reshape(devices, 4, 2 * loads)

    out_m, out_r = pl.pallas_call(
        functools.partial(last_kernel, extent),
        out_shape=(shaped((loads, 2, face)), shaped((loads, 2, face))),
        in_specs=[VMEM] * 9,
        out_specs=(VMEM, VMEM),
        compiler_params=params(12),
    )(scalars, residual, search, applied, change, next_a, next_b, got_a, got_b)
    return out_m.reshape(dual_load.shape), out_r.reshape(dual_load.shape)


def solution(mesh):
    in_specs = (
        P("cluster", "member", None, None, None),
        P(),
        P("cluster", "member", None),
        P("cluster", "member"),
        P("cluster", "member", None, None),
        P("cluster", "member", None, None, None),
        P(),
    )
    out_specs = (P("cluster", "member", None, None, None), P("cluster", "member", None, None, None))
    return jax.shard_map(
        per_device, mesh=mesh, in_specs=in_specs, out_specs=out_specs, check_vma=False
    )
```
